32 devices in a mesh: ens: 2 (over y), lat: 8 (over z, x), lev: 2 (over core).
Axes of the slice: x: 2, y: 2, z: 4, core: 2. Of those that a mesh axis runs over, the one named last changes fastest.
Arguments:
- constituent_densities: float32 [32, 4, 32, 1152], P('ens', 'lev', 'lat'), parts along dimension 0, may hold values from -6 to 6
- thermal_state: float32 [8, 32, 1152], P(('ens', 'lev'), 'lat'), parts along dimension 0, may hold values from 0.5 to 1.5
- integer_boxes_traversed: int32 [8, 32, 1152], P(('ens', 'lev'), 'lat'), parts along dimension 0, may hold values from 0 to 2
- partial_crossing_share: float32 [8, 32, 1152], P(('ens', 'lev'), 'lat'), parts along dimension 0, may hold values from 0 to 1
- northward_crossing_share: float32 [8, 32, 1152], P(('ens', 'lev'), 'lat'), parts along dimension 0, may hold values from -0.9 to 0.9
- higher_donor_stratum: int32 [8, 32, 1152], P('ens', 'lat', 'lev'), parts along dimension 0, may hold values from 0 to 2
- deeper_donor_share: float32 [8, 32, 1152], P('ens', 'lat', 'lev'), parts along dimension 0, may hold values from 0 to 1
- napierian_thickness_quotient: float32 [8, 32, 1152], P('ens', 'lat', 'lev'), parts along dimension 0, may hold values from 0.1 to 1
- ground_gravity_height: float32 [64, 1152], P(('ens', 'lat'), 'lev'), parts along dimension 0, may hold values from 0 to 2
Outputs:
- tracers_out: float32 [32, 4, 32, 1152], P('ens', 'lev', 'lat'), parts along dimension 0
- temperature_out: float32 [8, 32, 1152], P(('ens', 'lev'), 'lat'), parts along dimension 0
- geopotential: float32 [8, 32, 1152], P(('ens', 'lev'), 'lat'), parts along dimension 0
The draws below stay inside these ranges and needn't reach their ends.
There are 2 independent parts, one for each index of `ens`. The reference program is written for one: setup_inputs(seed, part) draws one part's arguments, and reference() takes and returns one part's arrays. A program takes and returns all parts, laid end to end along the dimension named above; each array names one. Nothing has to cross between parts.
All inputs are finite; a program needn't handle non-finite values.
Results may differ from the reference program's by a relative error of at most 0.0003.
Values sent between devices are 32-bit elements; how exact they have to be, the bound alone decides.
No kernel may reach another device: no remote copies, remote signals or barrier semaphores. Data moves between devices by JAX's collectives and lax.ppermute only.
A program may use at most 64 MiB of HBM per device.

```python
import math
import jax
import jax.numpy as jnp
from jax import lax

TRACERS = 16
EASTWARD_BOXES = 1152
NMAX = 2
PARALLEL_COUNT = 32
HEIGHT_STRATA = 4


def with_ends(result, stream_key, least, high):
    longest = result.shape.index(max(result.shape))
    spots = []
    for shift in (0, 1):
        where = [jax.random.randint(jax.random.fold_in(stream_key, axis), (), 0, length) for axis, length in enumerate(result.shape)]
        where[longest] = (where[longest] + shift) % result.shape[longest]
        spots.append(tuple(where))
    return result.at[spots[0]].set(least).at[spots[1]].set(high)


def shard_levels(rng, shape, split, low, top_value):
    factor_of, own = 1.0, jax.random.fold_in(rng, 6)
    for dim, blocks in split:
        draws = jnp.exp(jax.random.uniform(jax.random.fold_in(own, dim), (blocks,), jnp.float32, low / len(split), top_value / len(split)))
        factor_of = factor_of * jnp.repeat(draws, shape[dim] // blocks).reshape([-1 if axis == dim else 1 for axis in range(len(shape))])
    return factor_of


def gaussian(stream_key, extent, scale, limit, pieces=(), held_as=jnp.bfloat16):
    factor_of = shard_levels(stream_key, extent, pieces, -0.22, 0.18) if pieces else 1.0
    result = jax.random.normal(stream_key, extent, jnp.float32) * scale * factor_of
    return jnp.minimum(jnp.maximum(result, -limit), limit).astype(held_as)


def setup_inputs(seed: int = 0, part: int = 0) -> dict:
    key_of = jax.random.split(jax.random.key(seed), 10)
    part_keys = jax.random.split(jax.random.fold_in(key_of[9], part), 10)
    constituent_densities = gaussian(part_keys[0], (TRACERS, HEIGHT_STRATA, PARALLEL_COUNT, EASTWARD_BOXES), 1.0, 6.0, ((1, 2), (2, 8)), jnp.float32)
    thermal_state = jnp.clip(0.5 + 1.0 * jax.random.uniform(part_keys[1], (HEIGHT_STRATA, PARALLEL_COUNT, EASTWARD_BOXES), jnp.float32) ** shard_levels(part_keys[1], (HEIGHT_STRATA, PARALLEL_COUNT, EASTWARD_BOXES), ((0, 2), (1, 8)), -0.2, 0.2), 0.5, 1.5)
    integer_boxes_traversed = with_ends(jax.random.randint(part_keys[2], (HEIGHT_STRATA, PARALLEL_COUNT, EASTWARD_BOXES), 0, NMAX + 1), jax.random.fold_in(part_keys[2], 1), 0, NMAX).astype(jnp.int32)
    partial_crossing_share = jnp.clip(1.0 * jax.random.uniform(part_keys[3], (HEIGHT_STRATA, PARALLEL_COUNT, EASTWARD_BOXES), jnp.float32) ** shard_levels(part_keys[3], (HEIGHT_STRATA, PARALLEL_COUNT, EASTWARD_BOXES), ((0, 2), (1, 8)), -0.2, 0.2), 0.0, 1.0)
    northward_crossing_share = jnp.clip(jax.random.uniform(part_keys[4], (HEIGHT_STRATA, PARALLEL_COUNT, EASTWARD_BOXES), jnp.float32, -0.9, 0.9) * shard_levels(part_keys[4], (HEIGHT_STRATA, PARALLEL_COUNT, EASTWARD_BOXES), ((0, 2), (1, 8)), -0.4, 0.0), -0.9, 0.9)
    higher_donor_stratum = with_ends(jax.random.randint(part_keys[5], (HEIGHT_STRATA, PARALLEL_COUNT, EASTWARD_BOXES), 0, HEIGHT_STRATA - 1), jax.random.fold_in(part_keys[5], 1), 0, (HEIGHT_STRATA - 1) - 1).astype(jnp.int32)
    deeper_donor_share = jnp.clip(1.0 * jax.random.uniform(part_keys[6], (HEIGHT_STRATA, PARALLEL_COUNT, EASTWARD_BOXES), jnp.float32) ** shard_levels(part_keys[6], (HEIGHT_STRATA, PARALLEL_COUNT, EASTWARD_BOXES), ((1, 8), (2, 2)), -0.2, 0.2), 0.0, 1.0)
    napierian_thickness_quotient = jnp.clip(jnp.exp(math.log(1.0) - 2.3025851 * jax.random.uniform(part_keys[7], (HEIGHT_STRATA, PARALLEL_COUNT, EASTWARD_BOXES), jnp.float32) ** shard_levels(part_keys[7], (HEIGHT_STRATA, PARALLEL_COUNT, EASTWARD_BOXES), ((1, 8), (2, 2)), -0.2, 0.2)), 0.1, 1.0)
    ground_gravity_height = jnp.clip(2.0 * jax.random.uniform(part_keys[8], (PARALLEL_COUNT, EASTWARD_BOXES), jnp.float32) ** shard_levels(part_keys[8], (PARALLEL_COUNT, EASTWARD_BOXES), ((0, 8), (1, 2)), -0.2, 0.2), 0.0, 2.0)
    return dict(constituent_densities=constituent_densities, thermal_state=thermal_state, integer_boxes_traversed=integer_boxes_traversed, partial_crossing_share=partial_crossing_share, northward_crossing_share=northward_crossing_share, higher_donor_stratum=higher_donor_stratum, deeper_donor_share=deeper_donor_share, napierian_thickness_quotient=napierian_thickness_quotient, ground_gravity_height=ground_gravity_height)


def shift_lon(values, offset):
    return jnp.roll(values, offset, axis=-1)


def pad_poles(values, factor):
    row_count = values.shape[-2]
    lon_count = values.shape[-1]
    south_rows = factor * shift_lon(jnp.flip(values[..., 0:3, :], -2), lon_count // 2)
    north_rows = factor * shift_lon(jnp.flip(values[..., row_count - 3:row_count, :], -2), lon_count // 2)
    return jnp.concatenate([south_rows, values, north_rows], axis=-2)


def advect(padded, courant_y, whole_cells, fraction, first_row, lat_total):
    row_count = padded.shape[-2] - 6
    cell_values = padded[..., 3:row_count + 3, :]
    west_edge = (7.0 / 12.0) * (shift_lon(cell_values, 1) + cell_values) - (1.0 / 12.0) * (shift_lon(cell_values, 2) + shift_lon(cell_values, -1))
    east_edge = shift_lon(west_edge, -1)
    gradient = east_edge - west_edge
    parabola = 6.0 * cell_values - 3.0 * (west_edge + east_edge)
    crossed = jnp.zeros_like(cell_values)
    upwind_edge = jnp.zeros_like(cell_values)
    upwind_gradient = jnp.zeros_like(cell_values)
    upwind_parabola = jnp.zeros_like(cell_values)
    for offset in range(1, NMAX + 2):
        if offset <= NMAX:
            crossed = crossed + jnp.where(whole_cells >= offset, shift_lon(cell_values, offset), 0.0)
        landing = whole_cells == offset - 1
        upwind_edge = upwind_edge + jnp.where(landing, shift_lon(east_edge, offset), 0.0)
        upwind_gradient = upwind_gradient + jnp.where(landing, shift_lon(gradient, offset), 0.0)
        upwind_parabola = upwind_parabola + jnp.where(landing, shift_lon(parabola, offset), 0.0)
    zonal_flux = crossed + fraction * (upwind_edge - 0.5 * fraction * (upwind_gradient - (1.0 - 2.0 * fraction / 3.0) * upwind_parabola))
    zonal_change = shift_lon(zonal_flux, -1) - zonal_flux
    face_values = (7.0 / 12.0) * (padded[..., 1:row_count + 4, :] + padded[..., 2:row_count + 5, :]) - (1.0 / 12.0) * (padded[..., 0:row_count + 3, :] + padded[..., 3:row_count + 6, :])
    low_edge = face_values[..., 0:row_count + 2, :]
    high_edge = face_values[..., 1:row_count + 3, :]
    centers = padded[..., 2:row_count + 4, :]
    incline = high_edge - low_edge
    curvature = 6.0 * centers - 3.0 * (low_edge + high_edge)
    courant = courant_y[..., 2:row_count + 3, :]
    magnitude = jnp.abs(courant)
    northward = courant * (high_edge[..., 0:row_count + 1, :] - 0.5 * magnitude * (incline[..., 0:row_count + 1, :] - (1.0 - 2.0 * magnitude / 3.0) * curvature[..., 0:row_count + 1, :]))
    southward = courant * (low_edge[..., 1:row_count + 2, :] + 0.5 * magnitude * (incline[..., 1:row_count + 2, :] + (1.0 - 2.0 * magnitude / 3.0) * curvature[..., 1:row_count + 2, :]))
    face_flux = jnp.where(courant >= 0.0, northward, southward)
    face_rows = jnp.arange(row_count + 1, dtype=jnp.int32) + first_row
    face_cosine = jnp.sin(math.pi * jnp.minimum(face_rows, lat_total - face_rows).astype(jnp.float32) / lat_total)
    center_rows = (jnp.arange(row_count, dtype=jnp.int32) + first_row).astype(jnp.float32) + 0.5
    center_cosine = jnp.sin(math.pi * center_rows / lat_total)
    weighted = face_flux * face_cosine[:, None]
    meridional_change = (weighted[..., 1:, :] - weighted[..., :-1, :]) / center_cosine[:, None]
    return cell_values - zonal_change - meridional_change


def remap(source, level_index, weight):
    level_count = source.shape[1]
    remapped = jnp.zeros((source.shape[0],) + weight.shape, jnp.float32)
    for level in range(level_count - 1):
        blended = (1.0 - weight) * source[:, level][:, None] + weight * source[:, level + 1][:, None]
        remapped = remapped + jnp.where(level_index == level, blended, 0.0)
    return remapped


def layer_thickness(remapped, napierian_thickness_quotient):
    return remapped[-1] * (1.0 + 0.608 * remapped[0]) * napierian_thickness_quotient


def deeper_sum(thickness):
    return jnp.flip(jnp.cumsum(jnp.flip(thickness, 0), 0), 0) - thickness


def reference(constituent_densities, thermal_state, integer_boxes_traversed, partial_crossing_share, northward_crossing_share, higher_donor_stratum, deeper_donor_share, napierian_thickness_quotient, ground_gravity_height):
    constituent_arrays = jnp.concatenate([constituent_densities, thermal_state[None]], axis=0)
    padded_fields = pad_poles(constituent_arrays, 1.0)
    padded_courant = pad_poles(northward_crossing_share, -1.0)

    def one_field(padded):
        return advect(padded, padded_courant, integer_boxes_traversed, partial_crossing_share, 0, PARALLEL_COUNT)

    advected = lax.map(one_field, padded_fields)
    remapped = remap(advected, higher_donor_stratum, deeper_donor_share)
    thickness = layer_thickness(remapped, napierian_thickness_quotient)
    geopotential = ground_gravity_height + deeper_sum(thickness) + 0.5 * thickness
    return remapped[:TRACERS], remapped[TRACERS], geopotential
```

```python
import functools
import math

import jax
import jax.numpy as jnp
import numpy as np
from jax import lax
from jax.experimental import pallas as pl
from jax.experimental.pallas import tpu as pltpu
from jax.sharding import PartitionSpec as P

ROWS = 4
LEVELS = 2
LANE = 128


def lane_view(values):
    rows, lons = values.shape[-2:]
    lead = math.prod(values.shape[:-2])
    chunks = lons // LANE
    return (
        values.reshape(lead, rows, chunks, LANE)
        .transpose(0, 2, 1, 3)
        .reshape(lead * chunks * rows, LANE)
    )


def from_lane_view(values, shape):
    rows, lons = shape[-2:]
    lead = math.prod(shape[:-2])
    chunks = lons // LANE
    return values.reshape(lead, chunks, rows, LANE).transpose(0, 2, 1, 3).reshape(shape)


def lanes(chunk):
    return pl.ds(chunk * LANE, LANE)


def parity():
    return lax.rem(lax.axis_index("lat"), 2)


def pack_kernel(chunks, fields, x, t, c, edge, relay0, relay1, near, near_t):
    odd = parity()
    relay = (relay0, relay1)
    stride = LEVELS * ROWS * chunks
    for d in range(3):
        row = jnp.where(odd == 1, 1 + d, 2 - d)
        for chunk in range(chunks):
            for lev in range(LEVELS):
                start = lev * ROWS * chunks + chunk * ROWS + row
                relay[lev][d, :, lanes(chunk)] = x[pl.ds(start, fields, stride=stride), :]
            edge[pl.ds(2 * d, 2), lanes(chunk)] = t[
                pl.ds(chunk * ROWS + row, 2, stride=ROWS * chunks), :
            ]
    row = jnp.where(odd == 1, 0, ROWS - 1)
    for chunk in range(chunks):
        for lev in range(LEVELS):
            start = lev * ROWS * chunks + chunk * ROWS + row
            near[lev, :, lanes(chunk)] = x[pl.ds(start, fields, stride=stride), :]
        near_t[:, lanes(chunk)] = t[pl.ds(chunk * ROWS + row, 2, stride=ROWS * chunks), :]
        edge[pl.ds(6, 2), lanes(chunk)] = c[
            pl.ds(chunk * ROWS + ROWS - 1, 2, stride=ROWS * chunks), :
        ]


def parabola_weights(share):
    half = 0.5 * share
    curve = half * (1.0 - share * (2.0 / 3.0))
    right = (1.0 - half - 3.0 * curve) * (1.0 / 12.0)
    left = (half - 3.0 * curve) * (1.0 / 12.0)
    return (
        -share * left,
        share * (7.0 * left - right),
        share * (7.0 * (left + right) + 6.0 * curve),
        share * (7.0 * right - left),
        -share * right,
    )


def face_weights(courant):
    t = parabola_weights(jnp.abs(courant))
    north = courant >= 0.0
    zero = jnp.zeros_like(courant)
    return (
        jnp.where(north, t[0], zero),
        jnp.where(north, t[1], -t[4]),
        jnp.where(north, t[2], -t[3]),
        jnp.where(north, t[3], -t[2]),
        jnp.where(north, t[4], -t[1]),
        jnp.where(north, zero, -t[0]),
    )


def halo_terms(j):
    south = [(0, d, -(j + d)) for d in range(1, 4 - j)]
    north = [(1, d, ROWS - 1 - j + d) for d in range(1, j + 1)]
    return south + north


def spread(row, like):
    return jnp.broadcast_to(row, like.shape)


def pre_kernel(
    chunks, fields, last, scale, x, t, c, n, f, edge_near, edge_far,
    pre, pre_t, halo_w, q, qt, zonal_w, own_w,
):
    lat = lax.axis_index("lat")
    odd = lax.rem(lat, 2)
    lons = chunks * LANE
    stride = LEVELS * ROWS * chunks

    def row_of(ref, j):
        return jnp.concatenate(
            [ref[pl.ds(k * ROWS + j, LEVELS, stride=ROWS * chunks), :] for k in range(chunks)],
            axis=1,
        )

    for j in range(ROWS):
        qt[j] = row_of(t, j)
        for lev in range(LEVELS):
            for chunk in range(chunks):
                start = lev * ROWS * chunks + chunk * ROWS + j
                q[lev, j, :, lanes(chunk)] = x[pl.ds(start, fields, stride=stride), :]

    courants = [row_of(c, j) for j in range(ROWS)]
    below = jnp.where(odd == 1, edge_near[6:8, :], edge_far[6:8, :])
    below = jnp.where(lat == 0, -pltpu.roll(courants[0], lons // 2, 1), below)
    faces = [face_weights(v) for v in [below] + courants]
    for j in range(ROWS):
        low = scale[lat * 2 * ROWS + 2 * j]
        high = scale[lat * 2 * ROWS + 2 * j + 1]
        lower, upper = faces[j], faces[j + 1]

        def weight(offset):
            total = None
            if offset <= 2:
                total = low * lower[offset + 3]
            if offset >= -2:
                part = high * upper[offset + 2]
                total = -part if total is None else total - part
            return total

        for r in range(ROWS):
            own_w[j, r] = weight(r - j)
        for k, (_, _, offset) in enumerate(halo_terms(j)):
            halo_w[3 * j + k] = weight(offset)

    for j in range(ROWS):
        whole = row_of(n, j)
        s = parabola_weights(row_of(f, j))
        zero = jnp.zeros_like(s[0])
        one = jnp.ones_like(s[0])
        n0, n1 = whole == 0, whole == 1

        def pick(a, b, d):
            return jnp.where(n0, a, jnp.where(n1, b, d))

        zonal_w[j, 0] = pick(s[4], zero, zero)
        zonal_w[j, 1] = pick(s[3], s[4], zero)
        zonal_w[j, 2] = pick(s[2], s[3] + one, s[4] + one)
        zonal_w[j, 3] = pick(s[1], s[2], s[3] + one)
        zonal_w[j, 4] = pick(s[0], s[1], s[2])
        zonal_w[j, 5] = pick(zero, s[0], s[1])
        zonal_w[j, 6] = pick(zero, zero, s[0])

    def shifted(values, k):
        return values if k == 0 else pltpu.roll(values, (-k) % lons, 1)

    for j in range(ROWS):
        v = qt[j]
        flux = zonal_w[j, 1] * v
        for k in (0, 2, 3, 4, 5, 6):
            flux = flux + zonal_w[j, k] * shifted(v, 1 - k)
        total = v - (shifted(flux, 1) - flux)
        for r in range(ROWS):
            total = total + own_w[j, r] * qt[r]
        pre_t[j] = total

    for lev in range(LEVELS):

        @pl.loop(0, ROWS)
        def _(j):
            for g in range(fields // 8):
                span = pl.ds(8 * g, 8)
                v = q[lev, j, span, :]
                flux = spread(zonal_w[j, 1, lev : lev + 1, :], v) * v
                for k in (0, 2, 3, 4, 5, 6):
                    flux = flux + spread(zonal_w[j, k, lev : lev + 1, :], v) * shifted(v, 1 - k)
                total = v - (shifted(flux, 1) - flux)
                for r in range(ROWS):
                    total = total + spread(own_w[j, r, lev : lev + 1, :], v) * q[lev, r, span, :]
                pre[lev, j, span, :] = total

    def pole(side):
        for j in range(ROWS):
            for k, (where, d, _) in enumerate(halo_terms(j)):
                if where != side:
                    continue
                r = d - 1 if side == 0 else ROWS - d
                w = halo_w[3 * j + k]
                pre_t[j] = pre_t[j] + w * pltpu.roll(qt[r], lons // 2, 1)
                for lev in range(LEVELS):
                    for g in range(fields // 8):
                        span = pl.ds(8 * g, 8)
                        v = pltpu.roll(q[lev, r, span, :], lons // 2, 1)
                        pre[lev, j, span, :] = (
                            pre[lev, j, span, :] + spread(w[lev : lev + 1, :], v) * v
                        )
                halo_w[3 * j + k] = jnp.zeros_like(w)

    @pl.when(lat == 0)
    def _():
        pole(0)

    @pl.when(lat == last)
    def _():
        pole(1)


def fin_kernel(
    chunks, fields, pre, pre_t, halo_w, relay0, relay1, far0, far1, near, near_t, edge_near,
    edge_far, adv, adv_t,
):
    odd = parity()
    relay, far = (relay0, relay1), (far0, far1)

    def near_row(lev, d, lane):
        return near[lev, :, lane] if d == 1 else relay[lev][d - 2, :, lane]

    def far_row(lev, d, lane):
        return far[lev][3 - d, :, lane]

    def near_edge(d):
        return near_t[...] if d == 1 else edge_near[pl.ds(2 * (d - 2), 2), :]

    def far_edge(d):
        return edge_far[pl.ds(2 * (3 - d), 2), :]

    def body(rows, edges):
        for j in range(ROWS):
            total = pre_t[j]
            for k, (side, d, _) in enumerate(halo_terms(j)):
                total = total + halo_w[3 * j + k] * edges[side](d)
            for lev in range(LEVELS):
                adv_t[lev, j : j + 1, :] = total[lev : lev + 1, :]
            for lev in range(LEVELS):
                for chunk in range(chunks):
                    lane = lanes(chunk)
                    total = pre[lev, j, :, lane]
                    for k, (side, d, _) in enumerate(halo_terms(j)):
                        w = halo_w[3 * j + k, lev : lev + 1, lane]
                        total = total + spread(w, total) * rows[side](lev, d, lane)
                    adv[lev, j, :, lane] = total

    @pl.when(odd == 1)
    def _():
        body((near_row, far_row), (near_edge, far_edge))

    @pl.when(odd == 0)
    def _():
        body((far_row, near_row), (far_edge, near_edge))


def remap_kernel(
    chunks, fields, levels, adv_own, adv_peer, t_own, t_peer, columns,
    out, out_t, out_phi, weights, vapour, thick,
):
    group = lax.axis_index("lev")
    stride = LEVELS * ROWS * chunks
    sources = [(adv_own, t_own, lev, group * LEVELS + lev) for lev in range(LEVELS)]
    sources += [(adv_peer, t_peer, lev, (1 - group) * LEVELS + lev) for lev in range(LEVELS)]

    for s, (adv, _, lev, _) in enumerate(sources):
        for j in range(ROWS):
            vapour[s, j : j + 1, :] = adv[lev, j, 0:1, :]
    for k in range(levels):
        upper = columns[k]
        share = columns[levels + k]
        water = None
        heat = None
        for s, (_, temp, lev, level) in enumerate(sources):
            at = level.astype(jnp.float32)
            w = jnp.where(
                upper == at, 1.0 - share, jnp.where(upper + 1.0 == at, share, 0.0)
            )
            weights[k, s] = w
            water = w * vapour[s] if water is None else water + w * vapour[s]
            heat = w * temp[lev] if heat is None else heat + w * temp[lev]
        thick[k] = heat * (1.0 + 0.608 * water) * columns[2 * levels + k]
        thick[levels + k] = heat
    deeper = columns[3 * levels]
    for k in range(levels - 1, -1, -1):
        layer = thick[k]
        thick[k] = deeper + 0.5 * layer
        deeper = deeper + layer
    for lev in range(LEVELS):
        phi = thick[group * LEVELS + lev]
        heat = thick[levels + group * LEVELS + lev]
        for chunk in range(chunks):
            at = pl.ds((lev * chunks + chunk) * ROWS, ROWS)
            lane = slice(chunk * LANE, (chunk + 1) * LANE)
            out_phi[at, :] = phi[:, lane]
            out_t[at, :] = heat[:, lane]

    for j in range(ROWS):
        for chunk in range(chunks):
            lane = lanes(chunk)
            values = [adv[lev, j, :, lane] for adv, _, lev, _ in sources]
            for lev in range(LEVELS):
                k = group * LEVELS + lev
                total = None
                for s, v in enumerate(values):
                    part = spread(weights[k, s, j : j + 1, lane], v) * v
                    total = part if total is None else total + part
                start = (lev * chunks + chunk) * ROWS + j
                out[pl.ds(start, fields, stride=stride), :] = total


def call(kernel, outs, scratch=(), specs=None, cost=(0, 0), limit=16):
    return pl.pallas_call(
        kernel,
        out_shape=tuple(jax.ShapeDtypeStruct(s, jnp.float32) for s in outs),
        scratch_shapes=[pltpu.VMEM(s, jnp.float32) for s in scratch],
        compiler_params=pltpu.CompilerParams(vmem_limit_bytes=limit * 2**20),
        cost_estimate=pl.CostEstimate(flops=cost[0], bytes_accessed=cost[1], transcendentals=0),
        **({} if specs is None else {"in_specs": specs}),
    )


def on_device(
    constituent_densities,
    thermal_state,
    integer_boxes_traversed,
    partial_crossing_share,
    northward_crossing_share,
    higher_donor_stratum,
    deeper_donor_share,
    napierian_thickness_quotient,
    ground_gravity_height,
):
    fields, _, _, lons = constituent_densities.shape
    levels = higher_donor_stratum.shape[0]
    chunks = lons // LANE
    bands = lax.axis_size("lat")
    lat_total = bands * ROWS

    pairs = [(i, i ^ 1) for i in range(bands)]
    relays = [(i, i + 2) for i in range(0, bands - 2, 2)] + [(i, i - 2) for i in range(3, bands, 2)]
    cores = [(0, 1), (1, 0)]

    def swap(v):
        return lax.ppermute(v, "lat", pairs)

    def pass_on(v):
        return lax.ppermute(v, "lat", relays)

    def other_core(v):
        return lax.ppermute(v, "lev", cores)

    face = np.arange(lat_total + 1)
    face_sine = np.sin(math.pi * np.minimum(face, lat_total - face) / lat_total)
    face_sine[[0, -1]] = 0.0
    row_sine = np.sin(math.pi * (np.arange(lat_total) + 0.5) / lat_total)
    scale = np.stack([face_sine[:-1] / row_sine, face_sine[1:] / row_sine], 1)
    scale = jnp.asarray(scale.reshape(-1).astype(np.float32))

    x = lane_view(constituent_densities)
    t, n, f, c = (
        lane_view(v)
        for v in (
            thermal_state,
            integer_boxes_traversed,
            partial_crossing_share,
            northward_crossing_share,
        )
    )
    relay_shape = (3, fields, lons)
    field_shape = (LEVELS, ROWS, fields, lons)
    row = (LEVELS, lons)
    edge, relay0, relay1, near, near_t = call(
        functools.partial(pack_kernel, chunks, fields),
        [(8, lons), relay_shape, relay_shape, (LEVELS, fields, lons), row],
        cost=(0, 1400000),
    )(x, t, c)

    edge_near = swap(edge)
    relay0_near = swap(relay0)
    relay1_near = swap(relay1)
    near_near = swap(near)
    near_t_near = swap(near_t)
    edge_far = pass_on(edge_near)
    relay0_far = pass_on(relay0_near)
    relay1_far = pass_on(relay1_near)

    columns = jnp.concatenate(
        [
            higher_donor_stratum.astype(jnp.float32),
            deeper_donor_share,
            napierian_thickness_quotient,
            ground_gravity_height[None],
        ],
        axis=0,
    )
    peer_columns = other_core(columns)
    columns = jnp.where(
        lax.axis_index("lev") == 0,
        jnp.concatenate([columns, peer_columns], -1),
        jnp.concatenate([peer_columns, columns], -1),
    )

    vmem = pl.BlockSpec(memory_space=pltpu.VMEM)
    pre, pre_t, halo_w = call(
        functools.partial(pre_kernel, chunks, fields, bands - 1),
        [field_shape, (ROWS,) + row, (3 * ROWS,) + row],
        [field_shape, (ROWS,) + row, (ROWS, 7) + row, (ROWS, ROWS) + row],
        [pl.BlockSpec(memory_space=pltpu.SMEM)] + [vmem] * 7,
        cost=(20000000, 3000000),
    )(scale, x, t, c, n, f, edge_near, edge_far)

    adv, adv_t = call(
        functools.partial(fin_kernel, chunks, fields),
        [field_shape, (LEVELS, ROWS, lons)],
        cost=(2000000, 3000000),
    )(
        pre, pre_t, halo_w, relay0_near, relay1_near, relay0_far, relay1_far,
        near_near, near_t_near, edge_near, edge_far,
    )
    peer = other_core(adv)
    peer_t = other_core(adv_t)
    out, out_t, phi = call(
        functools.partial(remap_kernel, chunks, fields, levels),
        [x.shape, t.shape, t.shape],
        [(levels, 2 * LEVELS, ROWS, lons), (2 * LEVELS, ROWS, lons), (2 * levels, ROWS, lons)],
        cost=(3000000, 3000000),
    )(adv, peer, adv_t, peer_t, columns)
    return (
        from_lane_view(out, constituent_densities.shape),
        from_lane_view(out_t, thermal_state.shape),
        from_lane_view(phi, thermal_state.shape),
    )


def solution(mesh):
    return jax.shard_map(
        on_device,
        mesh=mesh,
        in_specs=(
            P("ens", "lev", "lat", None),
            P(("ens", "lev"), "lat", None),
            P(("ens", "lev"), "lat", None),
            P(("ens", "lev"), "lat", None),
            P(("ens", "lev"), "lat", None),
            P("ens", "lat", "lev"),
            P("ens", "lat", "lev"),
            P("ens", "lat", "lev"),
            P(("ens", "lat"), "lev"),
        ),
        out_specs=(
            P("ens", "lev", "lat", None),
            P(("ens", "lev"), "lat", None),
            P(("ens", "lev"), "lat", None),
        ),
        check_vma=False,
    )
```

```python
import functools
import math

import jax
import jax.numpy as jnp
import numpy as np
from jax import lax
from jax.experimental import pallas as pl
from jax.experimental.pallas import tpu as pltpu
from jax.sharding import PartitionSpec as P

ROWS = 4
LEVELS = 2
LANE = 128
SPLIT = 4


def lanes(chunk):
    return pl.ds(chunk * LANE, LANE)


def parity():
    return lax.rem(lax.axis_index("lat"), 2)


def both(odd, body):
    @pl.when(odd == 1)
    def _():
        body(True)

    @pl.when(odd == 0)
    def _():
        body(False)


def pack_kernel(fields, x, relay):
    def body(odd):
        for d in range(1, 4):
            row = d - 1 if odd else ROWS - d
            for f in range(fields):
                for lev in range(LEVELS):
                    relay[d - 1, lev, f : f + 1, :] = x[f, lev, row : row + 1, :]

    both(parity(), body)


def edge_kernel(t, c, edge):
    def body(odd):
        for lev in range(LEVELS):
            for d in range(1, 4):
                row = d - 1 if odd else ROWS - d
                at = 2 * (d - 1) + lev
                edge[at : at + 1, :] = t[lev, row : row + 1, :]
            edge[6 + lev : 7 + lev, :] = c[lev, ROWS - 1 : ROWS, :]

    both(parity(), body)


def parabola_weights(share):
    half = 0.5 * share
    curve = half * (1.0 - share * (2.0 / 3.0))
    right = (1.0 - half - 3.0 * curve) * (1.0 / 12.0)
    left = (half - 3.0 * curve) * (1.0 / 12.0)
    return (
        -share * left,
        share * (7.0 * left - right),
        share * (7.0 * (left + right) + 6.0 * curve),
        share * (7.0 * right - left),
        -share * right,
    )


def face_weights(courant):
    t = parabola_weights(jnp.abs(courant))
    north = courant >= 0.0
    zero = jnp.zeros_like(courant)
    return (
        jnp.where(north, t[0], zero),
        jnp.where(north, t[1], -t[4]),
        jnp.where(north, t[2], -t[3]),
        jnp.where(north, t[3], -t[2]),
        jnp.where(north, t[4], -t[1]),
        jnp.where(north, zero, -t[0]),
    )


def row_weights(c, below, scale, lat):
    row = lax.broadcasted_iota(jnp.int32, c.shape, 0)

    def by_row(parts):
        total = parts[ROWS - 1]
        for j in range(ROWS - 2, -1, -1):
            total = jnp.where(row == j, parts[j], total)
        return total

    low = by_row([jnp.full(c.shape, scale[lat * 2 * ROWS + 2 * j]) for j in range(ROWS)])
    high = by_row([jnp.full(c.shape, scale[lat * 2 * ROWS + 2 * j + 1]) for j in range(ROWS)])
    lower = face_weights(jnp.concatenate([below, c[: ROWS - 1]], axis=0))
    upper = face_weights(c)
    offsets = {}
    for o in range(-3, 4):
        total = jnp.zeros_like(c)
        if o <= 2:
            total = total + low * lower[o + 3]
        if o >= -2:
            total = total - high * upper[o + 2]
        offsets[o] = total
    zero = jnp.zeros_like(c)
    return [by_row([offsets.get(r - j, zero) for j in range(ROWS)]) for r in range(-3, ROWS + 3)]


def weights_kernel(last, scale, c, c_near, edge_far, out):
    lat = lax.axis_index("lat")
    odd = lax.rem(lat, 2)
    for lev in range(LEVELS):
        own = c[lev]
        below = jnp.where(odd == 1, c_near[lev, ROWS - 1 : ROWS, :], edge_far[6 + lev : 7 + lev, :])
        below = jnp.where(lat == 0, -pltpu.roll(own, own.shape[1] // 2, 1)[0:1], below)
        for r, w in enumerate(row_weights(own, below, scale, lat)):
            if r < 3:
                w = jnp.where(lat == 0, 0.0, w)
            if r >= ROWS + 3:
                w = jnp.where(lat == last, 0.0, w)
            out[r, lev] = w


def zonal_kernel(fields, last, scale, x, t, c, n, f, zon, zon_t, w):
    lat = lax.axis_index("lat")
    lons = x.shape[-1]

    def shifted(values, k):
        return values if k == 0 else pltpu.roll(values, (-k) % lons, 1)

    def advance(v, lev):
        flux = w[lev, 1] * v
        for k in (0, 2, 3, 4, 5, 6):
            flux = flux + w[lev, k] * shifted(v, 1 - k)
        return v - (shifted(flux, 1) - flux)

    for lev in range(LEVELS):
        whole = n[lev]
        s = parabola_weights(f[lev])
        zero = jnp.zeros_like(s[0])
        n0, n1 = whole == 0, whole == 1

        def pick(a, b, d):
            return jnp.where(n0, a, jnp.where(n1, b, d))

        w[lev, 0] = pick(s[4], zero, zero)
        w[lev, 1] = pick(s[3], s[4], zero)
        w[lev, 2] = pick(s[2], s[3] + 1.0, s[4] + 1.0)
        w[lev, 3] = pick(s[1], s[2], s[3] + 1.0)
        w[lev, 4] = pick(s[0], s[1], s[2])
        w[lev, 5] = pick(zero, s[0], s[1])
        w[lev, 6] = pick(zero, zero, s[0])

        @pl.loop(0, fields)
        def _(i):
            zon[i, lev] = advance(x[i, lev], lev)

        zon_t[lev] = advance(t[lev], lev)

    def pole(side):
        for lev in range(LEVELS):
            own = c[lev]
            below = -pltpu.roll(own, lons // 2, 1)[0:1]
            weights = row_weights(own, below, scale, lat)
            for d in range(1, 4):
                r = d - 1 if side == 0 else ROWS - d
                at = 3 - d if side == 0 else ROWS + 2 + d
                w[lev, d] = weights[at]
                w[lev, d + 3] = jnp.broadcast_to(t[lev, r : r + 1, :], own.shape)

            for d in range(1, 4):
                zon_t[lev] = zon_t[lev] + w[lev, d] * pltpu.roll(w[lev, d + 3], lons // 2, 1)

            @pl.loop(0, fields)
            def _(i):
                total = zon[i, lev]
                v = pltpu.roll(x[i, lev], lons // 2, 1)
                for d in range(1, 4):
                    r = d - 1 if side == 0 else ROWS - d
                    total = total + w[lev, d] * jnp.broadcast_to(v[r : r + 1], v.shape)
                zon[i, lev] = total

    @pl.when(lat == 0)
    def _():
        pole(0)

    @pl.when(lat == last)
    def _():
        pole(1)


def fin_kernel(fields, with_t, *refs):
    if with_t:
        x, zon, near, far, w, t, zon_t, t_near, edge_far, adv, adv_t = refs
    else:
        x, zon, near, far, w, adv = refs
    chunks = w.shape[-1] // LANE

    def body(odd):
        south_near = odd

        def halo(row, near_row, far_row):
            if 0 <= row < ROWS:
                return None
            d = -row if row < 0 else row - ROWS + 1
            if (row < 0) == south_near:
                return near_row(ROWS - d if south_near else d - 1)
            return far_row(d)

        for lev in range(LEVELS):
            for chunk in range(chunks):
                lane = lanes(chunk)
                weights = [w[r, lev, :, lane] for r in range(ROWS + 6)]

                def total_of(first, own_row, near_row, far_row):
                    total = first
                    for r in range(-3, ROWS + 3):
                        if 0 <= r < ROWS:
                            v = own_row(r)
                        else:
                            v = halo(r, near_row, far_row)
                        total = total + weights[r + 3] * jnp.broadcast_to(v, total.shape)
                    return total

                for f in range(fields):
                    adv[f, lev, :, lane] = total_of(
                        zon[f, lev, :, lane],
                        lambda r: x[f, lev, r : r + 1, lane],
                        lambda r: near[f, lev, r : r + 1, lane],
                        lambda d: far[d - 1, lev, f : f + 1, lane],
                    )
                if with_t:
                    adv_t[lev, :, lane] = total_of(
                        zon_t[lev, :, lane],
                        lambda r: t[lev, r : r + 1, lane],
                        lambda r: t_near[lev, r : r + 1, lane],
                        lambda d: edge_far[2 * (d - 1) + lev : 2 * (d - 1) + lev + 1, lane],
                    )

    both(parity(), body)


def remap_kernel(parts, levels, *refs):
    own, peer = refs[:parts], refs[parts : 2 * parts]
    t_own, t_peer, columns, out, out_t, out_phi, weights, vapour, thick = refs[2 * parts :]
    group = lax.axis_index("lev")
    chunks = out.shape[-1] // LANE
    sources = [(own, t_own, lev, group * LEVELS + lev) for lev in range(LEVELS)]
    sources += [(peer, t_peer, lev, (1 - group) * LEVELS + lev) for lev in range(LEVELS)]

    for k in range(levels):
        upper = columns[k]
        share = columns[levels + k]
        water = None
        heat = None
        for s, (adv, temp, lev, level) in enumerate(sources):
            at = level.astype(jnp.float32)
            w = jnp.where(upper == at, 1.0 - share, jnp.where(upper + 1.0 == at, share, 0.0))
            weights[k, s] = w
            water = w * adv[0][0, lev] if water is None else water + w * adv[0][0, lev]
            heat = w * temp[lev] if heat is None else heat + w * temp[lev]
        thick[k] = heat * (1.0 + 0.608 * water) * columns[2 * levels + k]
        thick[levels + k] = heat
    deeper = columns[3 * levels]
    for k in range(levels - 1, -1, -1):
        layer = thick[k]
        thick[k] = deeper + 0.5 * layer
        deeper = deeper + layer
    for lev in range(LEVELS):
        out_phi[lev] = thick[group * LEVELS + lev]
        out_t[lev] = thick[levels + group * LEVELS + lev]

    for chunk in range(chunks):
        lane = lanes(chunk)
        ws = [
            [weights[group * LEVELS + lev, s, :, lane] for s in range(2 * LEVELS)]
            for lev in range(LEVELS)
        ]
        field = 0
        for part in range(parts):
            for f in range(own[part].shape[0]):
                values = [adv[part][f, lev, :, lane] for adv, _, lev, _ in sources]
                for lev in range(LEVELS):
                    total = ws[lev][0] * values[0]
                    for s in range(1, 2 * LEVELS):
                        total = total + ws[lev][s] * values[s]
                    out[field, lev, :, lane] = total
                field += 1


def call(kernel, outs, scratch=(), specs=None, cost=(0, 0), limit=12):
    single = not isinstance(outs, list)
    shapes = tuple(jax.ShapeDtypeStruct(s, jnp.float32) for s in ([outs] if single else outs))
    return pl.pallas_call(
        kernel,
        out_shape=shapes[0] if single else shapes,
        scratch_shapes=[pltpu.VMEM(s, jnp.float32) for s in scratch],
        compiler_params=pltpu.CompilerParams(vmem_limit_bytes=limit * 2**20),
        cost_estimate=pl.CostEstimate(flops=cost[0], bytes_accessed=cost[1], transcendentals=0),
        **({} if specs is None else {"in_specs": specs}),
    )


def on_device(
    constituent_densities,
    thermal_state,
    integer_boxes_traversed,
    partial_crossing_share,
    northward_crossing_share,
    higher_donor_stratum,
    deeper_donor_share,
    napierian_thickness_quotient,
    ground_gravity_height,
):
    x, t, c = constituent_densities, thermal_state, northward_crossing_share
    fields, _, _, lons = x.shape
    levels = higher_donor_stratum.shape[0]
    bands = lax.axis_size("lat")
    lat_total = bands * ROWS

    pairs = [(i, i ^ 1) for i in range(bands)]
    relays = [(i, i + 2) for i in range(0, bands - 2, 2)] + [(i, i - 2) for i in range(3, bands, 2)]
    cores = [(0, 1), (1, 0)]

    def swap(v):
        return lax.ppermute(v, "lat", pairs)

    def pass_on(v):
        return lax.ppermute(v, "lat", relays)

    def other_core(v):
        return lax.ppermute(v, "lev", cores)

    face = np.arange(lat_total + 1)
    face_sine = np.sin(math.pi * np.minimum(face, lat_total - face) / lat_total)
    row_sine = np.sin(math.pi * (np.arange(lat_total) + 0.5) / lat_total)
    scale = np.stack([face_sine[:-1] / row_sine, face_sine[1:] / row_sine], 1)
    scale = jnp.asarray(scale.reshape(-1).astype(np.float32))

    smem, vmem = pl.BlockSpec(memory_space=pltpu.SMEM), pl.BlockSpec(memory_space=pltpu.VMEM)
    each = fields // SPLIT
    xs = [x[i * each : (i + 1) * each] for i in range(SPLIT)]
    t_near, c_near = swap(t), swap(c)
    near = [swap(v) for v in xs]

    zon, zon_t = call(
        functools.partial(zonal_kernel, fields, bands - 1),
        [x.shape, t.shape],
        [(LEVELS, 7, ROWS, lons)],
        [smem] + [vmem] * 5,
        cost=(4000000000, 3000000),
    )(scale, x, t, c, integer_boxes_traversed, partial_crossing_share)

    edge_far = pass_on(call(edge_kernel, (8, lons))(t_near, c_near))
    far = [
        pass_on(call(functools.partial(pack_kernel, each), (3, LEVELS, each, lons))(v)) for v in near
    ]

    columns = jnp.concatenate(
        [
            higher_donor_stratum.astype(jnp.float32),
            deeper_donor_share,
            napierian_thickness_quotient,
            ground_gravity_height[None],
        ],
        axis=0,
    )
    peer_columns = other_core(columns)
    columns = jnp.where(
        lax.axis_index("lev") == 0,
        jnp.concatenate([columns, peer_columns], -1),
        jnp.concatenate([peer_columns, columns], -1),
    )

    weights = call(
        functools.partial(weights_kernel, bands - 1),
        (ROWS + 6, LEVELS, ROWS, lons),
        (),
        [smem] + [vmem] * 3,
        cost=(400000000, 3000000),
    )(scale, c, c_near, edge_far)

    advected = []
    for i in range(SPLIT):
        args = [xs[i], zon[i * each : (i + 1) * each], near[i], far[i], weights]
        outs = [xs[i].shape]
        if i == 0:
            args += [t, zon_t, t_near, edge_far]
            outs.append(t.shape)
        advected += call(functools.partial(fin_kernel, each, i == 0), outs, cost=(200000000, 1000000))(
            *args
        )
    adv_t = advected.pop(1)
    peer = [other_core(v) for v in advected]
    peer_t = other_core(adv_t)
    return call(
        functools.partial(remap_kernel, SPLIT, levels),
        [x.shape, t.shape, t.shape],
        [(levels, 2 * LEVELS, ROWS, lons), (2 * LEVELS, ROWS, lons), (2 * levels, ROWS, lons)],
        cost=(3000000, 3000000),
    )(*advected, *peer, adv_t, peer_t, columns)


def solution(mesh):
    return jax.shard_map(
        on_device,
        mesh=mesh,
        in_specs=(
            P("ens", "lev", "lat", None),
            P(("ens", "lev"), "lat", None),
            P(("ens", "lev"), "lat", None),
            P(("ens", "lev"), "lat", None),
            P(("ens", "lev"), "lat", None),
            P("ens", "lat", "lev"),
            P("ens", "lat", "lev"),
            P("ens", "lat", "lev"),
            P(("ens", "lat"), "lev"),
        ),
        out_specs=(
            P("ens", "lev", "lat", None),
            P(("ens", "lev"), "lat", None),
            P(("ens", "lev"), "lat", None),
        ),
        check_vma=False,
    )
```

```python
import functools
import math

import jax
import jax.numpy as jnp
import numpy as np
from jax import lax
from jax.experimental import pallas as pl
from jax.experimental.pallas import tpu as pltpu
from jax.sharding import PartitionSpec as P

ROWS = 4
LEVELS = 2
LANE = 128


def lanes(chunk):
    return pl.ds(chunk * LANE, LANE)


def parity():
    return lax.rem(lax.axis_index("lat"), 2)


def both(odd, body):
    @pl.when(odd == 1)
    def _():
        body(True)

    @pl.when(odd == 0)
    def _():
        body(False)


def copy_kernel(x, out):
    out[...] = x[: out.shape[0]]


def side_rows(to_north):
    return (ROWS - 1, ROWS - 2, ROWS - 3) if to_north else (0, 1, 2)


def gather_rows(rows, x, t, out):
    count = out.shape[1]
    skip = x.shape[0] - count
    for d, row in enumerate(rows):
        for lev in range(LEVELS):
            at = d * LEVELS + lev
            for f in range(count):
                out[at, f : f + 1, :] = x[skip + f, lev, row : row + 1, :]
            out[3 * LEVELS, at : at + 1, :] = t[lev, row : row + 1, :]


def near_kernel(x, t, out):
    both(parity(), lambda odd: gather_rows(side_rows(not odd), x, t, out))


def relay_kernel(swapped, x, t, relay, out):
    def body(odd):
        for d, row in enumerate(side_rows(not odd)):
            for lev in range(LEVELS):
                for f in range(swapped.shape[0]):
                    relay[d * LEVELS + lev, f : f + 1, :] = swapped[f, lev, row : row + 1, :]
        gather_rows(side_rows(odd), x, t, out)

    both(parity(), body)


def parabola_weights(share):
    half = 0.5 * share
    curve = half * (1.0 - share * (2.0 / 3.0))
    right = (1.0 - half - 3.0 * curve) * (1.0 / 12.0)
    left = (half - 3.0 * curve) * (1.0 / 12.0)
    return (
        -share * left,
        share * (7.0 * left - right),
        share * (7.0 * (left + right) + 6.0 * curve),
        share * (7.0 * right - left),
        -share * right,
    )


def face_weights(courant):
    t = parabola_weights(jnp.abs(courant))
    north = courant >= 0.0
    zero = jnp.zeros_like(courant)
    return (
        jnp.where(north, t[0], zero),
        jnp.where(north, t[1], -t[4]),
        jnp.where(north, t[2], -t[3]),
        jnp.where(north, t[3], -t[2]),
        jnp.where(north, t[4], -t[1]),
        jnp.where(north, zero, -t[0]),
    )


def row_weights(c, below, scale, lat):
    row = lax.broadcasted_iota(jnp.int32, c.shape, 0)

    def by_row(parts):
        total = parts[ROWS - 1]
        for j in range(ROWS - 2, -1, -1):
            total = jnp.where(row == j, parts[j], total)
        return total

    low = by_row([jnp.full(c.shape, scale[lat * 2 * ROWS + 2 * j]) for j in range(ROWS)])
    high = by_row([jnp.full(c.shape, scale[lat * 2 * ROWS + 2 * j + 1]) for j in range(ROWS)])
    lower = face_weights(jnp.concatenate([below, c[: ROWS - 1]], axis=0))
    upper = face_weights(c)
    offsets = {}
    for o in range(-3, 4):
        total = jnp.zeros_like(c)
        if o <= 2:
            total = total + low * lower[o + 3]
        if o >= -2:
            total = total - high * upper[o + 2]
        offsets[o] = total
    zero = jnp.zeros_like(c)
    return [by_row([offsets.get(r - j, zero) for j in range(ROWS)]) for r in range(-3, ROWS + 3)]


def weights_kernel(fields, last, scale, c, c_near, c_far, x, t, zon_in, zon_t_in, relay, out, zon, zon_t):
    lat = lax.axis_index("lat")
    odd = lax.rem(lat, 2)
    lons = x.shape[-1]
    for lev in range(LEVELS):
        own = c[lev]
        north_row = slice(ROWS - 1, ROWS)
        below = jnp.where(odd == 1, c_near[lev, north_row, :], c_far[lev, north_row, :])
        below = jnp.where(lat == 0, -pltpu.roll(own, lons // 2, 1)[0:1], below)
        for r, w in enumerate(row_weights(own, below, scale, lat)):
            out[r, lev] = w

    def pole(rows):
        for lev in range(LEVELS):
            for source, at in rows:
                v = pltpu.roll(t[lev], lons // 2, 1)
                v = jnp.broadcast_to(v[source : source + 1], v.shape)
                zon_t[lev] = zon_t[lev] + out[at, lev] * v

            @pl.loop(0, fields)
            def _(i):
                total = zon[i, lev]
                v = pltpu.roll(x[i, lev], lons // 2, 1)
                for source, at in rows:
                    total = total + out[at, lev] * jnp.broadcast_to(v[source : source + 1], v.shape)
                zon[i, lev] = total

            for _, at in rows:
                out[at, lev] = jnp.zeros_like(out[at, lev])

    @pl.when(lat == 0)
    def _():
        pole([(d - 1, 3 - d) for d in range(1, 4)])

    @pl.when(lat == last)
    def _():
        pole([(ROWS - d, ROWS + 2 + d) for d in range(1, 4)])


def zonal_kernel(fields, x, t, n, f, zon, zon_t, w):
    lons = x.shape[-1]

    def shifted(values, k):
        return values if k == 0 else pltpu.roll(values, (-k) % lons, 1)

    def advance(v):
        flux = w[1] * v
        for k in (0, 2, 3, 4, 5, 6):
            flux = flux + w[k] * shifted(v, 1 - k)
        return v - (shifted(flux, 1) - flux)

    def stacked(ref):
        return jnp.concatenate([ref[lev] for lev in range(LEVELS)], axis=0)

    whole = stacked(n)
    s = parabola_weights(stacked(f))
    zero = jnp.zeros_like(s[0])
    n0, n1 = whole == 0, whole == 1

    def pick(a, b, d):
        return jnp.where(n0, a, jnp.where(n1, b, d))

    w[0] = pick(s[4], zero, zero)
    w[1] = pick(s[3], s[4], zero)
    w[2] = pick(s[2], s[3] + 1.0, s[4] + 1.0)
    w[3] = pick(s[1], s[2], s[3] + 1.0)
    w[4] = pick(s[0], s[1], s[2])
    w[5] = pick(zero, s[0], s[1])
    w[6] = pick(zero, zero, s[0])

    total = advance(stacked(t))
    for lev in range(LEVELS):
        zon_t[lev] = total[lev * ROWS : (lev + 1) * ROWS]

    @pl.loop(0, fields, step=2)
    def _(start):
        for i in (start, start + 1):
            total = advance(stacked(x.at[i]))
            for lev in range(LEVELS):
                zon[i, lev] = total[lev * ROWS : (lev + 1) * ROWS]


def fin_kernel(skip, count, direct, *refs):
    if direct:
        x, zon, near, far, w, t, zon_t, adv, adv_t = refs
    else:
        x, zon, near, far, w, adv = refs
    chunks = w.shape[-1] // LANE

    def body(odd):
        for lev in range(LEVELS):
            for chunk in range(chunks):
                lane = lanes(chunk)
                weights = [w[r, lev, :, lane] for r in range(ROWS + 6)]

                def total_of(total, own_row, near_row, far_row):
                    for r in range(-3, ROWS + 3):
                        if 0 <= r < ROWS:
                            v = own_row(r)
                        else:
                            d = -r if r < 0 else r - ROWS + 1
                            v = near_row(d) if (r < 0) == odd else far_row(d)
                        total = total + weights[r + 3] * jnp.broadcast_to(v, total.shape)
                    return total

                def gathered(ref, f):
                    return lambda d: ref[(d - 1) * LEVELS + lev, f : f + 1, lane]

                def swapped(ref, f):
                    def row_at(d):
                        row = side_rows(odd)[d - 1]
                        return ref[f, lev, row : row + 1, lane]

                    return row_at

                def gathered_t(ref):
                    def row_at(d):
                        at = (d - 1) * LEVELS + lev
                        return ref[3 * LEVELS, at : at + 1, lane]

                    return row_at

                for f in range(count):
                    adv[f, lev, :, lane] = total_of(
                        zon[skip + f, lev, :, lane],
                        lambda r: x[skip + f, lev, r : r + 1, lane],
                        gathered(near, f) if direct else swapped(near, f),
                        gathered(far, f),
                    )
                if direct:
                    adv_t[lev, :, lane] = total_of(
                        zon_t[lev, :, lane],
                        lambda r: t[lev, r : r + 1, lane],
                        gathered_t(near),
                        gathered_t(far),
                    )

    both(parity(), body)


def remap_kernel(parts, levels, *refs):
    own, peer = refs[:parts], refs[parts : 2 * parts]
    t_own, t_peer, columns, out, out_t, out_phi, weights, vapour, thick = refs[2 * parts :]
    group = lax.axis_index("lev")
    chunks = out.shape[-1] // LANE
    sources = [(own, t_own, lev, group * LEVELS + lev) for lev in range(LEVELS)]
    sources += [(peer, t_peer, lev, (1 - group) * LEVELS + lev) for lev in range(LEVELS)]

    for k in range(levels):
        upper = columns[k]
        share = columns[levels + k]
        water = None
        heat = None
        for s, (adv, temp, lev, level) in enumerate(sources):
            at = level.astype(jnp.float32)
            w = jnp.where(upper == at, 1.0 - share, jnp.where(upper + 1.0 == at, share, 0.0))
            weights[k, s] = w
            water = w * adv[0][0, lev] if water is None else water + w * adv[0][0, lev]
            heat = w * temp[lev] if heat is None else heat + w * temp[lev]
        thick[k] = heat * (1.0 + 0.608 * water) * columns[2 * levels + k]
        thick[levels + k] = heat
    deeper = columns[3 * levels]
    for k in range(levels - 1, -1, -1):
        layer = thick[k]
        thick[k] = deeper + 0.5 * layer
        deeper = deeper + layer
    for lev in range(LEVELS):
        out_phi[lev] = thick[group * LEVELS + lev]
        out_t[lev] = thick[levels + group * LEVELS + lev]

    for chunk in range(chunks):
        lane = lanes(chunk)
        ws = [
            [weights[group * LEVELS + lev, s, :, lane] for s in range(2 * LEVELS)]
            for lev in range(LEVELS)
        ]
        field = 0
        for part in range(parts):
            for f in range(own[part].shape[0]):
                values = [adv[part][f, lev, :, lane] for adv, _, lev, _ in sources]
                for lev in range(LEVELS):
                    total = ws[lev][0] * values[0]
                    for s in range(1, 2 * LEVELS):
                        total = total + ws[lev][s] * values[s]
                    out[field, lev, :, lane] = total
                field += 1


def call(kernel, outs, scratch=(), specs=None, cost=(0, 0), limit=12, aliases=None):
    single = not isinstance(outs, list)
    shapes = tuple(jax.ShapeDtypeStruct(s, jnp.float32) for s in ([outs] if single else outs))
    return pl.pallas_call(
        kernel,
        out_shape=shapes[0] if single else shapes,
        scratch_shapes=[pltpu.VMEM(s, jnp.float32) for s in scratch],
        compiler_params=pltpu.CompilerParams(vmem_limit_bytes=limit * 2**20),
        cost_estimate=pl.CostEstimate(flops=cost[0], bytes_accessed=cost[1], transcendentals=0),
        input_output_aliases=aliases or {},
        **({} if specs is None else {"in_specs": specs}),
    )


def on_device(
    constituent_densities,
    thermal_state,
    integer_boxes_traversed,
    partial_crossing_share,
    northward_crossing_share,
    higher_donor_stratum,
    deeper_donor_share,
    napierian_thickness_quotient,
    ground_gravity_height,
):
    x, t, c = constituent_densities, thermal_state, northward_crossing_share
    fields, _, _, lons = x.shape
    levels = higher_donor_stratum.shape[0]
    bands = lax.axis_size("lat")
    lat_total = bands * ROWS

    pairs = [(i, i ^ 1) for i in range(bands)]
    across = [(i, i + 1 if i % 2 else i - 1) for i in range(1, bands - 1)]
    relays = [(i, i + 2) for i in range(0, bands - 2, 2)] + [(i, i - 2) for i in range(3, bands, 2)]
    cores = [(0, 1), (1, 0)]

    def swap(v):
        return lax.ppermute(v, "lat", pairs)

    def exchange_across(v):
        return lax.ppermute(v, "lat", across)

    def pass_on(v):
        return lax.ppermute(v, "lat", relays)

    def other_core(v):
        return lax.ppermute(v, "lev", cores)

    face = np.arange(lat_total + 1)
    face_sine = np.sin(math.pi * np.minimum(face, lat_total - face) / lat_total)
    row_sine = np.sin(math.pi * (np.arange(lat_total) + 0.5) / lat_total)
    scale = np.stack([face_sine[:-1] / row_sine, face_sine[1:] / row_sine], 1)
    scale = jnp.asarray(scale.reshape(-1).astype(np.float32))

    smem, vmem = pl.BlockSpec(memory_space=pltpu.SMEM), pl.BlockSpec(memory_space=pltpu.VMEM)
    direct = fields // 2
    swapped = fields - direct
    direct_shape = (3 * LEVELS + 1, direct, lons)

    c_near = swap(c)
    near_a = swap(call(copy_kernel, (swapped,) + x.shape[1:])(x))
    near_b = swap(call(near_kernel, direct_shape)(x, t))
    c_far = exchange_across(c)

    zon, zon_t = call(
        functools.partial(zonal_kernel, fields),
        [x.shape, t.shape],
        [(7, LEVELS * ROWS, lons)],
        cost=(4000000000, 3000000),
    )(x, t, integer_boxes_traversed, partial_crossing_share)

    relay, direct_rows = call(relay_kernel, [(3 * LEVELS, swapped, lons), direct_shape])(near_a, x, t)
    far_a = pass_on(relay)
    far_b = exchange_across(direct_rows)

    columns = jnp.concatenate(
        [
            higher_donor_stratum.astype(jnp.float32),
            deeper_donor_share,
            napierian_thickness_quotient,
            ground_gravity_height[None],
        ],
        axis=0,
    )
    peer_columns = other_core(columns)
    columns = jnp.where(
        lax.axis_index("lev") == 0,
        jnp.concatenate([columns, peer_columns], -1),
        jnp.concatenate([peer_columns, columns], -1),
    )

    weights, zon, zon_t = call(
        functools.partial(weights_kernel, fields, bands - 1),
        [(ROWS + 6, LEVELS, ROWS, lons), x.shape, t.shape],
        (),
        [smem] + [vmem] * 8,
        cost=(2000000000, 3000000),
        aliases={6: 1, 7: 2},
    )(scale, c, c_near, c_far, x, t, zon, zon_t, relay)

    adv_a = call(
        functools.partial(fin_kernel, 0, swapped, False),
        (swapped,) + x.shape[1:],
        cost=(200000000, 1000000),
    )(x, zon, near_a, far_a, weights)
    peer_a = other_core(adv_a)
    adv_b, adv_t = call(
        functools.partial(fin_kernel, swapped, direct, True),
        [(direct,) + x.shape[1:], t.shape],
        cost=(200000000, 1000000),
    )(x, zon, near_b, far_b, weights, t, zon_t)
    peer_b = other_core(adv_b)
    peer_t = other_core(adv_t)
    return call(
        functools.partial(remap_kernel, 2, levels),
        [x.shape, t.shape, t.shape],
        [(levels, 2 * LEVELS, ROWS, lons), (2 * LEVELS, ROWS, lons), (2 * levels, ROWS, lons)],
        cost=(3000000, 3000000),
    )(adv_a, adv_b, peer_a, peer_b, adv_t, peer_t, columns)


def solution(mesh):
    return jax.shard_map(
        on_device,
        mesh=mesh,
        in_specs=(
            P("ens", "lev", "lat", None),
            P(("ens", "lev"), "lat", None),
            P(("ens", "lev"), "lat", None),
            P(("ens", "lev"), "lat", None),
            P(("ens", "lev"), "lat", None),
            P("ens", "lat", "lev"),
            P("ens", "lat", "lev"),
            P("ens", "lat", "lev"),
            P(("ens", "lat"), "lev"),
        ),
        out_specs=(
            P("ens", "lev", "lat", None),
            P(("ens", "lev"), "lat", None),
            P(("ens", "lev"), "lat", None),
        ),
        check_vma=False,
    )
```

```python
import functools
import math

import jax
import jax.numpy as jnp
import numpy as np
from jax import lax
from jax.experimental import pallas as pl
from jax.experimental.pallas import tpu as pltpu
from jax.sharding import PartitionSpec as P

ROWS = 4
LEVELS = 2
LANE = 128


def lanes(chunk):
    return pl.ds(chunk * LANE, LANE)


def parity():
    return lax.rem(lax.axis_index("lat"), 2)


def both(odd, body):
    @pl.when(odd == 1)
    def _():
        body(True)

    @pl.when(odd == 0)
    def _():
        body(False)


def copy_kernel(x, out):
    out[...] = x[: out.shape[0]]


def side_rows(to_north):
    return (ROWS - 1, ROWS - 2, ROWS - 3) if to_north else (0, 1, 2)


def gather_rows(rows, x, t, out):
    count = out.shape[1]
    skip = x.shape[0] - count
    for d, row in enumerate(rows):
        for lev in range(LEVELS):
            at = d * LEVELS + lev
            for f in range(count):
                out[at, f : f + 1, :] = x[skip + f, lev, row : row + 1, :]
            out[3 * LEVELS, at : at + 1, :] = t[lev, row : row + 1, :]


def relay_kernel(swapped, relay):
    def body(odd):
        for d, row in enumerate(side_rows(not odd)):
            for lev in range(LEVELS):
                for f in range(swapped.shape[0]):
                    relay[d * LEVELS + lev, f : f + 1, :] = swapped[f, lev, row : row + 1, :]

    both(parity(), body)


def parabola_weights(share):
    half = 0.5 * share
    curve = half * (1.0 - share * (2.0 / 3.0))
    right = (1.0 - half - 3.0 * curve) * (1.0 / 12.0)
    left = (half - 3.0 * curve) * (1.0 / 12.0)
    return (
        -share * left,
        share * (7.0 * left - right),
        share * (7.0 * (left + right) + 6.0 * curve),
        share * (7.0 * right - left),
        -share * right,
    )


def face_weights(courant):
    t = parabola_weights(jnp.abs(courant))
    north = courant >= 0.0
    zero = jnp.zeros_like(courant)
    return (
        jnp.where(north, t[0], zero),
        jnp.where(north, t[1], -t[4]),
        jnp.where(north, t[2], -t[3]),
        jnp.where(north, t[3], -t[2]),
        jnp.where(north, t[4], -t[1]),
        jnp.where(north, zero, -t[0]),
    )


def row_weights(c, below, scale, lat):
    row = lax.broadcasted_iota(jnp.int32, c.shape, 0)

    def by_row(parts):
        total = parts[ROWS - 1]
        for j in range(ROWS - 2, -1, -1):
            total = jnp.where(row == j, parts[j], total)
        return total

    low = by_row([jnp.full(c.shape, scale[lat * 2 * ROWS + 2 * j]) for j in range(ROWS)])
    high = by_row([jnp.full(c.shape, scale[lat * 2 * ROWS + 2 * j + 1]) for j in range(ROWS)])
    lower = face_weights(jnp.concatenate([below, c[: ROWS - 1]], axis=0))
    upper = face_weights(c)
    offsets = {}
    for o in range(-3, 4):
        total = jnp.zeros_like(c)
        if o <= 2:
            total = total + low * lower[o + 3]
        if o >= -2:
            total = total - high * upper[o + 2]
        offsets[o] = total
    zero = jnp.zeros_like(c)
    return [by_row([offsets.get(r - j, zero) for j in range(ROWS)]) for r in range(-3, ROWS + 3)]


def stacked(ref):
    return jnp.concatenate([ref[lev] for lev in range(LEVELS)], axis=0)


def weights_kernel(
    fields, last, scale, c, c_south, x, t, zon_in, zon_t_in, relay, out, zon, zon_t, direct, ws
):
    lat = lax.axis_index("lat")
    odd = lax.rem(lat, 2)
    lons = x.shape[-1]
    both(odd, lambda is_odd: gather_rows(side_rows(is_odd), x, t, direct))
    for lev in range(LEVELS):
        own = c[lev]
        below = c_south[lev, ROWS - 1 : ROWS, :]
        below = jnp.where(lat == 0, -pltpu.roll(own, lons // 2, 1)[0:1], below)
        for r, w in enumerate(row_weights(own, below, scale, lat)):
            out[r, lev] = w

    def pole(rows):
        for k, (_, at) in enumerate(rows):
            ws[k] = stacked(out.at[at])
            for lev in range(LEVELS):
                out[at, lev] = jnp.zeros_like(out[at, lev])

        def beyond(ref):
            v = pltpu.roll(stacked(ref), lons // 2, 1)
            total = jnp.zeros_like(v)
            for k, (source, _) in enumerate(rows):
                both_rows = [
                    jnp.broadcast_to(v[r : r + 1], (ROWS, lons))
                    for r in range(source, LEVELS * ROWS, ROWS)
                ]
                total = total + ws[k] * jnp.concatenate(both_rows, axis=0)
            return [total[lev * ROWS : (lev + 1) * ROWS] for lev in range(LEVELS)]

        for lev, part in enumerate(beyond(t)):
            zon_t[lev] = zon_t[lev] + part

        @pl.loop(0, fields, step=2)
        def _(start):
            for i in (start, start + 1):
                for lev, part in enumerate(beyond(x.at[i])):
                    zon[i, lev] = zon[i, lev] + part

    @pl.when(lat == 0)
    def _():
        pole([(d - 1, 3 - d) for d in range(1, 4)])

    @pl.when(lat == last)
    def _():
        pole([(ROWS - d, ROWS + 2 + d) for d in range(1, 4)])


def zonal_kernel(fields, x, t, n, f, c, zon, zon_t, near, c_copy, w):
    lons = x.shape[-1]
    c_copy[...] = c[...]
    both(parity(), lambda odd: gather_rows(side_rows(not odd), x, t, near))

    def shifted(values, k):
        return values if k == 0 else pltpu.roll(values, (-k) % lons, 1)

    def advance(v):
        flux = w[1] * v
        for k in (0, 2, 3, 4, 5, 6):
            flux = flux + w[k] * shifted(v, 1 - k)
        return v - (shifted(flux, 1) - flux)

    whole = stacked(n)
    s = parabola_weights(stacked(f))
    zero = jnp.zeros_like(s[0])
    n0, n1 = whole == 0, whole == 1

    def pick(a, b, d):
        return jnp.where(n0, a, jnp.where(n1, b, d))

    w[0] = pick(s[4], zero, zero)
    w[1] = pick(s[3], s[4], zero)
    w[2] = pick(s[2], s[3] + 1.0, s[4] + 1.0)
    w[3] = pick(s[1], s[2], s[3] + 1.0)
    w[4] = pick(s[0], s[1], s[2])
    w[5] = pick(zero, s[0], s[1])
    w[6] = pick(zero, zero, s[0])

    total = advance(stacked(t))
    for lev in range(LEVELS):
        zon_t[lev] = total[lev * ROWS : (lev + 1) * ROWS]

    @pl.loop(0, fields, step=2)
    def _(start):
        for i in (start, start + 1):
            total = advance(stacked(x.at[i]))
            for lev in range(LEVELS):
                zon[i, lev] = total[lev * ROWS : (lev + 1) * ROWS]


def fin_kernel(skip, count, direct, *refs):
    if direct:
        x, zon, near, far, w, t, zon_t, adv = refs
    else:
        x, zon, near, far, w, _, adv = refs
    chunks = w.shape[-1] // LANE

    def body(odd):
        for lev in range(LEVELS):
            for chunk in range(chunks):
                lane = lanes(chunk)
                weights = [w[r, lev, :, lane] for r in range(ROWS + 6)]

                def total_of(total, own_row, near_row, far_row):
                    for r in range(-3, ROWS + 3):
                        if 0 <= r < ROWS:
                            v = own_row(r)
                        else:
                            d = -r if r < 0 else r - ROWS + 1
                            v = near_row(d) if (r < 0) == odd else far_row(d)
                        total = total + weights[r + 3] * jnp.broadcast_to(v, total.shape)
                    return total

                def gathered(ref, f):
                    return lambda d: ref[(d - 1) * LEVELS + lev, f : f + 1, lane]

                def swapped(ref, f):
                    def row_at(d):
                        row = side_rows(odd)[d - 1]
                        return ref[f, lev, row : row + 1, lane]

                    return row_at

                def gathered_t(ref):
                    def row_at(d):
                        at = (d - 1) * LEVELS + lev
                        return ref[3 * LEVELS, at : at + 1, lane]

                    return row_at

                for f in range(count):
                    adv[f, lev, :, lane] = total_of(
                        zon[skip + f, lev, :, lane],
                        lambda r: x[skip + f, lev, r : r + 1, lane],
                        gathered(near, f) if direct else swapped(near, f),
                        gathered(far, f),
                    )
                if direct:
                    adv[count, lev, :, lane] = total_of(
                        zon_t[lev, :, lane],
                        lambda r: t[lev, r : r + 1, lane],
                        gathered_t(near),
                        gathered_t(far),
                    )

    both(parity(), body)


def mix_kernel(levels, columns, weights):
    group = lax.axis_index("lev")
    for k in range(levels):
        upper = columns[k]
        share = columns[levels + k]
        for s in range(2 * LEVELS):
            level = (group if s < LEVELS else 1 - group) * LEVELS + s % LEVELS
            at = level.astype(jnp.float32)
            weights[k, s] = jnp.where(
                upper == at, 1.0 - share, jnp.where(upper + 1.0 == at, share, 0.0)
            )


def mixed(weights, values):
    total = weights[0] * values[0]
    for w, v in zip(weights[1:], values[1:]):
        total = total + w * v
    return total


def remap_fields(skip, count, own, peer, weights, out, buffer, sems):
    group = lax.axis_index("lev")
    chunks = out.shape[-1] // LANE
    copies = []
    step = 4
    for first in range(0, count, step):
        for chunk in range(chunks):
            lane = lanes(chunk)
            ws = [
                [weights[group * LEVELS + lev, s, :, lane] for s in range(2 * LEVELS)]
                for lev in range(LEVELS)
            ]
            for f in range(first, first + step):
                values = [adv[f, lev, :, lane] for adv in (own, peer) for lev in range(LEVELS)]
                for lev in range(LEVELS):
                    buffer[f, lev, :, lane] = mixed(ws[lev], values)
        copy = pltpu.make_async_copy(
            buffer.at[pl.ds(first, step)],
            out.at[pl.ds(skip + first, step)],
            sems.at[first // step],
        )
        copy.start()
        copies.append(copy)
    return copies


def remap_first_kernel(count, own, peer, weights, out, buffer, sems):
    for copy in remap_fields(0, count, own, peer, weights, out, buffer, sems):
        copy.wait()


def remap_last_kernel(
    skip, count, levels, own, peer, first_own, first_peer, weights, columns, out_in,
    out, out_t, out_phi, buffer, thick, sems,
):
    group = lax.axis_index("lev")
    copies = remap_fields(skip, count, own, peer, weights, out, buffer, sems)
    vapour = [adv[0, lev] for adv in (first_own, first_peer) for lev in range(LEVELS)]
    temp = [adv[count, lev] for adv in (own, peer) for lev in range(LEVELS)]
    for k in range(levels):
        ws = [weights[k, s] for s in range(2 * LEVELS)]
        water = mixed(ws, vapour)
        heat = mixed(ws, temp)
        thick[k] = heat * (1.0 + 0.608 * water) * columns[2 * levels + k]
        thick[levels + k] = heat
    deeper = columns[3 * levels]
    for k in range(levels - 1, -1, -1):
        layer = thick[k]
        thick[k] = deeper + 0.5 * layer
        deeper = deeper + layer
    for lev in range(LEVELS):
        out_phi[lev] = thick[group * LEVELS + lev]
        out_t[lev] = thick[levels + group * LEVELS + lev]
    for copy in copies:
        copy.wait()


def call(kernel, outs, scratch=(), specs=None, cost=(0, 0), limit=12, aliases=None, out_specs=None):
    single = not isinstance(outs, list)
    shapes = tuple(jax.ShapeDtypeStruct(s, jnp.float32) for s in ([outs] if single else outs))
    extra = {} if specs is None else {"in_specs": specs}
    if out_specs is not None:
        extra["out_specs"] = out_specs
    return pl.pallas_call(
        kernel,
        out_shape=shapes[0] if single else shapes,
        scratch_shapes=[pltpu.VMEM(s, jnp.float32) if isinstance(s, tuple) else s for s in scratch],
        compiler_params=pltpu.CompilerParams(vmem_limit_bytes=limit * 2**20),
        cost_estimate=pl.CostEstimate(flops=cost[0], bytes_accessed=cost[1], transcendentals=0),
        input_output_aliases=aliases or {},
        **extra,
    )


def on_device(
    constituent_densities,
    thermal_state,
    integer_boxes_traversed,
    partial_crossing_share,
    northward_crossing_share,
    higher_donor_stratum,
    deeper_donor_share,
    napierian_thickness_quotient,
    ground_gravity_height,
):
    x, t, c = constituent_densities, thermal_state, northward_crossing_share
    fields, _, _, lons = x.shape
    levels = higher_donor_stratum.shape[0]
    bands = lax.axis_size("lat")
    lat_total = bands * ROWS

    pairs = [(i, i ^ 1) for i in range(bands)]
    across = [(i, i + 1 if i % 2 else i - 1) for i in range(1, bands - 1)]
    north = [(i, i + 1) for i in range(bands - 1)]
    relays = [(i, i + 2) for i in range(0, bands - 2, 2)] + [(i, i - 2) for i in range(3, bands, 2)]
    cores = [(0, 1), (1, 0)]

    def swap(v):
        return lax.ppermute(v, "lat", pairs)

    def exchange_across(v):
        return lax.ppermute(v, "lat", across)

    def pass_on(v):
        return lax.ppermute(v, "lat", relays)

    def other_core(v):
        return lax.ppermute(v, "lev", cores)

    face = np.arange(lat_total + 1)
    face_sine = np.sin(math.pi * np.minimum(face, lat_total - face) / lat_total)
    row_sine = np.sin(math.pi * (np.arange(lat_total) + 0.5) / lat_total)
    scale = np.stack([face_sine[:-1] / row_sine, face_sine[1:] / row_sine], 1)
    scale = jnp.asarray(scale.reshape(-1).astype(np.float32))

    smem, vmem = pl.BlockSpec(memory_space=pltpu.SMEM), pl.BlockSpec(memory_space=pltpu.VMEM)
    direct = fields // 2
    swapped = fields - direct
    direct_shape = (3 * LEVELS + 1, direct, lons)

    near_a = swap(call(copy_kernel, (swapped,) + x.shape[1:])(x))
    zon, zon_t, near_rows, c_copy = call(
        functools.partial(zonal_kernel, fields),
        [x.shape, t.shape, direct_shape, c.shape],
        [(7, LEVELS * ROWS, lons)],
        cost=(4000000000, 3000000),
    )(x, t, integer_boxes_traversed, partial_crossing_share, c)
    c_south = lax.ppermute(c_copy, "lat", north)
    near_b = swap(near_rows)

    relay = call(relay_kernel, (3 * LEVELS, swapped, lons))(near_a)
    far_a = pass_on(relay)

    columns = jnp.concatenate(
        [
            higher_donor_stratum.astype(jnp.float32),
            deeper_donor_share,
            napierian_thickness_quotient,
            ground_gravity_height[None],
        ],
        axis=0,
    )
    peer_columns = other_core(columns)
    columns = jnp.where(
        lax.axis_index("lev") == 0,
        jnp.concatenate([columns, peer_columns], -1),
        jnp.concatenate([peer_columns, columns], -1),
    )

    weights, zon, zon_t, far_rows = call(
        functools.partial(weights_kernel, fields, bands - 1),
        [(ROWS + 6, LEVELS, ROWS, lons), x.shape, t.shape, direct_shape],
        [(3, LEVELS * ROWS, lons)],
        [smem] + [vmem] * 7,
        cost=(2000000000, 3000000),
        aliases={5: 1, 6: 2},
    )(scale, c, c_south, x, t, zon, zon_t, relay)
    far_b = exchange_across(far_rows)
    mix = call(
        functools.partial(mix_kernel, levels), (levels, 2 * LEVELS, ROWS, lons), cost=(400000000, 1000000)
    )(columns)

    adv_a = call(
        functools.partial(fin_kernel, 0, swapped, False),
        (swapped,) + x.shape[1:],
        cost=(200000000, 1000000),
    )(x, zon, near_a, far_a, weights, mix)
    peer_a = other_core(adv_a)
    adv_b = call(
        functools.partial(fin_kernel, swapped, direct, True),
        (direct + 1,) + x.shape[1:],
        cost=(200000000, 1000000),
    )(x, zon, near_b, far_b, weights, t, zon_t)
    peer_b = other_core(adv_b)

    anywhere = pl.BlockSpec(memory_space=pl.ANY)
    out = call(
        functools.partial(remap_first_kernel, swapped),
        x.shape,
        [(swapped,) + x.shape[1:], pltpu.SemaphoreType.DMA((swapped // 4,))],
        cost=(200000000, 1000000),
        out_specs=anywhere,
    )(adv_a, peer_a, mix)
    return call(
        functools.partial(remap_last_kernel, swapped, direct, levels),
        [x.shape, t.shape, t.shape],
        [
            (direct,) + x.shape[1:],
            (2 * levels, ROWS, lons),
            pltpu.SemaphoreType.DMA((direct // 4,)),
        ],
        [vmem] * 6 + [anywhere],
        cost=(200000000, 1000000),
        aliases={6: 0},
        out_specs=(anywhere, vmem, vmem),
    )(adv_b, peer_b, adv_a, peer_a, mix, columns, out)


def solution(mesh):
    return jax.shard_map(
        on_device,
        mesh=mesh,
        in_specs=(
            P("ens", "lev", "lat", None),
            P(("ens", "lev"), "lat", None),
            P(("ens", "lev"), "lat", None),
            P(("ens", "lev"), "lat", None),
            P(("ens", "lev"), "lat", None),
            P("ens", "lat", "lev"),
            P("ens", "lat", "lev"),
            P("ens", "lat", "lev"),
            P(("ens", "lat"), "lev"),
        ),
        out_specs=(
            P("ens", "lev", "lat", None),
            P(("ens", "lev"), "lat", None),
            P(("ens", "lev"), "lat", None),
        ),
        check_vma=False,
    )
```

```python
import functools
import math

import jax
import jax.numpy as jnp
import numpy as np
from jax import lax
from jax.experimental import pallas as pl
from jax.experimental.pallas import tpu as pltpu
from jax.sharding import PartitionSpec as P

ROWS = 4
LEVELS = 2
LANE = 128

COST = dict(zonal=10000, relay=10000, weights=1, mix=1, fin_b=1, fin_a=1, first=1, last=1)


def lanes(chunk):
    return pl.ds(chunk * LANE, LANE)


def parity():
    return lax.rem(lax.axis_index("lat"), 2)


def both(odd, body):
    @pl.when(odd == 1)
    def _():
        body(True)

    @pl.when(odd == 0)
    def _():
        body(False)


def copy_kernel(x, out):
    skip = x.shape[0] - out.shape[0]
    out[...] = x[skip:]


def side_rows(to_north):
    return (ROWS - 1, ROWS - 2, ROWS - 3) if to_north else (0, 1, 2)


def gather_rows(rows, x, t, c, out):
    count = out.shape[1]
    last = 3 * LEVELS
    for d, row in enumerate(rows):
        for lev in range(LEVELS):
            at = d * LEVELS + lev
            for f in range(count):
                out[at, f : f + 1, :] = x[f, lev, row : row + 1, :]
            out[last, at : at + 1, :] = t[lev, row : row + 1, :]
    for lev in range(LEVELS):
        out[last, last + lev : last + lev + 1, :] = c[lev, ROWS - 1 : ROWS, :]


def relay_kernel(swapped, zon_t, relay):
    def body(odd):
        for d, row in enumerate(side_rows(not odd)):
            for lev in range(LEVELS):
                for f in range(swapped.shape[0]):
                    relay[d * LEVELS + lev, f : f + 1, :] = swapped[f, lev, row : row + 1, :]

    both(parity(), body)


def parabola_weights(share):
    half = 0.5 * share
    curve = half * (1.0 - share * (2.0 / 3.0))
    right = (1.0 - half - 3.0 * curve) * (1.0 / 12.0)
    left = (half - 3.0 * curve) * (1.0 / 12.0)
    return (
        -share * left,
        share * (7.0 * left - right),
        share * (7.0 * (left + right) + 6.0 * curve),
        share * (7.0 * right - left),
        -share * right,
    )


def face_weights(courant):
    t = parabola_weights(jnp.abs(courant))
    north = courant >= 0.0
    zero = jnp.zeros_like(courant)
    return (
        jnp.where(north, t[0], zero),
        jnp.where(north, t[1], -t[4]),
        jnp.where(north, t[2], -t[3]),
        jnp.where(north, t[3], -t[2]),
        jnp.where(north, t[4], -t[1]),
        jnp.where(north, zero, -t[0]),
    )


def row_weights(c, below, scale, lat):
    row = lax.broadcasted_iota(jnp.int32, c.shape, 0) % ROWS

    def by_row(parts):
        total = parts[ROWS - 1]
        for j in range(ROWS - 2, -1, -1):
            total = jnp.where(row == j, parts[j], total)
        return total

    low = by_row([jnp.full(c.shape, scale[lat * 2 * ROWS + 2 * j]) for j in range(ROWS)])
    high = by_row([jnp.full(c.shape, scale[lat * 2 * ROWS + 2 * j + 1]) for j in range(ROWS)])
    lower = face_weights(below)
    upper = face_weights(c)
    offsets = {}
    for o in range(-3, 4):
        total = jnp.zeros_like(c)
        if o <= 2:
            total = total + low * lower[o + 3]
        if o >= -2:
            total = total - high * upper[o + 2]
        offsets[o] = total
    zero = jnp.zeros_like(c)
    return [by_row([offsets.get(r - j, zero) for j in range(ROWS)]) for r in range(-3, ROWS + 3)]


def stacked(ref):
    return jnp.concatenate([ref[lev] for lev in range(LEVELS)], axis=0)


def weights_kernel(
    fields, last, scale, c, near, far, x, t, zon_in, zon_t_in, mix, out, zon, zon_t, ws
):
    lat = lax.axis_index("lat")
    odd = lax.rem(lat, 2)
    lons = x.shape[-1]
    block = 3 * LEVELS
    parts = []
    for lev in range(LEVELS):
        own = c[lev]
        at = slice(block + lev, block + lev + 1)
        south = jnp.where(odd == 1, near[block, at, :], far[block, at, :])
        south = jnp.where(lat == 0, -pltpu.roll(own, lons // 2, 1)[0:1], south)
        parts += [south, own[: ROWS - 1]]
    for r, w in enumerate(row_weights(stacked(c), jnp.concatenate(parts, axis=0), scale, lat)):
        for lev in range(LEVELS):
            out[r, lev] = w[lev * ROWS : (lev + 1) * ROWS]

    def pole(rows):
        for k, (_, at) in enumerate(rows):
            ws[k] = stacked(out.at[at])
            for lev in range(LEVELS):
                out[at, lev] = jnp.zeros_like(out[at, lev])

        def beyond(ref):
            v = pltpu.roll(stacked(ref), lons // 2, 1)
            total = jnp.zeros_like(v)
            for k, (source, _) in enumerate(rows):
                both_rows = [
                    jnp.broadcast_to(v[r : r + 1], (ROWS, lons))
                    for r in range(source, LEVELS * ROWS, ROWS)
                ]
                total = total + ws[k] * jnp.concatenate(both_rows, axis=0)
            return [total[lev * ROWS : (lev + 1) * ROWS] for lev in range(LEVELS)]

        for lev, part in enumerate(beyond(t)):
            zon_t[lev] = zon_t[lev] + part

        @pl.loop(0, fields, step=2)
        def _(start):
            for i in (start, start + 1):
                for lev, part in enumerate(beyond(x.at[i])):
                    zon[i, lev] = zon[i, lev] + part

    @pl.when(lat == 0)
    def _():
        pole([(d - 1, 3 - d) for d in range(1, 4)])

    @pl.when(lat == last)
    def _():
        pole([(ROWS - d, ROWS + 2 + d) for d in range(1, 4)])


def zonal_kernel(
    fields, x, t, n, f, c, upper, share, quotient, ground, zon, zon_t, near, far, columns, w
):
    lons = x.shape[-1]
    pack_columns(upper, share, quotient, ground, columns)

    def gather(odd):
        gather_rows(side_rows(not odd), x, t, c, near)
        gather_rows(side_rows(odd), x, t, c, far)

    both(parity(), gather)

    def shifted(values, k):
        return values if k == 0 else pltpu.roll(values, (-k) % lons, 1)

    def advance(v):
        flux = w[1] * v
        for k in (0, 2, 3, 4, 5, 6):
            flux = flux + w[k] * shifted(v, 1 - k)
        return v - (shifted(flux, 1) - flux)

    whole = stacked(n)
    s = parabola_weights(stacked(f))
    zero = jnp.zeros_like(s[0])
    n0, n1 = whole == 0, whole == 1

    def pick(a, b, d):
        return jnp.where(n0, a, jnp.where(n1, b, d))

    w[0] = pick(s[4], zero, zero)
    w[1] = pick(s[3], s[4], zero)
    w[2] = pick(s[2], s[3] + 1.0, s[4] + 1.0)
    w[3] = pick(s[1], s[2], s[3] + 1.0)
    w[4] = pick(s[0], s[1], s[2])
    w[5] = pick(zero, s[0], s[1])
    w[6] = pick(zero, zero, s[0])

    total = advance(stacked(t))
    for lev in range(LEVELS):
        zon_t[lev] = total[lev * ROWS : (lev + 1) * ROWS]

    @pl.loop(0, fields, step=2)
    def _(start):
        for i in (start, start + 1):
            total = advance(stacked(x.at[i]))
            for lev in range(LEVELS):
                zon[i, lev] = total[lev * ROWS : (lev + 1) * ROWS]


def fin_kernel(skip, count, direct, *refs):
    if direct:
        x, zon, near, far, w, t, zon_t, _, adv = refs
    else:
        x, zon, near, far, w, adv = refs
    chunks = w.shape[-1] // LANE

    def body(odd):
        for lev in range(LEVELS):
            for chunk in range(chunks):
                lane = lanes(chunk)
                weights = [w[r, lev, :, lane] for r in range(ROWS + 6)]

                def total_of(total, own_row, near_row, far_row):
                    for r in range(-3, ROWS + 3):
                        if 0 <= r < ROWS:
                            v = own_row(r)
                        else:
                            d = -r if r < 0 else r - ROWS + 1
                            v = near_row(d) if (r < 0) == odd else far_row(d)
                        total = total + weights[r + 3] * jnp.broadcast_to(v, total.shape)
                    return total

                def gathered(ref, f):
                    return lambda d: ref[(d - 1) * LEVELS + lev, f : f + 1, lane]

                def swapped(ref, f):
                    def row_at(d):
                        row = side_rows(odd)[d - 1]
                        return ref[f, lev, row : row + 1, lane]

                    return row_at

                def gathered_t(ref):
                    def row_at(d):
                        at = (d - 1) * LEVELS + lev
                        return ref[3 * LEVELS, at : at + 1, lane]

                    return row_at

                for f in range(count):
                    adv[f, lev, :, lane] = total_of(
                        zon[skip + f, lev, :, lane],
                        lambda r: x[skip + f, lev, r : r + 1, lane],
                        gathered(near, f) if direct else swapped(near, f),
                        gathered(far, f),
                    )
                if direct:
                    adv[count, lev, :, lane] = total_of(
                        zon_t[lev, :, lane],
                        lambda r: t[lev, r : r + 1, lane],
                        gathered_t(near),
                        gathered_t(far),
                    )

    both(parity(), body)


def pack_columns(upper, share, quotient, ground, out):
    levels = upper.shape[0]
    out[:levels] = upper[...].astype(jnp.float32)
    out[levels : 2 * levels] = share[...]
    out[2 * levels : 3 * levels] = quotient[...]
    out[3 * levels] = ground[...]


def mix_kernel(levels, columns, weights):
    group = lax.axis_index("lev")
    for k in range(levels):
        upper = columns[k]
        share = columns[levels + k]
        for s in range(2 * LEVELS):
            level = (group if s < LEVELS else 1 - group) * LEVELS + s % LEVELS
            at = level.astype(jnp.float32)
            weights[k, s] = jnp.where(
                upper == at, 1.0 - share, jnp.where(upper + 1.0 == at, share, 0.0)
            )


def mixed(weights, values):
    total = weights[0] * values[0]
    for w, v in zip(weights[1:], values[1:]):
        total = total + w * v
    return total


def remap_fields(skip, own, peer, weights, out, buffer, sems):
    group = lax.axis_index("lev")
    chunks = out.shape[-1] // LANE
    copies = []
    step = 4
    for first in range(0, buffer.shape[0], step):
        for chunk in range(chunks):
            lane = lanes(chunk)
            ws = [
                [weights[group * LEVELS + lev, s, :, lane] for s in range(2 * LEVELS)]
                for lev in range(LEVELS)
            ]
            for f in range(first, first + step):
                values = [adv[f, lev, :, lane] for adv in (own, peer) for lev in range(LEVELS)]
                for lev in range(LEVELS):
                    buffer[f, lev, :, lane] = mixed(ws[lev], values)
        copy = pltpu.make_async_copy(
            buffer.at[pl.ds(first, step)],
            out.at[pl.ds(skip + first, step)],
            sems.at[first // step],
        )
        copy.start()
        copies.append(copy)
    return copies


def remap_last_kernel(skip, own, peer, weights, out_in, out, buffer, sems):
    for copy in remap_fields(skip, own, peer, weights, out, buffer, sems):
        copy.wait()


def remap_first_kernel(
    levels, own, peer, weights, columns, out, out_t, out_phi, buffer, thick, sems, column_sems
):
    group = lax.axis_index("lev")
    count = buffer.shape[0]
    vapour = [adv[0, lev] for adv in (own, peer) for lev in range(LEVELS)]
    temp = [adv[count, lev] for adv in (own, peer) for lev in range(LEVELS)]
    for k in range(levels):
        ws = [weights[k, s] for s in range(2 * LEVELS)]
        water = mixed(ws, vapour)
        heat = mixed(ws, temp)
        thick[k] = heat * (1.0 + 0.608 * water) * columns[2 * levels + k]
        thick[levels + k] = heat
    deeper = columns[3 * levels]
    for k in range(levels - 1, -1, -1):
        layer = thick[k]
        thick[k] = deeper + 0.5 * layer
        deeper = deeper + layer
    copies = [
        pltpu.make_async_copy(
            thick.at[pl.ds(at + group * LEVELS, LEVELS)], target, column_sems.at[i]
        )
        for i, (at, target) in enumerate(((0, out_phi), (levels, out_t)))
    ]
    for copy in copies:
        copy.start()
    for copy in copies + remap_fields(0, own, peer, weights, out, buffer, sems):
        copy.wait()


def call(kernel, outs, scratch=(), specs=None, cost=0, limit=12, aliases=None, out_specs=None):
    single = not isinstance(outs, list)
    shapes = tuple(jax.ShapeDtypeStruct(s, jnp.float32) for s in ([outs] if single else outs))
    extra = {} if specs is None else {"in_specs": specs}
    if out_specs is not None:
        extra["out_specs"] = out_specs
    return pl.pallas_call(
        kernel,
        out_shape=shapes[0] if single else shapes,
        scratch_shapes=[pltpu.VMEM(s, jnp.float32) if isinstance(s, tuple) else s for s in scratch],
        compiler_params=pltpu.CompilerParams(vmem_limit_bytes=limit * 2**20),
        cost_estimate=pl.CostEstimate(flops=cost * 10**6, bytes_accessed=1000, transcendentals=0),
        input_output_aliases=aliases or {},
        **extra,
    )


def on_device(
    constituent_densities,
    thermal_state,
    integer_boxes_traversed,
    partial_crossing_share,
    northward_crossing_share,
    higher_donor_stratum,
    deeper_donor_share,
    napierian_thickness_quotient,
    ground_gravity_height,
):
    x, t, c = constituent_densities, thermal_state, northward_crossing_share
    fields, _, _, lons = x.shape
    levels = higher_donor_stratum.shape[0]
    bands = lax.axis_size("lat")
    lat_total = bands * ROWS

    pairs = [(i, i ^ 1) for i in range(bands)]
    across = [(i, i + 1 if i % 2 else i - 1) for i in range(1, bands - 1)]
    relays = [(i, i + 2) for i in range(0, bands - 2, 2)] + [(i, i - 2) for i in range(3, bands, 2)]
    cores = [(0, 1), (1, 0)]

    def swap(v):
        return lax.ppermute(v, "lat", pairs)

    def exchange_across(v):
        return lax.ppermute(v, "lat", across)

    def pass_on(v):
        return lax.ppermute(v, "lat", relays)

    def other_core(v):
        return lax.ppermute(v, "lev", cores)

    face = np.arange(lat_total + 1)
    face_sine = np.sin(math.pi * np.minimum(face, lat_total - face) / lat_total)
    row_sine = np.sin(math.pi * (np.arange(lat_total) + 0.5) / lat_total)
    scale = np.stack([face_sine[:-1] / row_sine, face_sine[1:] / row_sine], 1)
    scale = jnp.asarray(scale.reshape(-1).astype(np.float32))

    smem, vmem = pl.BlockSpec(memory_space=pltpu.SMEM), pl.BlockSpec(memory_space=pltpu.VMEM)
    direct = fields // 2
    swapped = fields - direct
    direct_shape = (3 * LEVELS + 1, direct, lons)

    near_a = swap(call(copy_kernel, (swapped,) + x.shape[1:])(x))
    zon, zon_t, near_rows, far_rows, columns = call(
        functools.partial(zonal_kernel, fields),
        [
            x.shape,
            t.shape,
            direct_shape,
            direct_shape,
            (3 * levels + 1,) + ground_gravity_height.shape,
        ],
        [(7, LEVELS * ROWS, lons)],
        cost=COST["zonal"],
    )(
        x,
        t,
        integer_boxes_traversed,
        partial_crossing_share,
        c,
        higher_donor_stratum,
        deeper_donor_share,
        napierian_thickness_quotient,
        ground_gravity_height,
    )
    far_b = exchange_across(far_rows)
    near_b = swap(near_rows)

    relay = call(relay_kernel, (3 * LEVELS, swapped, lons), cost=COST["relay"])(near_a, zon_t)
    far_a = pass_on(relay)

    peer_columns = other_core(columns)
    columns = jnp.where(
        lax.axis_index("lev") == 0,
        jnp.concatenate([columns, peer_columns], -1),
        jnp.concatenate([peer_columns, columns], -1),
    )

    mix = call(
        functools.partial(mix_kernel, levels), (levels, 2 * LEVELS, ROWS, lons), cost=COST["mix"]
    )(columns)
    weights, zon, zon_t = call(
        functools.partial(weights_kernel, fields, bands - 1),
        [(ROWS + 6, LEVELS, ROWS, lons), x.shape, t.shape],
        [(3, LEVELS * ROWS, lons)],
        [smem] + [vmem] * 8,
        cost=COST["weights"],
        aliases={6: 1, 7: 2},
    )(scale, c, near_b, far_b, x, t, zon, zon_t, mix)

    adv_b = call(
        functools.partial(fin_kernel, 0, direct, True),
        (direct + 1,) + x.shape[1:],
        cost=COST["fin_b"],
    )(x, zon, near_b, far_b, weights, t, zon_t, mix)
    peer_b = other_core(adv_b)
    adv_a = call(
        functools.partial(fin_kernel, direct, swapped, False),
        (swapped,) + x.shape[1:],
        cost=COST["fin_a"],
    )(x, zon, near_a, far_a, weights)
    peer_a = other_core(adv_a)

    anywhere = pl.BlockSpec(memory_space=pl.ANY)
    out, out_t, out_phi = call(
        functools.partial(remap_first_kernel, levels),
        [x.shape, t.shape, t.shape],
        [
            (direct,) + x.shape[1:],
            (2 * levels, ROWS, lons),
            pltpu.SemaphoreType.DMA((direct // 4,)),
            pltpu.SemaphoreType.DMA((2,)),
        ],
        cost=COST["first"],
        out_specs=(anywhere,) * 3,
    )(adv_b, peer_b, mix, columns)
    out = call(
        functools.partial(remap_last_kernel, direct),
        x.shape,
        [(swapped,) + x.shape[1:], pltpu.SemaphoreType.DMA((swapped // 4,))],
        [vmem] * 3 + [anywhere],
        cost=COST["last"],
        aliases={3: 0},
        out_specs=anywhere,
    )(adv_a, peer_a, mix, out)
    return out, out_t, out_phi


def solution(mesh):
    return jax.shard_map(
        on_device,
        mesh=mesh,
        in_specs=(
            P("ens", "lev", "lat", None),
            P(("ens", "lev"), "lat", None),
            P(("ens", "lev"), "lat", None),
            P(("ens", "lev"), "lat", None),
            P(("ens", "lev"), "lat", None),
            P("ens", "lat", "lev"),
            P("ens", "lat", "lev"),
            P("ens", "lat", "lev"),
            P(("ens", "lat"), "lev"),
        ),
        out_specs=(
            P("ens", "lev", "lat", None),
            P(("ens", "lev"), "lat", None),
            P(("ens", "lev"), "lat", None),
        ),
        check_vma=False,
    )
```

```python
import functools
import math

import jax
import jax.numpy as jnp
import numpy as np
from jax import lax
from jax.experimental import pallas as pl
from jax.experimental.pallas import tpu as pltpu
from jax.sharding import PartitionSpec as P

ROWS = 4
LEVELS = 2
LANE = 128

COST = dict(zonal=10000, relay=10000, early=1, patch=1, fin_b=1, fin_a=1, remap=1)


def lanes(chunk):
    return pl.ds(chunk * LANE, LANE)


def parity():
    return lax.rem(lax.axis_index("lat"), 2)


def both(odd, body):
    @pl.when(odd == 1)
    def _():
        body(True)

    @pl.when(odd == 0)
    def _():
        body(False)


def copy_kernel(x, out):
    skip = x.shape[0] - out.shape[0]
    out[...] = x[skip:]


def side_rows(to_north):
    return (ROWS - 1, ROWS - 2, ROWS - 3) if to_north else (0, 1, 2)


def gather_rows(rows, x, t, c, out):
    count = out.shape[1]
    last = 3 * LEVELS
    for d, row in enumerate(rows):
        for lev in range(LEVELS):
            at = d * LEVELS + lev
            for f in range(count):
                out[at, f : f + 1, :] = x[f, lev, row : row + 1, :]
            out[last, at : at + 1, :] = t[lev, row : row + 1, :]
    for lev in range(LEVELS):
        out[last, last + lev : last + lev + 1, :] = c[lev, ROWS - 1 : ROWS, :]


def relay_kernel(swapped, zon_t, relay):
    def body(odd):
        for d, row in enumerate(side_rows(not odd)):
            for lev in range(LEVELS):
                for f in range(swapped.shape[0]):
                    relay[d * LEVELS + lev, f : f + 1, :] = swapped[f, lev, row : row + 1, :]

    both(parity(), body)


def parabola_weights(share):
    half = 0.5 * share
    curve = half * (1.0 - share * (2.0 / 3.0))
    right = (1.0 - half - 3.0 * curve) * (1.0 / 12.0)
    left = (half - 3.0 * curve) * (1.0 / 12.0)
    return (
        -share * left,
        share * (7.0 * left - right),
        share * (7.0 * (left + right) + 6.0 * curve),
        share * (7.0 * right - left),
        -share * right,
    )


def face_weights(courant):
    t = parabola_weights(jnp.abs(courant))
    north = courant >= 0.0
    zero = jnp.zeros_like(courant)
    return (
        jnp.where(north, t[0], zero),
        jnp.where(north, t[1], -t[4]),
        jnp.where(north, t[2], -t[3]),
        jnp.where(north, t[3], -t[2]),
        jnp.where(north, t[4], -t[1]),
        jnp.where(north, zero, -t[0]),
    )


def row_weights(c, below, scale, lat):
    row = lax.broadcasted_iota(jnp.int32, c.shape, 0) % ROWS

    def by_row(parts):
        total = parts[ROWS - 1]
        for j in range(ROWS - 2, -1, -1):
            total = jnp.where(row == j, parts[j], total)
        return total

    low = by_row([jnp.full(c.shape, scale[lat * 2 * ROWS + 2 * j]) for j in range(ROWS)])
    high = by_row([jnp.full(c.shape, scale[lat * 2 * ROWS + 2 * j + 1]) for j in range(ROWS)])
    lower = face_weights(below)
    upper = face_weights(c)
    offsets = {}
    for o in range(-3, 4):
        total = jnp.zeros_like(c)
        if o <= 2:
            total = total + low * lower[o + 3]
        if o >= -2:
            total = total - high * upper[o + 2]
        offsets[o] = total
    zero = jnp.zeros_like(c)
    return [by_row([offsets.get(r - j, zero) for j in range(ROWS)]) for r in range(-3, ROWS + 3)]


def stacked(ref):
    return jnp.concatenate([ref[lev] for lev in range(LEVELS)], axis=0)


def early_kernel(
    fields, levels, last, scale, columns, c, x, t, zon_in, zon_t_in, mix, out, zon, zon_t, ws
):
    lat = lax.axis_index("lat")
    lons = x.shape[-1]
    mix_weights(levels, columns, mix)
    parts = []
    for lev in range(LEVELS):
        own = c[lev]
        parts += [
            jnp.where(lat == 0, -pltpu.roll(own, lons // 2, 1)[0:1], 0.0),
            own[: ROWS - 1],
        ]
    for r, w in enumerate(row_weights(stacked(c), jnp.concatenate(parts, axis=0), scale, lat)):
        for lev in range(LEVELS):
            out[r, lev] = w[lev * ROWS : (lev + 1) * ROWS]

    def pole(rows):
        for k, (_, at) in enumerate(rows):
            ws[k] = stacked(out.at[at])
            for lev in range(LEVELS):
                out[at, lev] = jnp.zeros_like(out[at, lev])

        def beyond(ref):
            v = pltpu.roll(stacked(ref), lons // 2, 1)
            total = jnp.zeros_like(v)
            for k, (source, _) in enumerate(rows):
                both_rows = [
                    jnp.broadcast_to(v[r : r + 1], (ROWS, lons))
                    for r in range(source, LEVELS * ROWS, ROWS)
                ]
                total = total + ws[k] * jnp.concatenate(both_rows, axis=0)
            return [total[lev * ROWS : (lev + 1) * ROWS] for lev in range(LEVELS)]

        for lev, part in enumerate(beyond(t)):
            zon_t[lev] = zon_t[lev] + part

        @pl.loop(0, fields, step=2)
        def _(start):
            for i in (start, start + 1):
                for lev, part in enumerate(beyond(x.at[i])):
                    zon[i, lev] = zon[i, lev] + part

    @pl.when(lat == 0)
    def _():
        pole([(d - 1, 3 - d) for d in range(1, 4)])

    @pl.when(lat == last)
    def _():
        pole([(ROWS - d, ROWS + 2 + d) for d in range(1, 4)])


def patch_kernel(scale, near, far, weights_in, weights):
    lat = lax.axis_index("lat")
    odd = lax.rem(lat, 2)
    block = 3 * LEVELS
    rows = slice(block, block + LEVELS)
    below = jnp.where(odd == 1, near[block, rows, :], far[block, rows, :])
    below = jnp.where(lat == 0, 0.0, below)
    low = scale[lat * 2 * ROWS]
    for r, part in enumerate(face_weights(below)):
        part = low * part
        for lev in range(LEVELS):
            weights[r, lev, 0:1, :] = weights[r, lev, 0:1, :] + part[lev : lev + 1]


def zonal_kernel(
    fields, x, t, n, f, c, upper, share, quotient, ground, zon, zon_t, near, far, columns, w
):
    lons = x.shape[-1]
    pack_columns(upper, share, quotient, ground, columns)

    def gather(odd):
        gather_rows(side_rows(not odd), x, t, c, near)
        gather_rows(side_rows(odd), x, t, c, far)

    both(parity(), gather)

    def shifted(values, k):
        return values if k == 0 else pltpu.roll(values, (-k) % lons, 1)

    def advance(v):
        flux = w[1] * v
        for k in (0, 2, 3, 4, 5, 6):
            flux = flux + w[k] * shifted(v, 1 - k)
        return v - (shifted(flux, 1) - flux)

    whole = stacked(n)
    s = parabola_weights(stacked(f))
    zero = jnp.zeros_like(s[0])
    n0, n1 = whole == 0, whole == 1

    def pick(a, b, d):
        return jnp.where(n0, a, jnp.where(n1, b, d))

    w[0] = pick(s[4], zero, zero)
    w[1] = pick(s[3], s[4], zero)
    w[2] = pick(s[2], s[3] + 1.0, s[4] + 1.0)
    w[3] = pick(s[1], s[2], s[3] + 1.0)
    w[4] = pick(s[0], s[1], s[2])
    w[5] = pick(zero, s[0], s[1])
    w[6] = pick(zero, zero, s[0])

    total = advance(stacked(t))
    for lev in range(LEVELS):
        zon_t[lev] = total[lev * ROWS : (lev + 1) * ROWS]

    @pl.loop(0, fields, step=2)
    def _(start):
        for i in (start, start + 1):
            total = advance(stacked(x.at[i]))
            for lev in range(LEVELS):
                zon[i, lev] = total[lev * ROWS : (lev + 1) * ROWS]


def fin_kernel(skip, count, direct, *refs):
    if direct:
        x, zon, near, far, w, t, zon_t, adv = refs
    else:
        x, zon, near, far, w, adv = refs
    chunks = w.shape[-1] // LANE

    def body(odd):
        for lev in range(LEVELS):
            for chunk in range(chunks):
                lane = lanes(chunk)
                weights = [w[r, lev, :, lane] for r in range(ROWS + 6)]

                def total_of(total, own_row, near_row, far_row):
                    for r in range(-3, ROWS + 3):
                        if 0 <= r < ROWS:
                            v = own_row(r)
                        else:
                            d = -r if r < 0 else r - ROWS + 1
                            v = near_row(d) if (r < 0) == odd else far_row(d)
                        total = total + weights[r + 3] * jnp.broadcast_to(v, total.shape)
                    return total

                def gathered(ref, f):
                    return lambda d: ref[(d - 1) * LEVELS + lev, f : f + 1, lane]

                def swapped(ref, f):
                    def row_at(d):
                        row = side_rows(odd)[d - 1]
                        return ref[f, lev, row : row + 1, lane]

                    return row_at

                def gathered_t(ref):
                    def row_at(d):
                        at = (d - 1) * LEVELS + lev
                        return ref[3 * LEVELS, at : at + 1, lane]

                    return row_at

                for f in range(count):
                    adv[f, lev, :, lane] = total_of(
                        zon[skip + f, lev, :, lane],
                        lambda r: x[skip + f, lev, r : r + 1, lane],
                        gathered(near, f) if direct else swapped(near, f),
                        gathered(far, f),
                    )
                if direct:
                    adv[count, lev, :, lane] = total_of(
                        zon_t[lev, :, lane],
                        lambda r: t[lev, r : r + 1, lane],
                        gathered_t(near),
                        gathered_t(far),
                    )

    both(parity(), body)


def pack_columns(upper, share, quotient, ground, out):
    levels = upper.shape[0]
    out[:levels] = upper[...].astype(jnp.float32)
    out[levels : 2 * levels] = share[...]
    out[2 * levels : 3 * levels] = quotient[...]
    out[3 * levels] = ground[...]


def mix_weights(levels, columns, weights):
    group = lax.axis_index("lev")
    for k in range(levels):
        upper = columns[k]
        share = columns[levels + k]
        for s in range(2 * LEVELS):
            level = (group if s < LEVELS else 1 - group) * LEVELS + s % LEVELS
            at = level.astype(jnp.float32)
            weights[k, s] = jnp.where(
                upper == at, 1.0 - share, jnp.where(upper + 1.0 == at, share, 0.0)
            )


def mixed(weights, values):
    total = weights[0] * values[0]
    for w, v in zip(weights[1:], values[1:]):
        total = total + w * v
    return total


def remap_kernel(
    levels, own_b, peer_b, own_a, peer_a, weights, columns,
    out, out_t, out_phi, buffer, thick, sems, column_sems,
):
    group = lax.axis_index("lev")
    chunks = out.shape[-1] // LANE
    copies = []
    step = 4
    count = own_b.shape[0] - 1

    def send(source, target, sem):
        copy = pltpu.make_async_copy(source, target, sem)
        copy.start()
        copies.append(copy)

    def blend(first):
        own, peer, skip = (own_b, peer_b, 0) if first < count else (own_a, peer_a, count)
        for chunk in range(chunks):
            lane = lanes(chunk)
            ws = [
                [weights[group * LEVELS + lev, s, :, lane] for s in range(2 * LEVELS)]
                for lev in range(LEVELS)
            ]
            for f in range(first, first + step):
                values = [adv[f - skip, lev, :, lane] for adv in (own, peer) for lev in range(LEVELS)]
                for lev in range(LEVELS):
                    buffer[f, lev, :, lane] = mixed(ws[lev], values)
        send(buffer.at[pl.ds(first, step)], out.at[pl.ds(first, step)], sems.at[first // step])

    fields = buffer.shape[0]
    for first in range(0, fields - step, step):
        blend(first)

    vapour = [adv[0, lev] for adv in (own_b, peer_b) for lev in range(LEVELS)]
    temp = [adv[count, lev] for adv in (own_b, peer_b) for lev in range(LEVELS)]
    for k in range(levels):
        ws = [weights[k, s] for s in range(2 * LEVELS)]
        water = mixed(ws, vapour)
        heat = mixed(ws, temp)
        thick[k] = heat * (1.0 + 0.608 * water) * columns[2 * levels + k]
        thick[levels + k] = heat
    deeper = columns[3 * levels]
    for k in range(levels - 1, -1, -1):
        layer = thick[k]
        thick[k] = deeper + 0.5 * layer
        deeper = deeper + layer
    mine = group * LEVELS
    send(thick.at[pl.ds(mine, LEVELS)], out_phi, column_sems.at[0])
    send(thick.at[pl.ds(levels + mine, LEVELS)], out_t, column_sems.at[1])
    blend(fields - step)
    for copy in copies:
        copy.wait()


def call(kernel, outs, scratch=(), specs=None, cost=0, limit=12, aliases=None, out_specs=None):
    single = not isinstance(outs, list)
    shapes = tuple(jax.ShapeDtypeStruct(s, jnp.float32) for s in ([outs] if single else outs))
    extra = {} if specs is None else {"in_specs": specs}
    if out_specs is not None:
        extra["out_specs"] = out_specs
    return pl.pallas_call(
        kernel,
        out_shape=shapes[0] if single else shapes,
        scratch_shapes=[pltpu.VMEM(s, jnp.float32) if isinstance(s, tuple) else s for s in scratch],
        compiler_params=pltpu.CompilerParams(vmem_limit_bytes=limit * 2**20),
        cost_estimate=pl.CostEstimate(flops=cost * 10**6, bytes_accessed=1000, transcendentals=0),
        input_output_aliases=aliases or {},
        **extra,
    )


def on_device(
    constituent_densities,
    thermal_state,
    integer_boxes_traversed,
    partial_crossing_share,
    northward_crossing_share,
    higher_donor_stratum,
    deeper_donor_share,
    napierian_thickness_quotient,
    ground_gravity_height,
):
    x, t, c = constituent_densities, thermal_state, northward_crossing_share
    fields, _, _, lons = x.shape
    levels = higher_donor_stratum.shape[0]
    bands = lax.axis_size("lat")
    lat_total = bands * ROWS

    pairs = [(i, i ^ 1) for i in range(bands)]
    across = [(i, i + 1 if i % 2 else i - 1) for i in range(1, bands - 1)]
    relays = [(i, i + 2) for i in range(0, bands - 2, 2)] + [(i, i - 2) for i in range(3, bands, 2)]
    cores = [(0, 1), (1, 0)]

    def swap(v):
        return lax.ppermute(v, "lat", pairs)

    def exchange_across(v):
        return lax.ppermute(v, "lat", across)

    def pass_on(v):
        return lax.ppermute(v, "lat", relays)

    def other_core(v):
        return lax.ppermute(v, "lev", cores)

    face = np.arange(lat_total + 1)
    face_sine = np.sin(math.pi * np.minimum(face, lat_total - face) / lat_total)
    row_sine = np.sin(math.pi * (np.arange(lat_total) + 0.5) / lat_total)
    scale = np.stack([face_sine[:-1] / row_sine, face_sine[1:] / row_sine], 1)
    scale = jnp.asarray(scale.reshape(-1).astype(np.float32))

    smem, vmem = pl.BlockSpec(memory_space=pltpu.SMEM), pl.BlockSpec(memory_space=pltpu.VMEM)
    direct = fields // 2
    swapped = fields - direct
    direct_shape = (3 * LEVELS + 1, direct, lons)

    near_a = swap(call(copy_kernel, (swapped,) + x.shape[1:])(x))
    zon, zon_t, near_rows, far_rows, columns = call(
        functools.partial(zonal_kernel, fields),
        [
            x.shape,
            t.shape,
            direct_shape,
            direct_shape,
            (3 * levels + 1,) + ground_gravity_height.shape,
        ],
        [(7, LEVELS * ROWS, lons)],
        cost=COST["zonal"],
    )(
        x,
        t,
        integer_boxes_traversed,
        partial_crossing_share,
        c,
        higher_donor_stratum,
        deeper_donor_share,
        napierian_thickness_quotient,
        ground_gravity_height,
    )
    far_b = exchange_across(far_rows)
    near_b = swap(near_rows)

    relay = call(relay_kernel, (3 * LEVELS, swapped, lons), cost=COST["relay"])(near_a, zon_t)
    far_a = pass_on(relay)

    peer_columns = other_core(columns)
    columns = jnp.where(
        lax.axis_index("lev") == 0,
        jnp.concatenate([columns, peer_columns], -1),
        jnp.concatenate([peer_columns, columns], -1),
    )

    mix, weights, zon, zon_t = call(
        functools.partial(early_kernel, fields, levels, bands - 1),
        [
            (levels, 2 * LEVELS, ROWS, lons),
            (ROWS + 6, LEVELS, ROWS, lons),
            x.shape,
            t.shape,
        ],
        [(3, LEVELS * ROWS, lons)],
        [smem] + [vmem] * 6,
        cost=COST["early"],
        aliases={5: 2, 6: 3},
    )(scale, columns, c, x, t, zon, zon_t)
    weights = call(
        patch_kernel,
        weights.shape,
        (),
        [smem] + [vmem] * 3,
        cost=COST["patch"],
        aliases={3: 0},
    )(scale, near_b, far_b, weights)

    adv_b = call(
        functools.partial(fin_kernel, 0, direct, True),
        (direct + 1,) + x.shape[1:],
        cost=COST["fin_b"],
    )(x, zon, near_b, far_b, weights, t, zon_t)
    peer_b = other_core(adv_b)
    adv_a = call(
        functools.partial(fin_kernel, direct, swapped, False),
        (swapped,) + x.shape[1:],
        cost=COST["fin_a"],
    )(x, zon, near_a, far_a, weights)
    peer_a = other_core(adv_a)

    anywhere = pl.BlockSpec(memory_space=pl.ANY)
    return call(
        functools.partial(remap_kernel, levels),
        [x.shape, t.shape, t.shape],
        [
            x.shape,
            (2 * levels, ROWS, lons),
            pltpu.SemaphoreType.DMA((fields // 4,)),
            pltpu.SemaphoreType.DMA((2,)),
        ],
        cost=COST["remap"],
        out_specs=(anywhere,) * 3,
    )(adv_b, peer_b, adv_a, peer_a, mix, columns)


def solution(mesh):
    return jax.shard_map(
        on_device,
        mesh=mesh,
        in_specs=(
            P("ens", "lev", "lat", None),
            P(("ens", "lev"), "lat", None),
            P(("ens", "lev"), "lat", None),
            P(("ens", "lev"), "lat", None),
            P(("ens", "lev"), "lat", None),
            P("ens", "lat", "lev"),
            P("ens", "lat", "lev"),
            P("ens", "lat", "lev"),
            P(("ens", "lat"), "lev"),
        ),
        out_specs=(
            P("ens", "lev", "lat", None),
            P(("ens", "lev"), "lat", None),
            P(("ens", "lev"), "lat", None),
        ),
        check_vma=False,
    )
```

```python
import functools
import math

import jax
import jax.numpy as jnp
import numpy as np
from jax import lax
from jax.experimental import pallas as pl
from jax.experimental.pallas import tpu as pltpu
from jax.sharding import PartitionSpec as P

ROWS = 4
LEVELS = 2
LANE = 128

COST = dict(zonal=10000, relay=10000, early=1, patch=1, fin_b=1, fin_a=1, first=1, last=1)


def lanes(chunk):
    return pl.ds(chunk * LANE, LANE)


def parity():
    return lax.rem(lax.axis_index("lat"), 2)


def both(odd, body):
    @pl.when(odd == 1)
    def _():
        body(True)

    @pl.when(odd == 0)
    def _():
        body(False)


def copy_kernel(x, out, sems):
    count = out.shape[0]
    skip = x.shape[0] - count
    copies = [
        pltpu.make_async_copy(x.at[skip + i], out.at[i], sems.at[i]) for i in range(count)
    ]
    for copy in copies:
        copy.start()
    for copy in copies:
        copy.wait()


def side_rows(to_north):
    return (ROWS - 1, ROWS - 2, ROWS - 3) if to_north else (0, 1, 2)


def gather_rows(rows, x, t, c, out):
    count = out.shape[1]
    last = 3 * LEVELS
    for d, row in enumerate(rows):
        for lev in range(LEVELS):
            at = d * LEVELS + lev
            for f in range(count):
                out[at, f : f + 1, :] = x[f, lev, row : row + 1, :]
            out[last, at : at + 1, :] = t[lev, row : row + 1, :]
    for lev in range(LEVELS):
        out[last, last + lev : last + lev + 1, :] = c[lev, ROWS - 1 : ROWS, :]


def relay_kernel(swapped, zon_t, relay):
    def body(odd):
        for d, row in enumerate(side_rows(not odd)):
            for lev in range(LEVELS):
                for f in range(swapped.shape[0]):
                    relay[d * LEVELS + lev, f : f + 1, :] = swapped[f, lev, row : row + 1, :]

    both(parity(), body)


def parabola_weights(share):
    half = 0.5 * share
    curve = half * (1.0 - share * (2.0 / 3.0))
    right = (1.0 - half - 3.0 * curve) * (1.0 / 12.0)
    left = (half - 3.0 * curve) * (1.0 / 12.0)
    return (
        -share * left,
        share * (7.0 * left - right),
        share * (7.0 * (left + right) + 6.0 * curve),
        share * (7.0 * right - left),
        -share * right,
    )


def face_weights(courant):
    t = parabola_weights(jnp.abs(courant))
    north = courant >= 0.0
    zero = jnp.zeros_like(courant)
    return (
        jnp.where(north, t[0], zero),
        jnp.where(north, t[1], -t[4]),
        jnp.where(north, t[2], -t[3]),
        jnp.where(north, t[3], -t[2]),
        jnp.where(north, t[4], -t[1]),
        jnp.where(north, zero, -t[0]),
    )


def row_weights(c, below, scale, lat):
    row = lax.broadcasted_iota(jnp.int32, c.shape, 0) % ROWS

    def by_row(parts):
        total = parts[ROWS - 1]
        for j in range(ROWS - 2, -1, -1):
            total = jnp.where(row == j, parts[j], total)
        return total

    low = by_row([jnp.full(c.shape, scale[lat * 2 * ROWS + 2 * j]) for j in range(ROWS)])
    high = by_row([jnp.full(c.shape, scale[lat * 2 * ROWS + 2 * j + 1]) for j in range(ROWS)])
    lower = face_weights(below)
    upper = face_weights(c)
    offsets = {}
    for o in range(-3, 4):
        total = jnp.zeros_like(c)
        if o <= 2:
            total = total + low * lower[o + 3]
        if o >= -2:
            total = total - high * upper[o + 2]
        offsets[o] = total
    zero = jnp.zeros_like(c)
    return [by_row([offsets.get(r - j, zero) for j in range(ROWS)]) for r in range(-3, ROWS + 3)]


def stacked(ref):
    return jnp.concatenate([ref[lev] for lev in range(LEVELS)], axis=0)


def early_kernel(
    fields, levels, last, scale, columns, c, x, t, zon_in, zon_t_in, mix, out, zon, zon_t, factor, ws
):
    lat = lax.axis_index("lat")
    lons = x.shape[-1]
    mix_weights(levels, columns, mix)
    factor[...] = jnp.full(factor.shape, jnp.where(lat == 0, 0.0, scale[lat * 2 * ROWS]))
    parts = []
    for lev in range(LEVELS):
        own = c[lev]
        parts += [
            jnp.where(lat == 0, -pltpu.roll(own, lons // 2, 1)[0:1], 0.0),
            own[: ROWS - 1],
        ]
    for r, w in enumerate(row_weights(stacked(c), jnp.concatenate(parts, axis=0), scale, lat)):
        for lev in range(LEVELS):
            out[r, lev] = w[lev * ROWS : (lev + 1) * ROWS]

    def pole(rows):
        for k, (_, at) in enumerate(rows):
            ws[k] = stacked(out.at[at])
            for lev in range(LEVELS):
                out[at, lev] = jnp.zeros_like(out[at, lev])

        def beyond(ref):
            v = pltpu.roll(stacked(ref), lons // 2, 1)
            total = jnp.zeros_like(v)
            for k, (source, _) in enumerate(rows):
                both_rows = [
                    jnp.broadcast_to(v[r : r + 1], (ROWS, lons))
                    for r in range(source, LEVELS * ROWS, ROWS)
                ]
                total = total + ws[k] * jnp.concatenate(both_rows, axis=0)
            return [total[lev * ROWS : (lev + 1) * ROWS] for lev in range(LEVELS)]

        for lev, part in enumerate(beyond(t)):
            zon_t[lev] = zon_t[lev] + part

        @pl.loop(0, fields, step=2)
        def _(start):
            for i in (start, start + 1):
                for lev, part in enumerate(beyond(x.at[i])):
                    zon[i, lev] = zon[i, lev] + part

    @pl.when(lat == 0)
    def _():
        pole([(d - 1, 3 - d) for d in range(1, 4)])

    @pl.when(lat == last)
    def _():
        pole([(ROWS - d, ROWS + 2 + d) for d in range(1, 4)])


def patch_kernel(factor, near, far, weights_in, weights):
    block = 3 * LEVELS
    rows = slice(block, block + LEVELS)
    below = jnp.where(parity() == 1, near[block, rows, :], far[block, rows, :])
    for r, part in enumerate(face_weights(below)):
        part = factor[...] * part
        for lev in range(LEVELS):
            weights[r, lev, 0:1, :] = weights[r, lev, 0:1, :] + part[lev : lev + 1]


def zonal_kernel(
    fields, x, t, n, f, c, upper, share, quotient, ground, zon, zon_t, near, far, columns, w
):
    lons = x.shape[-1]
    pack_columns(upper, share, quotient, ground, columns)

    def gather(odd):
        gather_rows(side_rows(not odd), x, t, c, near)
        gather_rows(side_rows(odd), x, t, c, far)

    both(parity(), gather)

    def shifted(values, k):
        return values if k == 0 else pltpu.roll(values, (-k) % lons, 1)

    def advance(v):
        flux = w[1] * v
        for k in (0, 2, 3, 4, 5, 6):
            flux = flux + w[k] * shifted(v, 1 - k)
        return v - (shifted(flux, 1) - flux)

    whole = stacked(n)
    s = parabola_weights(stacked(f))
    zero = jnp.zeros_like(s[0])
    n0, n1 = whole == 0, whole == 1

    def pick(a, b, d):
        return jnp.where(n0, a, jnp.where(n1, b, d))

    w[0] = pick(s[4], zero, zero)
    w[1] = pick(s[3], s[4], zero)
    w[2] = pick(s[2], s[3] + 1.0, s[4] + 1.0)
    w[3] = pick(s[1], s[2], s[3] + 1.0)
    w[4] = pick(s[0], s[1], s[2])
    w[5] = pick(zero, s[0], s[1])
    w[6] = pick(zero, zero, s[0])

    total = advance(stacked(t))
    for lev in range(LEVELS):
        zon_t[lev] = total[lev * ROWS : (lev + 1) * ROWS]

    @pl.loop(0, fields, step=2)
    def _(start):
        for i in (start, start + 1):
            total = advance(stacked(x.at[i]))
            for lev in range(LEVELS):
                zon[i, lev] = total[lev * ROWS : (lev + 1) * ROWS]


def fin_kernel(skip, count, direct, *refs):
    if direct:
        x, zon, near, far, w, t, zon_t, adv = refs
    else:
        x, zon, near, far, w, adv = refs
    chunks = w.shape[-1] // LANE

    def body(odd):
        for lev in range(LEVELS):
            for chunk in range(chunks):
                lane = lanes(chunk)
                weights = [w[r, lev, :, lane] for r in range(ROWS + 6)]

                def total_of(total, own_row, near_row, far_row):
                    for r in range(-3, ROWS + 3):
                        if 0 <= r < ROWS:
                            v = own_row(r)
                        else:
                            d = -r if r < 0 else r - ROWS + 1
                            v = near_row(d) if (r < 0) == odd else far_row(d)
                        total = total + weights[r + 3] * jnp.broadcast_to(v, total.shape)
                    return total

                def gathered(ref, f):
                    return lambda d: ref[(d - 1) * LEVELS + lev, f : f + 1, lane]

                def swapped(ref, f):
                    def row_at(d):
                        row = side_rows(odd)[d - 1]
                        return ref[f, lev, row : row + 1, lane]

                    return row_at

                def gathered_t(ref):
                    def row_at(d):
                        at = (d - 1) * LEVELS + lev
                        return ref[3 * LEVELS, at : at + 1, lane]

                    return row_at

                for f in range(count):
                    adv[f, lev, :, lane] = total_of(
                        zon[skip + f, lev, :, lane],
                        lambda r: x[skip + f, lev, r : r + 1, lane],
                        gathered(near, f) if direct else swapped(near, f),
                        gathered(far, f),
                    )
                if direct:
                    adv[count, lev, :, lane] = total_of(
                        zon_t[lev, :, lane],
                        lambda r: t[lev, r : r + 1, lane],
                        gathered_t(near),
                        gathered_t(far),
                    )

    both(parity(), body)


def pack_columns(upper, share, quotient, ground, out):
    levels = upper.shape[0]
    out[:levels] = upper[...].astype(jnp.float32)
    out[levels : 2 * levels] = share[...]
    out[2 * levels : 3 * levels] = quotient[...]
    out[3 * levels] = ground[...]


def mix_weights(levels, columns, weights):
    group = lax.axis_index("lev")
    for k in range(levels):
        upper = columns[k]
        share = columns[levels + k]
        for s in range(2 * LEVELS):
            level = (group if s < LEVELS else 1 - group) * LEVELS + s % LEVELS
            at = level.astype(jnp.float32)
            weights[k, s] = jnp.where(
                upper == at, 1.0 - share, jnp.where(upper + 1.0 == at, share, 0.0)
            )


def mixed(weights, values):
    total = weights[0] * values[0]
    for w, v in zip(weights[1:], values[1:]):
        total = total + w * v
    return total


def blend(own, peer, weights, out, fields, skip=0):
    group = lax.axis_index("lev")
    for chunk in range(own.shape[-1] // LANE):
        lane = lanes(chunk)
        ws = [
            [weights[group * LEVELS + lev, s, :, lane] for s in range(2 * LEVELS)]
            for lev in range(LEVELS)
        ]
        for f in fields:
            values = [adv[f, lev, :, lane] for adv in (own, peer) for lev in range(LEVELS)]
            for lev in range(LEVELS):
                out[skip + f, lev, :, lane] = mixed(ws[lev], values)


def remap_first_kernel(levels, own, peer, weights, columns, out, thick):
    count = out.shape[0]
    vapour = [adv[0, lev] for adv in (own, peer) for lev in range(LEVELS)]
    temp = [adv[count, lev] for adv in (own, peer) for lev in range(LEVELS)]
    for k in range(levels):
        ws = [weights[k, s] for s in range(2 * LEVELS)]
        water = mixed(ws, vapour)
        heat = mixed(ws, temp)
        thick[k] = heat * (1.0 + 0.608 * water) * columns[2 * levels + k]
        thick[levels + k] = heat
    deeper = columns[3 * levels]
    for k in range(levels - 1, -1, -1):
        layer = thick[k]
        thick[k] = deeper + 0.5 * layer
        deeper = deeper + layer
    blend(own, peer, weights, out, range(count))


def remap_last_kernel(levels, own, peer, weights, first, thick, out, out_t, out_phi, buffer, sems):
    group = lax.axis_index("lev")
    count = first.shape[0]
    copies = []

    def send(source, target):
        copy = pltpu.make_async_copy(source, target, sems.at[len(copies)])
        copy.start()
        copies.append(copy)

    half = count // 2
    for start in (0, half):
        send(first.at[pl.ds(start, half)], out.at[pl.ds(start, half)])
    mine = group * LEVELS
    send(thick.at[pl.ds(mine, LEVELS)], out_phi)
    send(thick.at[pl.ds(levels + mine, LEVELS)], out_t)
    step = 2
    for start in range(0, buffer.shape[0], step):
        blend(own, peer, weights, buffer, range(start, start + step))
        send(buffer.at[pl.ds(start, step)], out.at[pl.ds(count + start, step)])
    for copy in copies:
        copy.wait()


def call(kernel, outs, scratch=(), specs=None, cost=0, limit=12, aliases=None, out_specs=None):
    single = not isinstance(outs, list)
    shapes = tuple(jax.ShapeDtypeStruct(s, jnp.float32) for s in ([outs] if single else outs))
    extra = {} if specs is None else {"in_specs": specs}
    if out_specs is not None:
        extra["out_specs"] = out_specs
    return pl.pallas_call(
        kernel,
        out_shape=shapes[0] if single else shapes,
        scratch_shapes=[pltpu.VMEM(s, jnp.float32) if isinstance(s, tuple) else s for s in scratch],
        compiler_params=pltpu.CompilerParams(vmem_limit_bytes=limit * 2**20),
        cost_estimate=pl.CostEstimate(flops=cost * 10**6, bytes_accessed=1000, transcendentals=0),
        input_output_aliases=aliases or {},
        **extra,
    )


def on_device(
    constituent_densities,
    thermal_state,
    integer_boxes_traversed,
    partial_crossing_share,
    northward_crossing_share,
    higher_donor_stratum,
    deeper_donor_share,
    napierian_thickness_quotient,
    ground_gravity_height,
):
    x, t, c = constituent_densities, thermal_state, northward_crossing_share
    fields, _, _, lons = x.shape
    levels = higher_donor_stratum.shape[0]
    bands = lax.axis_size("lat")
    lat_total = bands * ROWS

    pairs = [(i, i ^ 1) for i in range(bands)]
    across = [(i, i + 1 if i % 2 else i - 1) for i in range(1, bands - 1)]
    relays = [(i, i + 2) for i in range(0, bands - 2, 2)] + [(i, i - 2) for i in range(3, bands, 2)]
    cores = [(0, 1), (1, 0)]

    def swap(v):
        return lax.ppermute(v, "lat", pairs)

    def exchange_across(v):
        return lax.ppermute(v, "lat", across)

    def pass_on(v):
        return lax.ppermute(v, "lat", relays)

    def other_core(v):
        return lax.ppermute(v, "lev", cores)

    face = np.arange(lat_total + 1)
    face_sine = np.sin(math.pi * np.minimum(face, lat_total - face) / lat_total)
    row_sine = np.sin(math.pi * (np.arange(lat_total) + 0.5) / lat_total)
    scale = np.stack([face_sine[:-1] / row_sine, face_sine[1:] / row_sine], 1)
    scale = jnp.asarray(scale.reshape(-1).astype(np.float32))

    smem, vmem = pl.BlockSpec(memory_space=pltpu.SMEM), pl.BlockSpec(memory_space=pltpu.VMEM)
    direct = fields // 2
    swapped = fields - direct
    direct_shape = (3 * LEVELS + 1, direct, lons)

    payload = call(
        copy_kernel,
        (swapped,) + x.shape[1:],
        [pltpu.SemaphoreType.DMA((swapped,))],
        [pl.BlockSpec(memory_space=pltpu.HBM)],
        limit=60,
    )(x)
    near_a = swap(payload)
    zon, zon_t, near_rows, far_rows, columns = call(
        functools.partial(zonal_kernel, fields),
        [
            x.shape,
            t.shape,
            direct_shape,
            direct_shape,
            (3 * levels + 1,) + ground_gravity_height.shape,
        ],
        [(7, LEVELS * ROWS, lons)],
        cost=COST["zonal"],
    )(
        x,
        t,
        integer_boxes_traversed,
        partial_crossing_share,
        c,
        higher_donor_stratum,
        deeper_donor_share,
        napierian_thickness_quotient,
        ground_gravity_height,
    )
    far_b = exchange_across(far_rows)
    near_b = swap(near_rows)

    relay = call(relay_kernel, (3 * LEVELS, swapped, lons), cost=COST["relay"])(near_a, zon_t)
    far_a = pass_on(relay)

    peer_columns = other_core(columns)
    columns = jnp.where(
        lax.axis_index("lev") == 0,
        jnp.concatenate([columns, peer_columns], -1),
        jnp.concatenate([peer_columns, columns], -1),
    )

    mix, weights, zon, zon_t, factor = call(
        functools.partial(early_kernel, fields, levels, bands - 1),
        [
            (levels, 2 * LEVELS, ROWS, lons),
            (ROWS + 6, LEVELS, ROWS, lons),
            x.shape,
            t.shape,
            (LEVELS, lons),
        ],
        [(3, LEVELS * ROWS, lons)],
        [smem] + [vmem] * 6,
        cost=COST["early"],
        aliases={5: 2, 6: 3},
    )(scale, columns, c, x, t, zon, zon_t)
    weights = call(
        patch_kernel,
        weights.shape,
        cost=COST["patch"],
        aliases={3: 0},
    )(factor, near_b, far_b, weights)

    adv_b = call(
        functools.partial(fin_kernel, 0, direct, True),
        (direct + 1,) + x.shape[1:],
        cost=COST["fin_b"],
    )(x, zon, near_b, far_b, weights, t, zon_t)
    peer_b = other_core(adv_b)
    adv_a = call(
        functools.partial(fin_kernel, direct, swapped, False),
        (swapped,) + x.shape[1:],
        cost=COST["fin_a"],
    )(x, zon, near_a, far_a, weights)
    peer_a = other_core(adv_a)

    anywhere = pl.BlockSpec(memory_space=pl.ANY)
    first, thick = call(
        functools.partial(remap_first_kernel, levels),
        [(direct,) + x.shape[1:], (2 * levels, ROWS, lons)],
        cost=COST["first"],
    )(adv_b, peer_b, mix, columns)
    return call(
        functools.partial(remap_last_kernel, levels),
        [x.shape, t.shape, t.shape],
        [(swapped,) + x.shape[1:], pltpu.SemaphoreType.DMA((4 + swapped // 2,))],
        cost=COST["last"],
        out_specs=(anywhere,) * 3,
    )(adv_a, peer_a, mix, first, thick)


def solution(mesh):
    return jax.shard_map(
        on_device,
        mesh=mesh,
        in_specs=(
            P("ens", "lev", "lat", None),
            P(("ens", "lev"), "lat", None),
            P(("ens", "lev"), "lat", None),
            P(("ens", "lev"), "lat", None),
            P(("ens", "lev"), "lat", None),
            P("ens", "lat", "lev"),
            P("ens", "lat", "lev"),
            P("ens", "lat", "lev"),
            P(("ens", "lat"), "lev"),
        ),
        out_specs=(
            P("ens", "lev", "lat", None),
            P(("ens", "lev"), "lat", None),
            P(("ens", "lev"), "lat", None),
        ),
        check_vma=False,
    )
```

```python
import functools
import math

import jax
import jax.numpy as jnp
import numpy as np
from jax import lax
from jax.experimental import pallas as pl
from jax.experimental.pallas import tpu as pltpu
from jax.sharding import PartitionSpec as P

ROWS = 4
LEVELS = 2
LANE = 128

COST = dict(zonal=10000, relay=10000, early=1, patch=1, fin_b=1, fin_a=1, first=1, last=1)


def lanes(chunk):
    return pl.ds(chunk * LANE, LANE)


def parity():
    return lax.rem(lax.axis_index("lat"), 2)


def both(odd, body):
    @pl.when(odd == 1)
    def _():
        body(True)

    @pl.when(odd == 0)
    def _():
        body(False)


def copy_kernel(x, out):
    skip = x.shape[0] - out.shape[0]
    out[...] = x[skip:]


def side_rows(to_north):
    return (ROWS - 1, ROWS - 2, ROWS - 3) if to_north else (0, 1, 2)


def gather_rows(rows, x, t, c, out):
    count = out.shape[1]
    last = 3 * LEVELS
    for d, row in enumerate(rows):
        for lev in range(LEVELS):
            at = d * LEVELS + lev
            for f in range(count):
                out[at, f : f + 1, :] = x[f, lev, row : row + 1, :]
            out[last, at : at + 1, :] = t[lev, row : row + 1, :]
    for lev in range(LEVELS):
        out[last, last + lev : last + lev + 1, :] = c[lev, ROWS - 1 : ROWS, :]


def relay_kernel(swapped, zon_t, relay):
    def body(odd):
        for d, row in enumerate(side_rows(not odd)):
            for lev in range(LEVELS):
                for f in range(swapped.shape[0]):
                    relay[d * LEVELS + lev, f : f + 1, :] = swapped[f, lev, row : row + 1, :]

    both(parity(), body)


def parabola_weights(share):
    half = 0.5 * share
    curve = half * (1.0 - share * (2.0 / 3.0))
    right = (1.0 - half - 3.0 * curve) * (1.0 / 12.0)
    left = (half - 3.0 * curve) * (1.0 / 12.0)
    return (
        -share * left,
        share * (7.0 * left - right),
        share * (7.0 * (left + right) + 6.0 * curve),
        share * (7.0 * right - left),
        -share * right,
    )


def face_weights(courant):
    t = parabola_weights(jnp.abs(courant))
    north = courant >= 0.0
    zero = jnp.zeros_like(courant)
    return (
        jnp.where(north, t[0], zero),
        jnp.where(north, t[1], -t[4]),
        jnp.where(north, t[2], -t[3]),
        jnp.where(north, t[3], -t[2]),
        jnp.where(north, t[4], -t[1]),
        jnp.where(north, zero, -t[0]),
    )


def row_weights(c, below, scale, lat):
    row = lax.broadcasted_iota(jnp.int32, c.shape, 0) % ROWS

    def by_row(parts):
        total = parts[ROWS - 1]
        for j in range(ROWS - 2, -1, -1):
            total = jnp.where(row == j, parts[j], total)
        return total

    low = by_row([jnp.full(c.shape, scale[lat * 2 * ROWS + 2 * j]) for j in range(ROWS)])
    high = by_row([jnp.full(c.shape, scale[lat * 2 * ROWS + 2 * j + 1]) for j in range(ROWS)])
    lower = face_weights(below)
    upper = face_weights(c)
    offsets = {}
    for o in range(-3, 4):
        total = jnp.zeros_like(c)
        if o <= 2:
            total = total + low * lower[o + 3]
        if o >= -2:
            total = total - high * upper[o + 2]
        offsets[o] = total
    zero = jnp.zeros_like(c)
    return [by_row([offsets.get(r - j, zero) for j in range(ROWS)]) for r in range(-3, ROWS + 3)]


def stacked(ref):
    return jnp.concatenate([ref[lev] for lev in range(LEVELS)], axis=0)


def early_kernel(
    fields, levels, last, scale, columns, c, x, t, zon_in, zon_t_in, mix, out, zon, zon_t, factor, ws
):
    lat = lax.axis_index("lat")
    lons = x.shape[-1]
    mix_weights(levels, columns, mix)
    factor[...] = jnp.full(factor.shape, jnp.where(lat == 0, 0.0, scale[lat * 2 * ROWS]))
    parts = []
    for lev in range(LEVELS):
        own = c[lev]
        parts += [
            jnp.where(lat == 0, -pltpu.roll(own, lons // 2, 1)[0:1], 0.0),
            own[: ROWS - 1],
        ]
    for r, w in enumerate(row_weights(stacked(c), jnp.concatenate(parts, axis=0), scale, lat)):
        for lev in range(LEVELS):
            out[r, lev] = w[lev * ROWS : (lev + 1) * ROWS]

    def pole(rows):
        for k, (_, at) in enumerate(rows):
            ws[k] = stacked(out.at[at])
            for lev in range(LEVELS):
                out[at, lev] = jnp.zeros_like(out[at, lev])

        def beyond(ref):
            v = pltpu.roll(stacked(ref), lons // 2, 1)
            total = jnp.zeros_like(v)
            for k, (source, _) in enumerate(rows):
                both_rows = [
                    jnp.broadcast_to(v[r : r + 1], (ROWS, lons))
                    for r in range(source, LEVELS * ROWS, ROWS)
                ]
                total = total + ws[k] * jnp.concatenate(both_rows, axis=0)
            return [total[lev * ROWS : (lev + 1) * ROWS] for lev in range(LEVELS)]

        for lev, part in enumerate(beyond(t)):
            zon_t[lev] = zon_t[lev] + part

        @pl.loop(0, fields, step=2)
        def _(start):
            for i in (start, start + 1):
                for lev, part in enumerate(beyond(x.at[i])):
                    zon[i, lev] = zon[i, lev] + part

    @pl.when(lat == 0)
    def _():
        pole([(d - 1, 3 - d) for d in range(1, 4)])

    @pl.when(lat == last)
    def _():
        pole([(ROWS - d, ROWS + 2 + d) for d in range(1, 4)])


def patch_kernel(factor, near, far, weights_in, weights):
    block = 3 * LEVELS
    rows = slice(block, block + LEVELS)
    below = jnp.where(parity() == 1, near[block, rows, :], far[block, rows, :])
    for r, part in enumerate(face_weights(below)):
        part = factor[...] * part
        for lev in range(LEVELS):
            weights[r, lev, 0:1, :] = weights[r, lev, 0:1, :] + part[lev : lev + 1]


def zonal_kernel(
    fields, x, t, n, f, c, upper, share, quotient, ground, zon, zon_t, near, far, columns, w
):
    lons = x.shape[-1]
    pack_columns(upper, share, quotient, ground, columns)

    def gather(odd):
        gather_rows(side_rows(not odd), x, t, c, near)
        gather_rows(side_rows(odd), x, t, c, far)

    both(parity(), gather)

    def shifted(values, k):
        return values if k == 0 else pltpu.roll(values, (-k) % lons, 1)

    def advance(v):
        flux = w[1] * v
        for k in (0, 2, 3, 4, 5, 6):
            flux = flux + w[k] * shifted(v, 1 - k)
        return v - (shifted(flux, 1) - flux)

    whole = stacked(n)
    s = parabola_weights(stacked(f))
    zero = jnp.zeros_like(s[0])
    n0, n1 = whole == 0, whole == 1

    def pick(a, b, d):
        return jnp.where(n0, a, jnp.where(n1, b, d))

    w[0] = pick(s[4], zero, zero)
    w[1] = pick(s[3], s[4], zero)
    w[2] = pick(s[2], s[3] + 1.0, s[4] + 1.0)
    w[3] = pick(s[1], s[2], s[3] + 1.0)
    w[4] = pick(s[0], s[1], s[2])
    w[5] = pick(zero, s[0], s[1])
    w[6] = pick(zero, zero, s[0])

    total = advance(stacked(t))
    for lev in range(LEVELS):
        zon_t[lev] = total[lev * ROWS : (lev + 1) * ROWS]

    @pl.loop(0, fields, step=2)
    def _(start):
        for i in (start, start + 1):
            total = advance(stacked(x.at[i]))
            for lev in range(LEVELS):
                zon[i, lev] = total[lev * ROWS : (lev + 1) * ROWS]


def fin_kernel(skip, count, direct, *refs):
    if direct:
        x, zon, near, far, w, t, zon_t, adv = refs
    else:
        x, zon, near, far, w, adv = refs
    chunks = w.shape[-1] // LANE

    def body(odd):
        for lev in range(LEVELS):
            for chunk in range(chunks):
                lane = lanes(chunk)
                weights = [w[r, lev, :, lane] for r in range(ROWS + 6)]

                def total_of(total, own_row, near_row, far_row):
                    for r in range(-3, ROWS + 3):
                        if 0 <= r < ROWS:
                            v = own_row(r)
                        else:
                            d = -r if r < 0 else r - ROWS + 1
                            v = near_row(d) if (r < 0) == odd else far_row(d)
                        total = total + weights[r + 3] * jnp.broadcast_to(v, total.shape)
                    return total

                def gathered(ref, f):
                    return lambda d: ref[(d - 1) * LEVELS + lev, f : f + 1, lane]

                def swapped(ref, f):
                    def row_at(d):
                        row = side_rows(odd)[d - 1]
                        return ref[f, lev, row : row + 1, lane]

                    return row_at

                def gathered_t(ref):
                    def row_at(d):
                        at = (d - 1) * LEVELS + lev
                        return ref[3 * LEVELS, at : at + 1, lane]

                    return row_at

                for f in range(count):
                    adv[f, lev, :, lane] = total_of(
                        zon[skip + f, lev, :, lane],
                        lambda r: x[skip + f, lev, r : r + 1, lane],
                        gathered(near, f) if direct else swapped(near, f),
                        gathered(far, f),
                    )
                if direct:
                    adv[count, lev, :, lane] = total_of(
                        zon_t[lev, :, lane],
                        lambda r: t[lev, r : r + 1, lane],
                        gathered_t(near),
                        gathered_t(far),
                    )

    both(parity(), body)


def pack_columns(upper, share, quotient, ground, out):
    levels = upper.shape[0]
    out[:levels] = upper[...].astype(jnp.float32)
    out[levels : 2 * levels] = share[...]
    out[2 * levels : 3 * levels] = quotient[...]
    out[3 * levels] = ground[...]


def mix_weights(levels, columns, weights):
    group = lax.axis_index("lev")
    for k in range(levels):
        upper = columns[k]
        share = columns[levels + k]
        for s in range(2 * LEVELS):
            level = (group if s < LEVELS else 1 - group) * LEVELS + s % LEVELS
            at = level.astype(jnp.float32)
            weights[k, s] = jnp.where(
                upper == at, 1.0 - share, jnp.where(upper + 1.0 == at, share, 0.0)
            )


def mixed(weights, values):
    total = weights[0] * values[0]
    for w, v in zip(weights[1:], values[1:]):
        total = total + w * v
    return total


def blend(own, peer, weights, out, fields, skip=0):
    group = lax.axis_index("lev")
    for chunk in range(own.shape[-1] // LANE):
        lane = lanes(chunk)
        ws = [
            [weights[group * LEVELS + lev, s, :, lane] for s in range(2 * LEVELS)]
            for lev in range(LEVELS)
        ]
        for f in fields:
            values = [adv[f, lev, :, lane] for adv in (own, peer) for lev in range(LEVELS)]
            for lev in range(LEVELS):
                out[skip + f, lev, :, lane] = mixed(ws[lev], values)


def remap_first_kernel(levels, own, peer, weights, columns, out, thick):
    count = out.shape[0]
    vapour = [adv[0, lev] for adv in (own, peer) for lev in range(LEVELS)]
    temp = [adv[count, lev] for adv in (own, peer) for lev in range(LEVELS)]
    for k in range(levels):
        ws = [weights[k, s] for s in range(2 * LEVELS)]
        water = mixed(ws, vapour)
        heat = mixed(ws, temp)
        thick[k] = heat * (1.0 + 0.608 * water) * columns[2 * levels + k]
        thick[levels + k] = heat
    deeper = columns[3 * levels]
    for k in range(levels - 1, -1, -1):
        layer = thick[k]
        thick[k] = deeper + 0.5 * layer
        deeper = deeper + layer
    blend(own, peer, weights, out, range(count))


def remap_last_kernel(levels, own, peer, weights, first, thick, out, out_t, out_phi, buffer, sems):
    group = lax.axis_index("lev")
    count = first.shape[0]
    copies = []

    def send(source, target):
        copy = pltpu.make_async_copy(source, target, sems.at[len(copies)])
        copy.start()
        copies.append(copy)

    half = count // 2
    for start in (0, half):
        send(first.at[pl.ds(start, half)], out.at[pl.ds(start, half)])
    mine = group * LEVELS
    send(thick.at[pl.ds(mine, LEVELS)], out_phi)
    send(thick.at[pl.ds(levels + mine, LEVELS)], out_t)
    step = 2
    for start in range(0, buffer.shape[0], step):
        blend(own, peer, weights, buffer, range(start, start + step))
        send(buffer.at[pl.ds(start, step)], out.at[pl.ds(count + start, step)])
    for copy in copies:
        copy.wait()


def call(kernel, outs, scratch=(), specs=None, cost=0, limit=12, aliases=None, out_specs=None):
    single = not isinstance(outs, list)
    shapes = tuple(jax.ShapeDtypeStruct(s, jnp.float32) for s in ([outs] if single else outs))
    extra = {} if specs is None else {"in_specs": specs}
    if out_specs is not None:
        extra["out_specs"] = out_specs
    return pl.pallas_call(
        kernel,
        out_shape=shapes[0] if single else shapes,
        scratch_shapes=[pltpu.VMEM(s, jnp.float32) if isinstance(s, tuple) else s for s in scratch],
        compiler_params=pltpu.CompilerParams(vmem_limit_bytes=limit * 2**20),
        cost_estimate=pl.CostEstimate(flops=cost * 10**6, bytes_accessed=1000, transcendentals=0),
        input_output_aliases=aliases or {},
        **extra,
    )


def on_device(
    constituent_densities,
    thermal_state,
    integer_boxes_traversed,
    partial_crossing_share,
    northward_crossing_share,
    higher_donor_stratum,
    deeper_donor_share,
    napierian_thickness_quotient,
    ground_gravity_height,
):
    x, t, c = constituent_densities, thermal_state, northward_crossing_share
    fields, _, _, lons = x.shape
    levels = higher_donor_stratum.shape[0]
    bands = lax.axis_size("lat")
    lat_total = bands * ROWS

    pairs = [(i, i ^ 1) for i in range(bands)]
    across = [(i, i + 1 if i % 2 else i - 1) for i in range(1, bands - 1)]
    relays = [(i, i + 2) for i in range(0, bands - 2, 2)] + [(i, i - 2) for i in range(3, bands, 2)]
    cores = [(0, 1), (1, 0)]

    def swap(v):
        return lax.ppermute(v, "lat", pairs)

    def exchange_across(v):
        return lax.ppermute(v, "lat", across)

    def pass_on(v):
        return lax.ppermute(v, "lat", relays)

    def other_core(v):
        return lax.ppermute(v, "lev", cores)

    face = np.arange(lat_total + 1)
    face_sine = np.sin(math.pi * np.minimum(face, lat_total - face) / lat_total)
    row_sine = np.sin(math.pi * (np.arange(lat_total) + 0.5) / lat_total)
    scale = np.stack([face_sine[:-1] / row_sine, face_sine[1:] / row_sine], 1)
    scale = jnp.asarray(scale.reshape(-1).astype(np.float32))

    smem, vmem = pl.BlockSpec(memory_space=pltpu.SMEM), pl.BlockSpec(memory_space=pltpu.VMEM)
    direct = fields // 2
    swapped = fields - direct
    direct_shape = (3 * LEVELS + 1, direct, lons)

    payload = call(copy_kernel, (swapped,) + x.shape[1:])(x)
    near_a = swap(payload)
    zon, zon_t, near_rows, far_rows, columns = call(
        functools.partial(zonal_kernel, fields),
        [
            x.shape,
            t.shape,
            direct_shape,
            direct_shape,
            (3 * levels + 1,) + ground_gravity_height.shape,
        ],
        [(7, LEVELS * ROWS, lons)],
        cost=COST["zonal"],
    )(
        x,
        t,
        integer_boxes_traversed,
        partial_crossing_share,
        c,
        higher_donor_stratum,
        deeper_donor_share,
        napierian_thickness_quotient,
        ground_gravity_height,
    )
    far_b = exchange_across(far_rows)
    near_b = swap(near_rows)

    relay = call(relay_kernel, (3 * LEVELS, swapped, lons), cost=COST["relay"])(near_a, zon_t)
    far_a = pass_on(relay)

    peer_columns = other_core(columns)
    columns = jnp.where(
        lax.axis_index("lev") == 0,
        jnp.concatenate([columns, peer_columns], -1),
        jnp.concatenate([peer_columns, columns], -1),
    )

    mix, weights, zon, zon_t, factor = call(
        functools.partial(early_kernel, fields, levels, bands - 1),
        [
            (levels, 2 * LEVELS, ROWS, lons),
            (ROWS + 6, LEVELS, ROWS, lons),
            x.shape,
            t.shape,
            (LEVELS, lons),
        ],
        [(3, LEVELS * ROWS, lons)],
        [smem] + [vmem] * 6,
        cost=COST["early"],
        aliases={5: 2, 6: 3},
    )(scale, columns, c, x, t, zon, zon_t)
    weights = call(
        patch_kernel,
        weights.shape,
        cost=COST["patch"],
        aliases={3: 0},
    )(factor, near_b, far_b, weights)

    adv_b = call(
        functools.partial(fin_kernel, 0, direct, True),
        (direct + 1,) + x.shape[1:],
        cost=COST["fin_b"],
    )(x, zon, near_b, far_b, weights, t, zon_t)
    peer_b = other_core(adv_b)
    adv_a = call(
        functools.partial(fin_kernel, direct, swapped, False),
        (swapped,) + x.shape[1:],
        cost=COST["fin_a"],
    )(x, zon, near_a, far_a, weights)
    peer_a = other_core(adv_a)

    anywhere = pl.BlockSpec(memory_space=pl.ANY)
    first, thick = call(
        functools.partial(remap_first_kernel, levels),
        [(direct,) + x.shape[1:], (2 * levels, ROWS, lons)],
        cost=COST["first"],
    )(adv_b, peer_b, mix, columns)
    return call(
        functools.partial(remap_last_kernel, levels),
        [x.shape, t.shape, t.shape],
        [(swapped,) + x.shape[1:], pltpu.SemaphoreType.DMA((4 + swapped // 2,))],
        cost=COST["last"],
        out_specs=(anywhere,) * 3,
    )(adv_a, peer_a, mix, first, thick)


def solution(mesh):
    return jax.shard_map(
        on_device,
        mesh=mesh,
        in_specs=(
            P("ens", "lev", "lat", None),
            P(("ens", "lev"), "lat", None),
            P(("ens", "lev"), "lat", None),
            P(("ens", "lev"), "lat", None),
            P(("ens", "lev"), "lat", None),
            P("ens", "lat", "lev"),
            P("ens", "lat", "lev"),
            P("ens", "lat", "lev"),
            P(("ens", "lat"), "lev"),
        ),
        out_specs=(
            P("ens", "lev", "lat", None),
            P(("ens", "lev"), "lat", None),
            P(("ens", "lev"), "lat", None),
        ),
        check_vma=False,
    )
```

```python
import functools
import math

import jax
import jax.numpy as jnp
import numpy as np
from jax import lax
from jax.experimental import pallas as pl
from jax.experimental.pallas import tpu as pltpu
from jax.sharding import PartitionSpec as P

ROWS = 4
LEVELS = 2
LANE = 128

COST = dict(zonal=10000, relay=10000, mix=1, early=1, fin_b=1, fin_a=1, first=1, last=1)


def lanes(chunk):
    return pl.ds(chunk * LANE, LANE)


def parity():
    return lax.rem(lax.axis_index("lat"), 2)


def both(odd, body):
    @pl.when(odd == 1)
    def _():
        body(True)

    @pl.when(odd == 0)
    def _():
        body(False)


def copy_kernel(x, out):
    skip = x.shape[0] - out.shape[0]
    out[...] = x[skip:]


def side_rows(to_north):
    return (ROWS - 1, ROWS - 2, ROWS - 3) if to_north else (0, 1, 2)


def gather_rows(rows, x, t, out):
    count = out.shape[1]
    last = 3 * LEVELS
    for d, row in enumerate(rows):
        for lev in range(LEVELS):
            at = d * LEVELS + lev
            for f in range(count):
                out[at, f : f + 1, :] = x[f, lev, row : row + 1, :]
            out[last, at : at + 1, :] = t[lev, row : row + 1, :]


def relay_kernel(swapped, zon_t, relay):
    def body(odd):
        for d, row in enumerate(side_rows(not odd)):
            for lev in range(LEVELS):
                for f in range(swapped.shape[0]):
                    relay[d * LEVELS + lev, f : f + 1, :] = swapped[f, lev, row : row + 1, :]

    both(parity(), body)


def parabola_weights(share):
    half = 0.5 * share
    curve = half * (1.0 - share * (2.0 / 3.0))
    right = (1.0 - half - 3.0 * curve) * (1.0 / 12.0)
    left = (half - 3.0 * curve) * (1.0 / 12.0)
    return (
        -share * left,
        share * (7.0 * left - right),
        share * (7.0 * (left + right) + 6.0 * curve),
        share * (7.0 * right - left),
        -share * right,
    )


def face_weights(courant):
    t = parabola_weights(jnp.abs(courant))
    north = courant >= 0.0
    zero = jnp.zeros_like(courant)
    return (
        jnp.where(north, t[0], zero),
        jnp.where(north, t[1], -t[4]),
        jnp.where(north, t[2], -t[3]),
        jnp.where(north, t[3], -t[2]),
        jnp.where(north, t[4], -t[1]),
        jnp.where(north, zero, -t[0]),
    )


def row_weights(c, below, scale, lat):
    row = lax.broadcasted_iota(jnp.int32, c.shape, 0) % ROWS

    def by_row(parts):
        total = parts[ROWS - 1]
        for j in range(ROWS - 2, -1, -1):
            total = jnp.where(row == j, parts[j], total)
        return total

    low = by_row([jnp.full(c.shape, scale[lat * 2 * ROWS + 2 * j]) for j in range(ROWS)])
    high = by_row([jnp.full(c.shape, scale[lat * 2 * ROWS + 2 * j + 1]) for j in range(ROWS)])
    lower = face_weights(below)
    upper = face_weights(c)
    offsets = {}
    for o in range(-3, 4):
        total = jnp.zeros_like(c)
        if o <= 2:
            total = total + low * lower[o + 3]
        if o >= -2:
            total = total - high * upper[o + 2]
        offsets[o] = total
    zero = jnp.zeros_like(c)
    return [by_row([offsets.get(r - j, zero) for j in range(ROWS)]) for r in range(-3, ROWS + 3)]


def stacked(ref):
    return jnp.concatenate([ref[lev] for lev in range(LEVELS)], axis=0)


def mix_kernel(levels, columns, c, relay, mix, c_rows):
    mix_weights(levels, columns, mix)
    for lev in range(LEVELS):
        c_rows[lev : lev + 1, :] = c[lev, ROWS - 1 : ROWS, :]


def early_kernel(fields, last, scale, c, c_south, x, t, zon_in, zon_t_in, out, zon, zon_t, ws):
    lat = lax.axis_index("lat")
    lons = x.shape[-1]
    parts = []
    for lev in range(LEVELS):
        own = c[lev]
        beyond_pole = -pltpu.roll(own, lons // 2, 1)[0:1]
        parts += [
            jnp.where(lat == 0, beyond_pole, c_south[lev : lev + 1, :]),
            own[: ROWS - 1],
        ]
    for r, w in enumerate(row_weights(stacked(c), jnp.concatenate(parts, axis=0), scale, lat)):
        for lev in range(LEVELS):
            out[r, lev] = w[lev * ROWS : (lev + 1) * ROWS]

    for lev in range(LEVELS):
        for chunk in range(lons // LANE):
            lane = lanes(chunk)
            weights = [out[r + 3, lev, :, lane] for r in range(ROWS)]

            def with_own_rows(total, row_at):
                for r, w in enumerate(weights):
                    total = total + w * jnp.broadcast_to(row_at(r), total.shape)
                return total

            zon_t[lev, :, lane] = with_own_rows(
                zon_t_in[lev, :, lane], lambda r: t[lev, r : r + 1, lane]
            )
            for i in range(fields):
                zon[i, lev, :, lane] = with_own_rows(
                    zon_in[i, lev, :, lane], lambda r: x[i, lev, r : r + 1, lane]
                )

    def pole(rows):
        for k, (_, at) in enumerate(rows):
            ws[k] = stacked(out.at[at])
            for lev in range(LEVELS):
                out[at, lev] = jnp.zeros_like(out[at, lev])

        def beyond(ref):
            v = pltpu.roll(stacked(ref), lons // 2, 1)
            total = jnp.zeros_like(v)
            for k, (source, _) in enumerate(rows):
                both_rows = [
                    jnp.broadcast_to(v[r : r + 1], (ROWS, lons))
                    for r in range(source, LEVELS * ROWS, ROWS)
                ]
                total = total + ws[k] * jnp.concatenate(both_rows, axis=0)
            return [total[lev * ROWS : (lev + 1) * ROWS] for lev in range(LEVELS)]

        for lev, part in enumerate(beyond(t)):
            zon_t[lev] = zon_t[lev] + part

        @pl.loop(0, fields, step=2)
        def _(start):
            for i in (start, start + 1):
                for lev, part in enumerate(beyond(x.at[i])):
                    zon[i, lev] = zon[i, lev] + part

    @pl.when(lat == 0)
    def _():
        pole([(d - 1, 3 - d) for d in range(1, 4)])

    @pl.when(lat == last)
    def _():
        pole([(ROWS - d, ROWS + 2 + d) for d in range(1, 4)])


def zonal_kernel(
    fields, x, t, n, f, upper, share, quotient, ground, zon, zon_t, near, far, columns, w
):
    lons = x.shape[-1]
    pack_columns(upper, share, quotient, ground, columns)

    def gather(odd):
        gather_rows(side_rows(not odd), x, t, near)
        gather_rows(side_rows(odd), x, t, far)

    both(parity(), gather)

    def shifted(values, k):
        return values if k == 0 else pltpu.roll(values, (-k) % lons, 1)

    def advance(v):
        flux = w[1] * v
        for k in (0, 2, 3, 4, 5, 6):
            flux = flux + w[k] * shifted(v, 1 - k)
        return v - (shifted(flux, 1) - flux)

    whole = stacked(n)
    s = parabola_weights(stacked(f))
    zero = jnp.zeros_like(s[0])
    n0, n1 = whole == 0, whole == 1

    def pick(a, b, d):
        return jnp.where(n0, a, jnp.where(n1, b, d))

    w[0] = pick(s[4], zero, zero)
    w[1] = pick(s[3], s[4], zero)
    w[2] = pick(s[2], s[3] + 1.0, s[4] + 1.0)
    w[3] = pick(s[1], s[2], s[3] + 1.0)
    w[4] = pick(s[0], s[1], s[2])
    w[5] = pick(zero, s[0], s[1])
    w[6] = pick(zero, zero, s[0])

    total = advance(stacked(t))
    for lev in range(LEVELS):
        zon_t[lev] = total[lev * ROWS : (lev + 1) * ROWS]

    @pl.loop(0, fields, step=2)
    def _(start):
        for i in (start, start + 1):
            total = advance(stacked(x.at[i]))
            for lev in range(LEVELS):
                zon[i, lev] = total[lev * ROWS : (lev + 1) * ROWS]


def fin_kernel(skip, count, direct, *refs):
    if direct:
        base, near, far, w, base_t, adv = refs
    else:
        base, near, far, w, adv = refs
    chunks = w.shape[-1] // LANE

    def body(odd):
        for lev in range(LEVELS):
            for chunk in range(chunks):
                lane = lanes(chunk)
                sides = [
                    (w[3 - d, lev, :, lane], w[ROWS + 2 + d, lev, :, lane]) for d in range(1, 4)
                ]

                def total_of(total, near_row, far_row):
                    for d, (south, north) in enumerate(sides, 1):
                        for weight, is_near in ((south, odd), (north, not odd)):
                            v = near_row(d) if is_near else far_row(d)
                            total = total + weight * jnp.broadcast_to(v, total.shape)
                    return total

                def gathered(ref, f):
                    return lambda d: ref[(d - 1) * LEVELS + lev, f : f + 1, lane]

                def swapped(ref, f):
                    def row_at(d):
                        row = side_rows(odd)[d - 1]
                        return ref[f, lev, row : row + 1, lane]

                    return row_at

                def gathered_t(ref):
                    def row_at(d):
                        at = (d - 1) * LEVELS + lev
                        return ref[3 * LEVELS, at : at + 1, lane]

                    return row_at

                for f in range(count):
                    adv[f, lev, :, lane] = total_of(
                        base[skip + f, lev, :, lane],
                        gathered(near, f) if direct else swapped(near, f),
                        gathered(far, f),
                    )
                if direct:
                    adv[count, lev, :, lane] = total_of(
                        base_t[lev, :, lane],
                        gathered_t(near),
                        gathered_t(far),
                    )

    both(parity(), body)


def pack_columns(upper, share, quotient, ground, out):
    levels = upper.shape[0]
    out[:levels] = upper[...].astype(jnp.float32)
    out[levels : 2 * levels] = share[...]
    out[2 * levels : 3 * levels] = quotient[...]
    out[3 * levels] = ground[...]


def mix_weights(levels, columns, weights):
    group = lax.axis_index("lev")
    for k in range(levels):
        upper = columns[k]
        share = columns[levels + k]
        for s in range(2 * LEVELS):
            level = (group if s < LEVELS else 1 - group) * LEVELS + s % LEVELS
            at = level.astype(jnp.float32)
            weights[k, s] = jnp.where(
                upper == at, 1.0 - share, jnp.where(upper + 1.0 == at, share, 0.0)
            )


def mixed(weights, values):
    total = weights[0] * values[0]
    for w, v in zip(weights[1:], values[1:]):
        total = total + w * v
    return total


def blend(own, peer, weights, out, fields, skip=0):
    group = lax.axis_index("lev")
    for chunk in range(own.shape[-1] // LANE):
        lane = lanes(chunk)
        ws = [
            [weights[group * LEVELS + lev, s, :, lane] for s in range(2 * LEVELS)]
            for lev in range(LEVELS)
        ]
        for f in fields:
            values = [adv[f, lev, :, lane] for adv in (own, peer) for lev in range(LEVELS)]
            for lev in range(LEVELS):
                out[skip + f, lev, :, lane] = mixed(ws[lev], values)


def remap_first_kernel(levels, own, peer, weights, columns, out, thick):
    count = out.shape[0]
    vapour = [adv[0, lev] for adv in (own, peer) for lev in range(LEVELS)]
    temp = [adv[count, lev] for adv in (own, peer) for lev in range(LEVELS)]
    for k in range(levels):
        ws = [weights[k, s] for s in range(2 * LEVELS)]
        water = mixed(ws, vapour)
        heat = mixed(ws, temp)
        thick[k] = heat * (1.0 + 0.608 * water) * columns[2 * levels + k]
        thick[levels + k] = heat
    deeper = columns[3 * levels]
    for k in range(levels - 1, -1, -1):
        layer = thick[k]
        thick[k] = deeper + 0.5 * layer
        deeper = deeper + layer
    blend(own, peer, weights, out, range(count))


def remap_last_kernel(levels, own, peer, weights, first, thick, out, out_t, out_phi, buffer, sems):
    group = lax.axis_index("lev")
    count = first.shape[0]
    copies = []

    def send(source, target):
        copy = pltpu.make_async_copy(source, target, sems.at[len(copies)])
        copy.start()
        copies.append(copy)

    half = count // 2
    for start in (0, half):
        send(first.at[pl.ds(start, half)], out.at[pl.ds(start, half)])
    mine = group * LEVELS
    send(thick.at[pl.ds(mine, LEVELS)], out_phi)
    send(thick.at[pl.ds(levels + mine, LEVELS)], out_t)
    step = 2
    for start in range(0, buffer.shape[0], step):
        blend(own, peer, weights, buffer, range(start, start + step))
        send(buffer.at[pl.ds(start, step)], out.at[pl.ds(count + start, step)])
    for copy in copies:
        copy.wait()


def call(kernel, outs, scratch=(), specs=None, cost=0, limit=12, aliases=None, out_specs=None):
    single = not isinstance(outs, list)
    shapes = tuple(jax.ShapeDtypeStruct(s, jnp.float32) for s in ([outs] if single else outs))
    extra = {} if specs is None else {"in_specs": specs}
    if out_specs is not None:
        extra["out_specs"] = out_specs
    return pl.pallas_call(
        kernel,
        out_shape=shapes[0] if single else shapes,
        scratch_shapes=[pltpu.VMEM(s, jnp.float32) if isinstance(s, tuple) else s for s in scratch],
        compiler_params=pltpu.CompilerParams(vmem_limit_bytes=limit * 2**20),
        cost_estimate=pl.CostEstimate(flops=cost * 10**6, bytes_accessed=1000, transcendentals=0),
        input_output_aliases=aliases or {},
        **extra,
    )


def on_device(
    constituent_densities,
    thermal_state,
    integer_boxes_traversed,
    partial_crossing_share,
    northward_crossing_share,
    higher_donor_stratum,
    deeper_donor_share,
    napierian_thickness_quotient,
    ground_gravity_height,
):
    x, t, c = constituent_densities, thermal_state, northward_crossing_share
    fields, _, _, lons = x.shape
    levels = higher_donor_stratum.shape[0]
    bands = lax.axis_size("lat")
    lat_total = bands * ROWS

    pairs = [(i, i ^ 1) for i in range(bands)]
    across = [(i, i + 1 if i % 2 else i - 1) for i in range(1, bands - 1)]
    relays = [(i, i + 2) for i in range(0, bands - 2, 2)] + [(i, i - 2) for i in range(3, bands, 2)]
    cores = [(0, 1), (1, 0)]

    def swap(v):
        return lax.ppermute(v, "lat", pairs)

    def exchange_across(v):
        return lax.ppermute(v, "lat", across)

    def pass_on(v):
        return lax.ppermute(v, "lat", relays)

    def other_core(v):
        return lax.ppermute(v, "lev", cores)

    face = np.arange(lat_total + 1)
    face_sine = np.sin(math.pi * np.minimum(face, lat_total - face) / lat_total)
    row_sine = np.sin(math.pi * (np.arange(lat_total) + 0.5) / lat_total)
    scale = np.stack([face_sine[:-1] / row_sine, face_sine[1:] / row_sine], 1)
    scale = jnp.asarray(scale.reshape(-1).astype(np.float32))

    smem, vmem = pl.BlockSpec(memory_space=pltpu.SMEM), pl.BlockSpec(memory_space=pltpu.VMEM)
    direct = fields // 2
    swapped = fields - direct
    direct_shape = (3 * LEVELS + 1, direct, lons)

    payload = call(copy_kernel, (swapped,) + x.shape[1:])(x)
    near_a = swap(payload)
    zon, zon_t, near_rows, far_rows, columns = call(
        functools.partial(zonal_kernel, fields),
        [
            x.shape,
            t.shape,
            direct_shape,
            direct_shape,
            (3 * levels + 1,) + ground_gravity_height.shape,
        ],
        [(7, LEVELS * ROWS, lons)],
        cost=COST["zonal"],
    )(
        x,
        t,
        integer_boxes_traversed,
        partial_crossing_share,
        higher_donor_stratum,
        deeper_donor_share,
        napierian_thickness_quotient,
        ground_gravity_height,
    )
    far_b = exchange_across(far_rows)
    near_b = swap(near_rows)

    relay = call(relay_kernel, (3 * LEVELS, swapped, lons), cost=COST["relay"])(near_a, zon_t)
    far_a = pass_on(relay)

    peer_columns = other_core(columns)
    columns = jnp.where(
        lax.axis_index("lev") == 0,
        jnp.concatenate([columns, peer_columns], -1),
        jnp.concatenate([peer_columns, columns], -1),
    )

    mix, c_rows = call(
        functools.partial(mix_kernel, levels),
        [(levels, 2 * LEVELS, ROWS, lons), (LEVELS, lons)],
        cost=COST["mix"],
    )(columns, c, relay)
    c_south = lax.ppermute(c_rows, "lat", [(i, i + 1) for i in range(bands - 1)])
    weights, base, base_t = call(
        functools.partial(early_kernel, fields, bands - 1),
        [(ROWS + 6, LEVELS, ROWS, lons), x.shape, t.shape],
        [(3, LEVELS * ROWS, lons)],
        [smem] + [vmem] * 6,
        cost=COST["early"],
        aliases={5: 1, 6: 2},
    )(scale, c, c_south, x, t, zon, zon_t)

    adv_b = call(
        functools.partial(fin_kernel, 0, direct, True),
        (direct + 1,) + x.shape[1:],
        cost=COST["fin_b"],
    )(base, near_b, far_b, weights, base_t)
    peer_b = other_core(adv_b)
    adv_a = call(
        functools.partial(fin_kernel, direct, swapped, False),
        (swapped,) + x.shape[1:],
        cost=COST["fin_a"],
    )(base, near_a, far_a, weights)
    peer_a = other_core(adv_a)

    anywhere = pl.BlockSpec(memory_space=pl.ANY)
    first, thick = call(
        functools.partial(remap_first_kernel, levels),
        [(direct,) + x.shape[1:], (2 * levels, ROWS, lons)],
        cost=COST["first"],
    )(adv_b, peer_b, mix, columns)
    return call(
        functools.partial(remap_last_kernel, levels),
        [x.shape, t.shape, t.shape],
        [(swapped,) + x.shape[1:], pltpu.SemaphoreType.DMA((4 + swapped // 2,))],
        cost=COST["last"],
        out_specs=(anywhere,) * 3,
    )(adv_a, peer_a, mix, first, thick)


def solution(mesh):
    return jax.shard_map(
        on_device,
        mesh=mesh,
        in_specs=(
            P("ens", "lev", "lat", None),
            P(("ens", "lev"), "lat", None),
            P(("ens", "lev"), "lat", None),
            P(("ens", "lev"), "lat", None),
            P(("ens", "lev"), "lat", None),
            P("ens", "lat", "lev"),
            P("ens", "lat", "lev"),
            P("ens", "lat", "lev"),
            P(("ens", "lat"), "lev"),
        ),
        out_specs=(
            P("ens", "lev", "lat", None),
            P(("ens", "lev"), "lat", None),
            P(("ens", "lev"), "lat", None),
        ),
        check_vma=False,
    )
```

```python
import functools
import math

import jax
import jax.numpy as jnp
import numpy as np
from jax import lax
from jax.experimental import pallas as pl
from jax.experimental.pallas import tpu as pltpu
from jax.sharding import PartitionSpec as P

ROWS = 4
LEVELS = 2
LANE = 128

COST = dict(zonal=10000, relay=10000, early=1, patch=1, fin_b=1, fin_a=1, first=1, last=1)


def lanes(chunk):
    return pl.ds(chunk * LANE, LANE)


def parity():
    return lax.rem(lax.axis_index("lat"), 2)


def both(odd, body):
    @pl.when(odd == 1)
    def _():
        body(True)

    @pl.when(odd == 0)
    def _():
        body(False)


def copy_kernel(x, out):
    skip = x.shape[0] - out.shape[0]
    out[...] = x[skip:]


def side_rows(to_north):
    return (ROWS - 1, ROWS - 2, ROWS - 3) if to_north else (0, 1, 2)


def gather_rows(rows, x, t, c, out):
    count = out.shape[1]
    last = 3 * LEVELS
    for d, row in enumerate(rows):
        for lev in range(LEVELS):
            at = d * LEVELS + lev
            for f in range(count):
                out[at, f : f + 1, :] = x[f, lev, row : row + 1, :]
            out[last, at : at + 1, :] = t[lev, row : row + 1, :]
    for lev in range(LEVELS):
        out[last, last + lev : last + lev + 1, :] = c[lev, ROWS - 1 : ROWS, :]


def relay_kernel(swapped, zon_t, relay):
    def body(odd):
        for d, row in enumerate(side_rows(not odd)):
            for lev in range(LEVELS):
                for f in range(swapped.shape[0]):
                    relay[d * LEVELS + lev, f : f + 1, :] = swapped[f, lev, row : row + 1, :]

    both(parity(), body)


def parabola_weights(share):
    half = 0.5 * share
    curve = half * (1.0 - share * (2.0 / 3.0))
    right = (1.0 - half - 3.0 * curve) * (1.0 / 12.0)
    left = (half - 3.0 * curve) * (1.0 / 12.0)
    return (
        -share * left,
        share * (7.0 * left - right),
        share * (7.0 * (left + right) + 6.0 * curve),
        share * (7.0 * right - left),
        -share * right,
    )


def face_weights(courant):
    t = parabola_weights(jnp.abs(courant))
    north = courant >= 0.0
    zero = jnp.zeros_like(courant)
    return (
        jnp.where(north, t[0], zero),
        jnp.where(north, t[1], -t[4]),
        jnp.where(north, t[2], -t[3]),
        jnp.where(north, t[3], -t[2]),
        jnp.where(north, t[4], -t[1]),
        jnp.where(north, zero, -t[0]),
    )


def row_weights(c, below, scale, lat):
    row = lax.broadcasted_iota(jnp.int32, c.shape, 0) % ROWS

    def by_row(parts):
        total = parts[ROWS - 1]
        for j in range(ROWS - 2, -1, -1):
            total = jnp.where(row == j, parts[j], total)
        return total

    low = by_row([jnp.full(c.shape, scale[lat * 2 * ROWS + 2 * j]) for j in range(ROWS)])
    high = by_row([jnp.full(c.shape, scale[lat * 2 * ROWS + 2 * j + 1]) for j in range(ROWS)])
    lower = face_weights(below)
    upper = face_weights(c)
    offsets = {}
    for o in range(-3, 4):
        total = jnp.zeros_like(c)
        if o <= 2:
            total = total + low * lower[o + 3]
        if o >= -2:
            total = total - high * upper[o + 2]
        offsets[o] = total
    zero = jnp.zeros_like(c)
    return [by_row([offsets.get(r - j, zero) for j in range(ROWS)]) for r in range(-3, ROWS + 3)]


def stacked(ref):
    return jnp.concatenate([ref[lev] for lev in range(LEVELS)], axis=0)


def early_kernel(
    fields, levels, last, scale, columns, c, x, t, zon_in, zon_t_in,
    mix, out, zon, zon_t, factor, south_rows, south_rows_t, ws,
):
    lat = lax.axis_index("lat")
    lons = x.shape[-1]
    mix_weights(levels, columns, mix)
    factor[...] = jnp.full(factor.shape, jnp.where(lat == 0, 0.0, scale[lat * 2 * ROWS]))
    parts = []
    for lev in range(LEVELS):
        own = c[lev]
        parts += [
            jnp.where(lat == 0, -pltpu.roll(own, lons // 2, 1)[0:1], 0.0),
            own[: ROWS - 1],
        ]
    for r, w in enumerate(row_weights(stacked(c), jnp.concatenate(parts, axis=0), scale, lat)):
        for lev in range(LEVELS):
            out[r, lev] = w[lev * ROWS : (lev + 1) * ROWS]

    for lev in range(LEVELS):
        for r in range(3):
            at = r * LEVELS + lev
            south_rows_t[at : at + 1, :] = t[lev, r : r + 1, :]
            for i in range(fields):
                south_rows[at, i : i + 1, :] = x[i, lev, r : r + 1, :]
        for chunk in range(lons // LANE):
            lane = lanes(chunk)
            weights = [out[r + 3, lev, :, lane] for r in range(ROWS)]

            def with_own_rows(total, row_at):
                for r, w in enumerate(weights):
                    total = total + w * jnp.broadcast_to(row_at(r), total.shape)
                return total

            zon_t[lev, :, lane] = with_own_rows(
                zon_t_in[lev, :, lane], lambda r: t[lev, r : r + 1, lane]
            )
            for i in range(fields):
                zon[i, lev, :, lane] = with_own_rows(
                    zon_in[i, lev, :, lane], lambda r: x[i, lev, r : r + 1, lane]
                )

    def pole(rows):
        for k, (_, at) in enumerate(rows):
            ws[k] = stacked(out.at[at])
            for lev in range(LEVELS):
                out[at, lev] = jnp.zeros_like(out[at, lev])

        def beyond(ref):
            v = pltpu.roll(stacked(ref), lons // 2, 1)
            total = jnp.zeros_like(v)
            for k, (source, _) in enumerate(rows):
                both_rows = [
                    jnp.broadcast_to(v[r : r + 1], (ROWS, lons))
                    for r in range(source, LEVELS * ROWS, ROWS)
                ]
                total = total + ws[k] * jnp.concatenate(both_rows, axis=0)
            return [total[lev * ROWS : (lev + 1) * ROWS] for lev in range(LEVELS)]

        for lev, part in enumerate(beyond(t)):
            zon_t[lev] = zon_t[lev] + part

        @pl.loop(0, fields, step=2)
        def _(start):
            for i in (start, start + 1):
                for lev, part in enumerate(beyond(x.at[i])):
                    zon[i, lev] = zon[i, lev] + part

    @pl.when(lat == 0)
    def _():
        pole([(d - 1, 3 - d) for d in range(1, 4)])

    @pl.when(lat == last)
    def _():
        pole([(ROWS - d, ROWS + 2 + d) for d in range(1, 4)])


def patch_kernel(factor, near, far, weights, south_rows, south_rows_t, low, delta, delta_t):
    block = 3 * LEVELS
    rows = slice(block, block + LEVELS)
    below = jnp.where(parity() == 1, near[block, rows, :], far[block, rows, :])
    parts = [factor[...] * part for part in face_weights(below)]
    for r in range(3):
        for lev in range(LEVELS):
            w = weights[r, lev]
            low[r, lev] = w
            low[r, lev, 0:1, :] = w[0:1] + parts[r][lev : lev + 1]
    total_t = None
    for r in range(3):
        term = parts[r + 3] * south_rows_t[LEVELS * r : LEVELS * (r + 1), :]
        total_t = term if total_t is None else total_t + term
    delta_t[...] = total_t
    for lev in range(LEVELS):
        total = None
        for r in range(3):
            v = south_rows[r * LEVELS + lev]
            term = jnp.broadcast_to(parts[r + 3][lev : lev + 1], v.shape) * v
            total = term if total is None else total + term
        delta[lev] = total


def zonal_kernel(
    fields, x, t, n, f, c, upper, share, quotient, ground, zon, zon_t, near, far, columns, w
):
    lons = x.shape[-1]
    pack_columns(upper, share, quotient, ground, columns)

    def gather(odd):
        gather_rows(side_rows(not odd), x, t, c, near)
        gather_rows(side_rows(odd), x, t, c, far)

    both(parity(), gather)

    def shifted(values, k):
        return values if k == 0 else pltpu.roll(values, (-k) % lons, 1)

    def advance(v):
        flux = w[1] * v
        for k in (0, 2, 3, 4, 5, 6):
            flux = flux + w[k] * shifted(v, 1 - k)
        return v - (shifted(flux, 1) - flux)

    whole = stacked(n)
    s = parabola_weights(stacked(f))
    zero = jnp.zeros_like(s[0])
    n0, n1 = whole == 0, whole == 1

    def pick(a, b, d):
        return jnp.where(n0, a, jnp.where(n1, b, d))

    w[0] = pick(s[4], zero, zero)
    w[1] = pick(s[3], s[4], zero)
    w[2] = pick(s[2], s[3] + 1.0, s[4] + 1.0)
    w[3] = pick(s[1], s[2], s[3] + 1.0)
    w[4] = pick(s[0], s[1], s[2])
    w[5] = pick(zero, s[0], s[1])
    w[6] = pick(zero, zero, s[0])

    total = advance(stacked(t))
    for lev in range(LEVELS):
        zon_t[lev] = total[lev * ROWS : (lev + 1) * ROWS]

    @pl.loop(0, fields, step=2)
    def _(start):
        for i in (start, start + 1):
            total = advance(stacked(x.at[i]))
            for lev in range(LEVELS):
                zon[i, lev] = total[lev * ROWS : (lev + 1) * ROWS]


def fin_kernel(skip, count, direct, *refs):
    if direct:
        base, near, far, w, low, delta, base_t, delta_t, adv = refs
    else:
        base, near, far, w, low, delta, adv = refs
    chunks = w.shape[-1] // LANE
    first_row = lax.broadcasted_iota(jnp.int32, (ROWS, LANE), 0) == 0

    def body(odd):
        for lev in range(LEVELS):
            for chunk in range(chunks):
                lane = lanes(chunk)
                sides = [
                    (low[3 - d, lev, :, lane], w[ROWS + 2 + d, lev, :, lane]) for d in range(1, 4)
                ]

                def total_of(total, row_0, near_row, far_row):
                    total = total + jnp.where(first_row, jnp.broadcast_to(row_0, total.shape), 0.0)
                    for d, (south, north) in enumerate(sides, 1):
                        for weight, is_near in ((south, odd), (north, not odd)):
                            v = near_row(d) if is_near else far_row(d)
                            total = total + weight * jnp.broadcast_to(v, total.shape)
                    return total

                def gathered(ref, f):
                    return lambda d: ref[(d - 1) * LEVELS + lev, f : f + 1, lane]

                def swapped(ref, f):
                    def row_at(d):
                        row = side_rows(odd)[d - 1]
                        return ref[f, lev, row : row + 1, lane]

                    return row_at

                def gathered_t(ref):
                    def row_at(d):
                        at = (d - 1) * LEVELS + lev
                        return ref[3 * LEVELS, at : at + 1, lane]

                    return row_at

                for f in range(count):
                    adv[f, lev, :, lane] = total_of(
                        base[skip + f, lev, :, lane],
                        delta[lev, skip + f : skip + f + 1, lane],
                        gathered(near, f) if direct else swapped(near, f),
                        gathered(far, f),
                    )
                if direct:
                    adv[count, lev, :, lane] = total_of(
                        base_t[lev, :, lane],
                        delta_t[lev : lev + 1, lane],
                        gathered_t(near),
                        gathered_t(far),
                    )

    both(parity(), body)


def pack_columns(upper, share, quotient, ground, out):
    levels = upper.shape[0]
    out[:levels] = upper[...].astype(jnp.float32)
    out[levels : 2 * levels] = share[...]
    out[2 * levels : 3 * levels] = quotient[...]
    out[3 * levels] = ground[...]


def mix_weights(levels, columns, weights):
    group = lax.axis_index("lev")
    for k in range(levels):
        upper = columns[k]
        share = columns[levels + k]
        for s in range(2 * LEVELS):
            level = (group if s < LEVELS else 1 - group) * LEVELS + s % LEVELS
            at = level.astype(jnp.float32)
            weights[k, s] = jnp.where(
                upper == at, 1.0 - share, jnp.where(upper + 1.0 == at, share, 0.0)
            )


def mixed(weights, values):
    total = weights[0] * values[0]
    for w, v in zip(weights[1:], values[1:]):
        total = total + w * v
    return total


def blend(own, peer, weights, out, fields, skip=0):
    group = lax.axis_index("lev")
    for chunk in range(own.shape[-1] // LANE):
        lane = lanes(chunk)
        ws = [
            [weights[group * LEVELS + lev, s, :, lane] for s in range(2 * LEVELS)]
            for lev in range(LEVELS)
        ]
        for f in fields:
            values = [adv[f, lev, :, lane] for adv in (own, peer) for lev in range(LEVELS)]
            for lev in range(LEVELS):
                out[skip + f, lev, :, lane] = mixed(ws[lev], values)


def remap_first_kernel(levels, own, peer, weights, columns, out, thick):
    count = out.shape[0]
    vapour = [adv[0, lev] for adv in (own, peer) for lev in range(LEVELS)]
    temp = [adv[count, lev] for adv in (own, peer) for lev in range(LEVELS)]
    for k in range(levels):
        ws = [weights[k, s] for s in range(2 * LEVELS)]
        water = mixed(ws, vapour)
        heat = mixed(ws, temp)
        thick[k] = heat * (1.0 + 0.608 * water) * columns[2 * levels + k]
        thick[levels + k] = heat
    deeper = columns[3 * levels]
    for k in range(levels - 1, -1, -1):
        layer = thick[k]
        thick[k] = deeper + 0.5 * layer
        deeper = deeper + layer
    blend(own, peer, weights, out, range(count))


def remap_last_kernel(levels, own, peer, weights, first, thick, out, out_t, out_phi, buffer, sems):
    group = lax.axis_index("lev")
    count = first.shape[0]
    copies = []

    def send(source, target):
        copy = pltpu.make_async_copy(source, target, sems.at[len(copies)])
        copy.start()
        copies.append(copy)

    half = count // 2
    for start in (0, half):
        send(first.at[pl.ds(start, half)], out.at[pl.ds(start, half)])
    mine = group * LEVELS
    send(thick.at[pl.ds(mine, LEVELS)], out_phi)
    send(thick.at[pl.ds(levels + mine, LEVELS)], out_t)
    step = 2
    for start in range(0, buffer.shape[0], step):
        blend(own, peer, weights, buffer, range(start, start + step))
        send(buffer.at[pl.ds(start, step)], out.at[pl.ds(count + start, step)])
    for copy in copies:
        copy.wait()


def call(kernel, outs, scratch=(), specs=None, cost=0, limit=12, aliases=None, out_specs=None):
    single = not isinstance(outs, list)
    shapes = tuple(jax.ShapeDtypeStruct(s, jnp.float32) for s in ([outs] if single else outs))
    extra = {} if specs is None else {"in_specs": specs}
    if out_specs is not None:
        extra["out_specs"] = out_specs
    return pl.pallas_call(
        kernel,
        out_shape=shapes[0] if single else shapes,
        scratch_shapes=[pltpu.VMEM(s, jnp.float32) if isinstance(s, tuple) else s for s in scratch],
        compiler_params=pltpu.CompilerParams(vmem_limit_bytes=limit * 2**20),
        cost_estimate=pl.CostEstimate(flops=cost * 10**6, bytes_accessed=1000, transcendentals=0),
        input_output_aliases=aliases or {},
        **extra,
    )


def on_device(
    constituent_densities,
    thermal_state,
    integer_boxes_traversed,
    partial_crossing_share,
    northward_crossing_share,
    higher_donor_stratum,
    deeper_donor_share,
    napierian_thickness_quotient,
    ground_gravity_height,
):
    x, t, c = constituent_densities, thermal_state, northward_crossing_share
    fields, _, _, lons = x.shape
    levels = higher_donor_stratum.shape[0]
    bands = lax.axis_size("lat")
    lat_total = bands * ROWS

    pairs = [(i, i ^ 1) for i in range(bands)]
    across = [(i, i + 1 if i % 2 else i - 1) for i in range(1, bands - 1)]
    relays = [(i, i + 2) for i in range(0, bands - 2, 2)] + [(i, i - 2) for i in range(3, bands, 2)]
    cores = [(0, 1), (1, 0)]

    def swap(v):
        return lax.ppermute(v, "lat", pairs)

    def exchange_across(v):
        return lax.ppermute(v, "lat", across)

    def pass_on(v):
        return lax.ppermute(v, "lat", relays)

    def other_core(v):
        return lax.ppermute(v, "lev", cores)

    face = np.arange(lat_total + 1)
    face_sine = np.sin(math.pi * np.minimum(face, lat_total - face) / lat_total)
    row_sine = np.sin(math.pi * (np.arange(lat_total) + 0.5) / lat_total)
    scale = np.stack([face_sine[:-1] / row_sine, face_sine[1:] / row_sine], 1)
    scale = jnp.asarray(scale.reshape(-1).astype(np.float32))

    smem, vmem = pl.BlockSpec(memory_space=pltpu.SMEM), pl.BlockSpec(memory_space=pltpu.VMEM)
    direct = fields // 2
    swapped = fields - direct
    direct_shape = (3 * LEVELS + 1, direct, lons)

    payload = call(copy_kernel, (swapped,) + x.shape[1:])(x)
    near_a = swap(payload)
    zon, zon_t, near_rows, far_rows, columns = call(
        functools.partial(zonal_kernel, fields),
        [
            x.shape,
            t.shape,
            direct_shape,
            direct_shape,
            (3 * levels + 1,) + ground_gravity_height.shape,
        ],
        [(7, LEVELS * ROWS, lons)],
        cost=COST["zonal"],
    )(
        x,
        t,
        integer_boxes_traversed,
        partial_crossing_share,
        c,
        higher_donor_stratum,
        deeper_donor_share,
        napierian_thickness_quotient,
        ground_gravity_height,
    )
    far_b = exchange_across(far_rows)
    near_b = swap(near_rows)

    relay = call(relay_kernel, (3 * LEVELS, swapped, lons), cost=COST["relay"])(near_a, zon_t)
    far_a = pass_on(relay)

    peer_columns = other_core(columns)
    columns = jnp.where(
        lax.axis_index("lev") == 0,
        jnp.concatenate([columns, peer_columns], -1),
        jnp.concatenate([peer_columns, columns], -1),
    )

    mix, weights, base, base_t, factor, south_rows, south_rows_t = call(
        functools.partial(early_kernel, fields, levels, bands - 1),
        [
            (levels, 2 * LEVELS, ROWS, lons),
            (ROWS + 6, LEVELS, ROWS, lons),
            x.shape,
            t.shape,
            (LEVELS, lons),
            (3 * LEVELS, fields, lons),
            (3 * LEVELS, lons),
        ],
        [(3, LEVELS * ROWS, lons)],
        [smem] + [vmem] * 6,
        cost=COST["early"],
    )(scale, columns, c, x, t, zon, zon_t)
    low, delta, delta_t = call(
        patch_kernel,
        [(3, LEVELS, ROWS, lons), (LEVELS, fields, lons), (LEVELS, lons)],
        cost=COST["patch"],
    )(factor, near_b, far_b, weights, south_rows, south_rows_t)

    adv_b = call(
        functools.partial(fin_kernel, 0, direct, True),
        (direct + 1,) + x.shape[1:],
        cost=COST["fin_b"],
    )(base, near_b, far_b, weights, low, delta, base_t, delta_t)
    peer_b = other_core(adv_b)
    adv_a = call(
        functools.partial(fin_kernel, direct, swapped, False),
        (swapped,) + x.shape[1:],
        cost=COST["fin_a"],
    )(base, near_a, far_a, weights, low, delta)
    peer_a = other_core(adv_a)

    anywhere = pl.BlockSpec(memory_space=pl.ANY)
    first, thick = call(
        functools.partial(remap_first_kernel, levels),
        [(direct,) + x.shape[1:], (2 * levels, ROWS, lons)],
        cost=COST["first"],
    )(adv_b, peer_b, mix, columns)
    return call(
        functools.partial(remap_last_kernel, levels),
        [x.shape, t.shape, t.shape],
        [(swapped,) + x.shape[1:], pltpu.SemaphoreType.DMA((4 + swapped // 2,))],
        cost=COST["last"],
        out_specs=(anywhere,) * 3,
    )(adv_a, peer_a, mix, first, thick)


def solution(mesh):
    return jax.shard_map(
        on_device,
        mesh=mesh,
        in_specs=(
            P("ens", "lev", "lat", None),
            P(("ens", "lev"), "lat", None),
            P(("ens", "lev"), "lat", None),
            P(("ens", "lev"), "lat", None),
            P(("ens", "lev"), "lat", None),
            P("ens", "lat", "lev"),
            P("ens", "lat", "lev"),
            P("ens", "lat", "lev"),
            P(("ens", "lat"), "lev"),
        ),
        out_specs=(
            P("ens", "lev", "lat", None),
            P(("ens", "lev"), "lat", None),
            P(("ens", "lev"), "lat", None),
        ),
        check_vma=False,
    )
```

```python
import functools
import math

import jax
import jax.numpy as jnp
import numpy as np
from jax import lax
from jax.experimental import pallas as pl
from jax.experimental.pallas import tpu as pltpu
from jax.sharding import PartitionSpec as P

ROWS = 4
LEVELS = 2
LANE = 128

COST = dict(zonal=10000, relay=10000, early=1, patch=1, fin_b=1, fin_a=1, first=1, last=1)


def lanes(chunk):
    return pl.ds(chunk * LANE, LANE)


def parity():
    return lax.rem(lax.axis_index("lat"), 2)


def both(odd, body):
    @pl.when(odd == 1)
    def _():
        body(True)

    @pl.when(odd == 0)
    def _():
        body(False)


def copy_kernel(x, out):
    skip = x.shape[0] - out.shape[0]
    out[...] = x[skip:]


def side_rows(to_north):
    return (ROWS - 1, ROWS - 2, ROWS - 3) if to_north else (0, 1, 2)


def gather_rows(rows, x, t, c, out):
    count = out.shape[1]
    last = 3 * LEVELS
    for d, row in enumerate(rows):
        for lev in range(LEVELS):
            at = d * LEVELS + lev
            for f in range(count):
                out[at, f : f + 1, :] = x[f, lev, row : row + 1, :]
            out[last, at : at + 1, :] = t[lev, row : row + 1, :]
    for lev in range(LEVELS):
        out[last, last + lev : last + lev + 1, :] = c[lev, ROWS - 1 : ROWS, :]


def relay_kernel(swapped, zon_t, relay):
    def body(odd):
        for d, row in enumerate(side_rows(not odd)):
            for lev in range(LEVELS):
                for f in range(swapped.shape[0]):
                    relay[d * LEVELS + lev, f : f + 1, :] = swapped[f, lev, row : row + 1, :]

    both(parity(), body)


def parabola_weights(share):
    half = 0.5 * share
    curve = half * (1.0 - share * (2.0 / 3.0))
    right = (1.0 - half - 3.0 * curve) * (1.0 / 12.0)
    left = (half - 3.0 * curve) * (1.0 / 12.0)
    return (
        -share * left,
        share * (7.0 * left - right),
        share * (7.0 * (left + right) + 6.0 * curve),
        share * (7.0 * right - left),
        -share * right,
    )


def face_weights(courant):
    t = parabola_weights(jnp.abs(courant))
    north = courant >= 0.0
    zero = jnp.zeros_like(courant)
    return (
        jnp.where(north, t[0], zero),
        jnp.where(north, t[1], -t[4]),
        jnp.where(north, t[2], -t[3]),
        jnp.where(north, t[3], -t[2]),
        jnp.where(north, t[4], -t[1]),
        jnp.where(north, zero, -t[0]),
    )


def row_weights(c, below, scale, lat):
    row = lax.broadcasted_iota(jnp.int32, c.shape, 0) % ROWS

    def by_row(parts):
        total = parts[ROWS - 1]
        for j in range(ROWS - 2, -1, -1):
            total = jnp.where(row == j, parts[j], total)
        return total

    low = by_row([jnp.full(c.shape, scale[lat * 2 * ROWS + 2 * j]) for j in range(ROWS)])
    high = by_row([jnp.full(c.shape, scale[lat * 2 * ROWS + 2 * j + 1]) for j in range(ROWS)])
    lower = face_weights(below)
    upper = face_weights(c)
    offsets = {}
    for o in range(-3, 4):
        total = jnp.zeros_like(c)
        if o <= 2:
            total = total + low * lower[o + 3]
        if o >= -2:
            total = total - high * upper[o + 2]
        offsets[o] = total
    zero = jnp.zeros_like(c)
    return [by_row([offsets.get(r - j, zero) for j in range(ROWS)]) for r in range(-3, ROWS + 3)]


def stacked(ref):
    return jnp.concatenate([ref[lev] for lev in range(LEVELS)], axis=0)


def early_kernel(
    fields, levels, last, scale, columns, c, x, t, zon_in, zon_t_in,
    mix, out, zon, zon_t, factor, south_rows, south_rows_t, ws,
):
    lat = lax.axis_index("lat")
    lons = x.shape[-1]
    mix_weights(levels, columns, mix)
    factor[...] = jnp.full(factor.shape, jnp.where(lat == 0, 0.0, scale[lat * 2 * ROWS]))
    parts = []
    for lev in range(LEVELS):
        own = c[lev]
        parts += [
            jnp.where(lat == 0, -pltpu.roll(own, lons // 2, 1)[0:1], 0.0),
            own[: ROWS - 1],
        ]
    for r, w in enumerate(row_weights(stacked(c), jnp.concatenate(parts, axis=0), scale, lat)):
        for lev in range(LEVELS):
            out[r, lev] = w[lev * ROWS : (lev + 1) * ROWS]

    for lev in range(LEVELS):
        for r in range(3):
            at = r * LEVELS + lev
            south_rows_t[at : at + 1, :] = t[lev, r : r + 1, :]
            for i in range(fields):
                south_rows[at, i : i + 1, :] = x[i, lev, r : r + 1, :]
        for chunk in range(lons // LANE):
            lane = lanes(chunk)
            weights = [out[r + 3, lev, :, lane] for r in range(ROWS)]

            def with_own_rows(total, row_at):
                for r, w in enumerate(weights):
                    total = total + w * jnp.broadcast_to(row_at(r), total.shape)
                return total

            zon_t[lev, :, lane] = with_own_rows(
                zon_t_in[lev, :, lane], lambda r: t[lev, r : r + 1, lane]
            )
            for i in range(fields):
                zon[i, lev, :, lane] = with_own_rows(
                    zon_in[i, lev, :, lane], lambda r: x[i, lev, r : r + 1, lane]
                )

    def pole(rows):
        for k, (_, at) in enumerate(rows):
            ws[k] = stacked(out.at[at])
            for lev in range(LEVELS):
                out[at, lev] = jnp.zeros_like(out[at, lev])

        def beyond(ref):
            v = pltpu.roll(stacked(ref), lons // 2, 1)
            total = jnp.zeros_like(v)
            for k, (source, _) in enumerate(rows):
                both_rows = [
                    jnp.broadcast_to(v[r : r + 1], (ROWS, lons))
                    for r in range(source, LEVELS * ROWS, ROWS)
                ]
                total = total + ws[k] * jnp.concatenate(both_rows, axis=0)
            return [total[lev * ROWS : (lev + 1) * ROWS] for lev in range(LEVELS)]

        for lev, part in enumerate(beyond(t)):
            zon_t[lev] = zon_t[lev] + part

        @pl.loop(0, fields, step=2)
        def _(start):
            for i in (start, start + 1):
                for lev, part in enumerate(beyond(x.at[i])):
                    zon[i, lev] = zon[i, lev] + part

    @pl.when(lat == 0)
    def _():
        pole([(d - 1, 3 - d) for d in range(1, 4)])

    @pl.when(lat == last)
    def _():
        pole([(ROWS - d, ROWS + 2 + d) for d in range(1, 4)])


def patch_kernel(factor, near, far, weights, south_rows, south_rows_t, low, delta, delta_t):
    block = 3 * LEVELS
    rows = slice(block, block + LEVELS)
    below = jnp.where(parity() == 1, near[block, rows, :], far[block, rows, :])
    parts = [factor[...] * part for part in face_weights(below)]
    for r in range(3):
        for lev in range(LEVELS):
            w = weights[r, lev]
            low[r, lev] = w
            low[r, lev, 0:1, :] = w[0:1] + parts[r][lev : lev + 1]
    total_t = None
    for r in range(3):
        term = parts[r + 3] * south_rows_t[LEVELS * r : LEVELS * (r + 1), :]
        total_t = term if total_t is None else total_t + term
    delta_t[...] = total_t
    for lev in range(LEVELS):
        total = None
        for r in range(3):
            v = south_rows[r * LEVELS + lev]
            term = jnp.broadcast_to(parts[r + 3][lev : lev + 1], v.shape) * v
            total = term if total is None else total + term
        delta[lev] = total


def zonal_kernel(
    fields, x, t, n, f, c, upper, share, quotient, ground, zon, zon_t, near, far, columns, w
):
    lons = x.shape[-1]
    pack_columns(upper, share, quotient, ground, columns)

    def gather(odd):
        gather_rows(side_rows(not odd), x, t, c, near)
        gather_rows(side_rows(odd), x, t, c, far)

    both(parity(), gather)

    def shifted(values, k):
        return values if k == 0 else pltpu.roll(values, (-k) % lons, 1)

    def advance(v):
        flux = w[1] * v
        for k in (0, 2, 3, 4, 5, 6):
            flux = flux + w[k] * shifted(v, 1 - k)
        return v - (shifted(flux, 1) - flux)

    whole = stacked(n)
    s = parabola_weights(stacked(f))
    zero = jnp.zeros_like(s[0])
    n0, n1 = whole == 0, whole == 1

    def pick(a, b, d):
        return jnp.where(n0, a, jnp.where(n1, b, d))

    w[0] = pick(s[4], zero, zero)
    w[1] = pick(s[3], s[4], zero)
    w[2] = pick(s[2], s[3] + 1.0, s[4] + 1.0)
    w[3] = pick(s[1], s[2], s[3] + 1.0)
    w[4] = pick(s[0], s[1], s[2])
    w[5] = pick(zero, s[0], s[1])
    w[6] = pick(zero, zero, s[0])

    total = advance(stacked(t))
    for lev in range(LEVELS):
        zon_t[lev] = total[lev * ROWS : (lev + 1) * ROWS]

    @pl.loop(0, fields, step=2)
    def _(start):
        for i in (start, start + 1):
            total = advance(stacked(x.at[i]))
            for lev in range(LEVELS):
                zon[i, lev] = total[lev * ROWS : (lev + 1) * ROWS]


def fin_kernel(skip, count, direct, *refs):
    if direct:
        base, near, far, w, low, delta, base_t, delta_t, adv = refs
    else:
        base, near, far, w, low, delta, adv = refs
    chunks = w.shape[-1] // LANE
    first_row = lax.broadcasted_iota(jnp.int32, (ROWS, LANE), 0) == 0

    def body(odd):
        for lev in range(LEVELS):
            for chunk in range(chunks):
                lane = lanes(chunk)
                sides = [
                    (low[3 - d, lev, :, lane], w[ROWS + 2 + d, lev, :, lane]) for d in range(1, 4)
                ]

                def total_of(total, row_0, near_row, far_row):
                    total = total + jnp.where(first_row, jnp.broadcast_to(row_0, total.shape), 0.0)
                    for d, (south, north) in enumerate(sides, 1):
                        for weight, is_near in ((south, odd), (north, not odd)):
                            v = near_row(d) if is_near else far_row(d)
                            total = total + weight * jnp.broadcast_to(v, total.shape)
                    return total

                def gathered(ref, f):
                    return lambda d: ref[(d - 1) * LEVELS + lev, f : f + 1, lane]

                def swapped(ref, f):
                    def row_at(d):
                        row = side_rows(odd)[d - 1]
                        return ref[f, lev, row : row + 1, lane]

                    return row_at

                def gathered_t(ref):
                    def row_at(d):
                        at = (d - 1) * LEVELS + lev
                        return ref[3 * LEVELS, at : at + 1, lane]

                    return row_at

                for f in range(count):
                    adv[f, lev, :, lane] = total_of(
                        base[skip + f, lev, :, lane],
                        delta[lev, skip + f : skip + f + 1, lane],
                        gathered(near, f) if direct else swapped(near, f),
                        gathered(far, f),
                    )
                if direct:
                    adv[count, lev, :, lane] = total_of(
                        base_t[lev, :, lane],
                        delta_t[lev : lev + 1, lane],
                        gathered_t(near),
                        gathered_t(far),
                    )

    both(parity(), body)


def pack_columns(upper, share, quotient, ground, out):
    levels = upper.shape[0]
    out[:levels] = upper[...].astype(jnp.float32)
    out[levels : 2 * levels] = share[...]
    out[2 * levels : 3 * levels] = quotient[...]
    out[3 * levels] = ground[...]


def mix_weights(levels, columns, weights):
    group = lax.axis_index("lev")
    for k in range(levels):
        upper = columns[k]
        share = columns[levels + k]
        for s in range(2 * LEVELS):
            level = (group if s < LEVELS else 1 - group) * LEVELS + s % LEVELS
            at = level.astype(jnp.float32)
            weights[k, s] = jnp.where(
                upper == at, 1.0 - share, jnp.where(upper + 1.0 == at, share, 0.0)
            )


def mixed(weights, values):
    total = weights[0] * values[0]
    for w, v in zip(weights[1:], values[1:]):
        total = total + w * v
    return total


def blend(own, peer, weights, out, fields, skip=0):
    group = lax.axis_index("lev")
    for chunk in range(own.shape[-1] // LANE):
        lane = lanes(chunk)
        ws = [
            [weights[group * LEVELS + lev, s, :, lane] for s in range(2 * LEVELS)]
            for lev in range(LEVELS)
        ]
        for f in fields:
            values = [adv[f, lev, :, lane] for adv in (own, peer) for lev in range(LEVELS)]
            for lev in range(LEVELS):
                out[skip + f, lev, :, lane] = mixed(ws[lev], values)


def remap_first_kernel(levels, own, peer, weights, columns, out, thick):
    count = out.shape[0]
    vapour = [adv[0, lev] for adv in (own, peer) for lev in range(LEVELS)]
    temp = [adv[count, lev] for adv in (own, peer) for lev in range(LEVELS)]
    for k in range(levels):
        ws = [weights[k, s] for s in range(2 * LEVELS)]
        water = mixed(ws, vapour)
        heat = mixed(ws, temp)
        thick[k] = heat * (1.0 + 0.608 * water) * columns[2 * levels + k]
        thick[levels + k] = heat
    deeper = columns[3 * levels]
    for k in range(levels - 1, -1, -1):
        layer = thick[k]
        thick[k] = deeper + 0.5 * layer
        deeper = deeper + layer
    blend(own, peer, weights, out, range(count))


def remap_last_kernel(levels, own, peer, weights, first, thick, out, out_t, out_phi, buffer, sems):
    group = lax.axis_index("lev")
    count = first.shape[0]
    copies = []

    def send(source, target):
        copy = pltpu.make_async_copy(source, target, sems.at[len(copies)])
        copy.start()
        copies.append(copy)

    piece = count // 1
    for start in range(0, count, piece):
        send(first.at[pl.ds(start, piece)], out.at[pl.ds(start, piece)])
    mine = group * LEVELS
    send(thick.at[pl.ds(mine, LEVELS)], out_phi)
    send(thick.at[pl.ds(levels + mine, LEVELS)], out_t)
    step = 4
    for start in range(0, buffer.shape[0], step):
        blend(own, peer, weights, buffer, range(start, start + step))
        send(buffer.at[pl.ds(start, step)], out.at[pl.ds(count + start, step)])
    for copy in copies:
        copy.wait()


def call(kernel, outs, scratch=(), specs=None, cost=0, limit=12, aliases=None, out_specs=None):
    single = not isinstance(outs, list)
    shapes = tuple(jax.ShapeDtypeStruct(s, jnp.float32) for s in ([outs] if single else outs))
    extra = {} if specs is None else {"in_specs": specs}
    if out_specs is not None:
        extra["out_specs"] = out_specs
    return pl.pallas_call(
        kernel,
        out_shape=shapes[0] if single else shapes,
        scratch_shapes=[pltpu.VMEM(s, jnp.float32) if isinstance(s, tuple) else s for s in scratch],
        compiler_params=pltpu.CompilerParams(vmem_limit_bytes=limit * 2**20),
        cost_estimate=pl.CostEstimate(flops=cost * 10**6, bytes_accessed=1000, transcendentals=0),
        input_output_aliases=aliases or {},
        **extra,
    )


def on_device(
    constituent_densities,
    thermal_state,
    integer_boxes_traversed,
    partial_crossing_share,
    northward_crossing_share,
    higher_donor_stratum,
    deeper_donor_share,
    napierian_thickness_quotient,
    ground_gravity_height,
):
    x, t, c = constituent_densities, thermal_state, northward_crossing_share
    fields, _, _, lons = x.shape
    levels = higher_donor_stratum.shape[0]
    bands = lax.axis_size("lat")
    lat_total = bands * ROWS

    pairs = [(i, i ^ 1) for i in range(bands)]
    across = [(i, i + 1 if i % 2 else i - 1) for i in range(1, bands - 1)]
    relays = [(i, i + 2) for i in range(0, bands - 2, 2)] + [(i, i - 2) for i in range(3, bands, 2)]
    cores = [(0, 1), (1, 0)]

    def swap(v):
        return lax.ppermute(v, "lat", pairs)

    def exchange_across(v):
        return lax.ppermute(v, "lat", across)

    def pass_on(v):
        return lax.ppermute(v, "lat", relays)

    def other_core(v):
        return lax.ppermute(v, "lev", cores)

    face = np.arange(lat_total + 1)
    face_sine = np.sin(math.pi * np.minimum(face, lat_total - face) / lat_total)
    row_sine = np.sin(math.pi * (np.arange(lat_total) + 0.5) / lat_total)
    scale = np.stack([face_sine[:-1] / row_sine, face_sine[1:] / row_sine], 1)
    scale = jnp.asarray(scale.reshape(-1).astype(np.float32))

    smem, vmem = pl.BlockSpec(memory_space=pltpu.SMEM), pl.BlockSpec(memory_space=pltpu.VMEM)
    direct = fields // 2
    swapped = fields - direct
    direct_shape = (3 * LEVELS + 1, direct, lons)

    payload = call(copy_kernel, (swapped,) + x.shape[1:])(x)
    near_a = swap(payload)
    zon, zon_t, near_rows, far_rows, columns = call(
        functools.partial(zonal_kernel, fields),
        [
            x.shape,
            t.shape,
            direct_shape,
            direct_shape,
            (3 * levels + 1,) + ground_gravity_height.shape,
        ],
        [(7, LEVELS * ROWS, lons)],
        cost=COST["zonal"],
    )(
        x,
        t,
        integer_boxes_traversed,
        partial_crossing_share,
        c,
        higher_donor_stratum,
        deeper_donor_share,
        napierian_thickness_quotient,
        ground_gravity_height,
    )
    far_b = exchange_across(far_rows)
    near_b = swap(near_rows)

    relay = call(relay_kernel, (3 * LEVELS, swapped, lons), cost=COST["relay"])(near_a, zon_t)
    far_a = pass_on(relay)

    peer_columns = other_core(columns)
    columns = jnp.where(
        lax.axis_index("lev") == 0,
        jnp.concatenate([columns, peer_columns], -1),
        jnp.concatenate([peer_columns, columns], -1),
    )

    mix, weights, base, base_t, factor, south_rows, south_rows_t = call(
        functools.partial(early_kernel, fields, levels, bands - 1),
        [
            (levels, 2 * LEVELS, ROWS, lons),
            (ROWS + 6, LEVELS, ROWS, lons),
            x.shape,
            t.shape,
            (LEVELS, lons),
            (3 * LEVELS, fields, lons),
            (3 * LEVELS, lons),
        ],
        [(3, LEVELS * ROWS, lons)],
        [smem] + [vmem] * 6,
        cost=COST["early"],
    )(scale, columns, c, x, t, zon, zon_t)
    low, delta, delta_t = call(
        patch_kernel,
        [(3, LEVELS, ROWS, lons), (LEVELS, fields, lons), (LEVELS, lons)],
        cost=COST["patch"],
    )(factor, near_b, far_b, weights, south_rows, south_rows_t)

    adv_b = call(
        functools.partial(fin_kernel, 0, direct, True),
        (direct + 1,) + x.shape[1:],
        cost=COST["fin_b"],
    )(base, near_b, far_b, weights, low, delta, base_t, delta_t)
    peer_b = other_core(adv_b)
    adv_a = call(
        functools.partial(fin_kernel, direct, swapped, False),
        (swapped,) + x.shape[1:],
        cost=COST["fin_a"],
    )(base, near_a, far_a, weights, low, delta)
    peer_a = other_core(adv_a)

    anywhere = pl.BlockSpec(memory_space=pl.ANY)
    first, thick = call(
        functools.partial(remap_first_kernel, levels),
        [(direct,) + x.shape[1:], (2 * levels, ROWS, lons)],
        cost=COST["first"],
    )(adv_b, peer_b, mix, columns)
    return call(
        functools.partial(remap_last_kernel, levels),
        [x.shape, t.shape, t.shape],
        [(swapped,) + x.shape[1:], pltpu.SemaphoreType.DMA((2 + 1 + swapped // 4,))],
        cost=COST["last"],
        out_specs=(anywhere,) * 3,
    )(adv_a, peer_a, mix, first, thick)


def solution(mesh):
    return jax.shard_map(
        on_device,
        mesh=mesh,
        in_specs=(
            P("ens", "lev", "lat", None),
            P(("ens", "lev"), "lat", None),
            P(("ens", "lev"), "lat", None),
            P(("ens", "lev"), "lat", None),
            P(("ens", "lev"), "lat", None),
            P("ens", "lat", "lev"),
            P("ens", "lat", "lev"),
            P("ens", "lat", "lev"),
            P(("ens", "lat"), "lev"),
        ),
        out_specs=(
            P("ens", "lev", "lat", None),
            P(("ens", "lev"), "lat", None),
            P(("ens", "lev"), "lat", None),
        ),
        check_vma=False,
    )
```

```python
import functools
import math

import jax
import jax.numpy as jnp
import numpy as np
from jax import lax
from jax.experimental import pallas as pl
from jax.experimental.pallas import tpu as pltpu
from jax.sharding import PartitionSpec as P

ROWS = 4
LEVELS = 2
LANE = 128

COST = dict(zonal=10000, relay=10000, early=1, patch=1, fin_b=1, fin_a=1, first=1, last=1)


def lanes(chunk):
    return pl.ds(chunk * LANE, LANE)


def parity():
    return lax.rem(lax.axis_index("lat"), 2)


def both(odd, body):
    @pl.when(odd == 1)
    def _():
        body(True)

    @pl.when(odd == 0)
    def _():
        body(False)


def copy_kernel(x, out):
    skip = x.shape[0] - out.shape[0]
    out[...] = x[skip:]


def side_rows(to_north):
    return (ROWS - 1, ROWS - 2, ROWS - 3) if to_north else (0, 1, 2)


def gather_rows(rows, x, t, c, out):
    count = out.shape[1]
    last = 3 * LEVELS
    for d, row in enumerate(rows):
        for lev in range(LEVELS):
            at = d * LEVELS + lev
            for f in range(count):
                out[at, f : f + 1, :] = x[f, lev, row : row + 1, :]
            out[last, at : at + 1, :] = t[lev, row : row + 1, :]
    for lev in range(LEVELS):
        out[last, last + lev : last + lev + 1, :] = c[lev, ROWS - 1 : ROWS, :]


def relay_kernel(swapped, zon_t, relay):
    def body(odd):
        for d, row in enumerate(side_rows(not odd)):
            for lev in range(LEVELS):
                for f in range(swapped.shape[0]):
                    relay[d * LEVELS + lev, f : f + 1, :] = swapped[f, lev, row : row + 1, :]

    both(parity(), body)


def parabola_weights(share):
    half = 0.5 * share
    curve = half * (1.0 - share * (2.0 / 3.0))
    right = (1.0 - half - 3.0 * curve) * (1.0 / 12.0)
    left = (half - 3.0 * curve) * (1.0 / 12.0)
    return (
        -share * left,
        share * (7.0 * left - right),
        share * (7.0 * (left + right) + 6.0 * curve),
        share * (7.0 * right - left),
        -share * right,
    )


def face_weights(courant):
    t = parabola_weights(jnp.abs(courant))
    north = courant >= 0.0
    zero = jnp.zeros_like(courant)
    return (
        jnp.where(north, t[0], zero),
        jnp.where(north, t[1], -t[4]),
        jnp.where(north, t[2], -t[3]),
        jnp.where(north, t[3], -t[2]),
        jnp.where(north, t[4], -t[1]),
        jnp.where(north, zero, -t[0]),
    )


def row_weights(c, below, scale, lat):
    row = lax.broadcasted_iota(jnp.int32, c.shape, 0) % ROWS

    def by_row(parts):
        total = parts[ROWS - 1]
        for j in range(ROWS - 2, -1, -1):
            total = jnp.where(row == j, parts[j], total)
        return total

    low = by_row([jnp.full(c.shape, scale[lat * 2 * ROWS + 2 * j]) for j in range(ROWS)])
    high = by_row([jnp.full(c.shape, scale[lat * 2 * ROWS + 2 * j + 1]) for j in range(ROWS)])
    lower = face_weights(below)
    upper = face_weights(c)
    offsets = {}
    for o in range(-3, 4):
        total = jnp.zeros_like(c)
        if o <= 2:
            total = total + low * lower[o + 3]
        if o >= -2:
            total = total - high * upper[o + 2]
        offsets[o] = total
    zero = jnp.zeros_like(c)
    return [by_row([offsets.get(r - j, zero) for j in range(ROWS)]) for r in range(-3, ROWS + 3)]


def stacked(ref):
    return jnp.concatenate([ref[lev] for lev in range(LEVELS)], axis=0)


def early_kernel(
    fields, levels, last, scale, columns, c, x, t, zon_in, zon_t_in, swapped,
    mix, out, zon, zon_t, factor, south_rows, south_rows_t, south_near, ws,
):
    lat = lax.axis_index("lat")
    lons = x.shape[-1]
    mix_weights(levels, columns, mix)
    factor[...] = jnp.full(factor.shape, jnp.where(lat == 0, 0.0, scale[lat * 2 * ROWS]))
    parts = []
    for lev in range(LEVELS):
        own = c[lev]
        parts += [
            jnp.where(lat == 0, -pltpu.roll(own, lons // 2, 1)[0:1], 0.0),
            own[: ROWS - 1],
        ]
    for r, w in enumerate(row_weights(stacked(c), jnp.concatenate(parts, axis=0), scale, lat)):
        for lev in range(LEVELS):
            out[r, lev] = w[lev * ROWS : (lev + 1) * ROWS]

    for lev in range(LEVELS):
        for r in range(3):
            at = r * LEVELS + lev
            south_rows_t[at : at + 1, :] = t[lev, r : r + 1, :]
            for i in range(fields):
                south_rows[at, i : i + 1, :] = x[i, lev, r : r + 1, :]
        for chunk in range(lons // LANE):
            lane = lanes(chunk)
            weights = [out[r + 3, lev, :, lane] for r in range(ROWS)]

            def with_own_rows(total, row_at):
                for r, w in enumerate(weights):
                    total = total + w * jnp.broadcast_to(row_at(r), total.shape)
                return total

            zon_t[lev, :, lane] = with_own_rows(
                zon_t_in[lev, :, lane], lambda r: t[lev, r : r + 1, lane]
            )
            for i in range(fields):
                zon[i, lev, :, lane] = with_own_rows(
                    zon_in[i, lev, :, lane], lambda r: x[i, lev, r : r + 1, lane]
                )

    def near_terms(odd):
        count = swapped.shape[0]
        skip = fields - count
        rows = side_rows(odd)
        for lev in range(LEVELS):
            for d, row in enumerate(rows, 1):
                at = (3 - d) * LEVELS + lev
                for i in range(count):
                    south_near[at, i : i + 1, :] = (
                        swapped[i, lev, row : row + 1, :] if odd else jnp.zeros((1, lons), jnp.float32)
                    )
            for chunk in range(lons // LANE):
                lane = lanes(chunk)
                weights = [out[3 - d if odd else ROWS + 2 + d, lev, :, lane] for d in range(1, 4)]
                for i in range(count):
                    total = zon[skip + i, lev, :, lane]
                    for w, row in zip(weights, rows):
                        v = swapped[i, lev, row : row + 1, lane]
                        total = total + w * jnp.broadcast_to(v, total.shape)
                    zon[skip + i, lev, :, lane] = total

    both(lax.rem(lat, 2), near_terms)

    def pole(rows):
        for k, (_, at) in enumerate(rows):
            ws[k] = stacked(out.at[at])
            for lev in range(LEVELS):
                out[at, lev] = jnp.zeros_like(out[at, lev])

        def beyond(ref):
            v = pltpu.roll(stacked(ref), lons // 2, 1)
            total = jnp.zeros_like(v)
            for k, (source, _) in enumerate(rows):
                both_rows = [
                    jnp.broadcast_to(v[r : r + 1], (ROWS, lons))
                    for r in range(source, LEVELS * ROWS, ROWS)
                ]
                total = total + ws[k] * jnp.concatenate(both_rows, axis=0)
            return [total[lev * ROWS : (lev + 1) * ROWS] for lev in range(LEVELS)]

        for lev, part in enumerate(beyond(t)):
            zon_t[lev] = zon_t[lev] + part

        @pl.loop(0, fields, step=2)
        def _(start):
            for i in (start, start + 1):
                for lev, part in enumerate(beyond(x.at[i])):
                    zon[i, lev] = zon[i, lev] + part

    @pl.when(lat == 0)
    def _():
        pole([(d - 1, 3 - d) for d in range(1, 4)])

    @pl.when(lat == last)
    def _():
        pole([(ROWS - d, ROWS + 2 + d) for d in range(1, 4)])


def patch_kernel(
    factor, near, far, weights, south_rows, south_rows_t, south_near, low, delta, delta_t
):
    block = 3 * LEVELS
    rows = slice(block, block + LEVELS)
    below = jnp.where(parity() == 1, near[block, rows, :], far[block, rows, :])
    parts = [factor[...] * part for part in face_weights(below)]
    for r in range(3):
        for lev in range(LEVELS):
            w = weights[r, lev]
            low[r, lev] = w
            low[r, lev, 0:1, :] = w[0:1] + parts[r][lev : lev + 1]
    total_t = None
    for r in range(3):
        term = parts[r + 3] * south_rows_t[LEVELS * r : LEVELS * (r + 1), :]
        total_t = term if total_t is None else total_t + term
    delta_t[...] = total_t
    for lev in range(LEVELS):
        total = None
        for r in range(3):
            v = south_rows[r * LEVELS + lev]
            term = jnp.broadcast_to(parts[r + 3][lev : lev + 1], v.shape) * v
            total = term if total is None else total + term
        delta[lev] = total
        skip = total.shape[0] - south_near.shape[1]
        total = total[skip:]
        for r in range(3):
            v = south_near[r * LEVELS + lev]
            total = total + jnp.broadcast_to(parts[r][lev : lev + 1], v.shape) * v
        delta[lev, skip:, :] = total


def zonal_kernel(
    fields, x, t, n, f, c, upper, share, quotient, ground, zon, zon_t, near, far, columns, w
):
    lons = x.shape[-1]
    pack_columns(upper, share, quotient, ground, columns)

    def gather(odd):
        gather_rows(side_rows(not odd), x, t, c, near)
        gather_rows(side_rows(odd), x, t, c, far)

    both(parity(), gather)

    def shifted(values, k):
        return values if k == 0 else pltpu.roll(values, (-k) % lons, 1)

    def advance(v):
        flux = w[1] * v
        for k in (0, 2, 3, 4, 5, 6):
            flux = flux + w[k] * shifted(v, 1 - k)
        return v - (shifted(flux, 1) - flux)

    whole = stacked(n)
    s = parabola_weights(stacked(f))
    zero = jnp.zeros_like(s[0])
    n0, n1 = whole == 0, whole == 1

    def pick(a, b, d):
        return jnp.where(n0, a, jnp.where(n1, b, d))

    w[0] = pick(s[4], zero, zero)
    w[1] = pick(s[3], s[4], zero)
    w[2] = pick(s[2], s[3] + 1.0, s[4] + 1.0)
    w[3] = pick(s[1], s[2], s[3] + 1.0)
    w[4] = pick(s[0], s[1], s[2])
    w[5] = pick(zero, s[0], s[1])
    w[6] = pick(zero, zero, s[0])

    total = advance(stacked(t))
    for lev in range(LEVELS):
        zon_t[lev] = total[lev * ROWS : (lev + 1) * ROWS]

    @pl.loop(0, fields, step=2)
    def _(start):
        for i in (start, start + 1):
            total = advance(stacked(x.at[i]))
            for lev in range(LEVELS):
                zon[i, lev] = total[lev * ROWS : (lev + 1) * ROWS]


def fin_kernel(skip, count, direct, *refs):
    if direct:
        base, near, far, w, low, delta, base_t, delta_t, adv = refs
    else:
        base, far, w, low, delta, adv = refs
    chunks = w.shape[-1] // LANE
    first_row = lax.broadcasted_iota(jnp.int32, (ROWS, LANE), 0) == 0

    def body(odd):
        for lev in range(LEVELS):
            for chunk in range(chunks):
                lane = lanes(chunk)
                sides = [
                    (low[3 - d, lev, :, lane], w[ROWS + 2 + d, lev, :, lane]) for d in range(1, 4)
                ]

                def total_of(total, row_0, near_row, far_row):
                    total = total + jnp.where(first_row, jnp.broadcast_to(row_0, total.shape), 0.0)
                    for d, (south, north) in enumerate(sides, 1):
                        for weight, is_near in ((south, odd), (north, not odd)):
                            if is_near and near_row is None:
                                continue
                            v = near_row(d) if is_near else far_row(d)
                            total = total + weight * jnp.broadcast_to(v, total.shape)
                    return total

                def gathered(ref, f):
                    return lambda d: ref[(d - 1) * LEVELS + lev, f : f + 1, lane]

                def gathered_t(ref):
                    def row_at(d):
                        at = (d - 1) * LEVELS + lev
                        return ref[3 * LEVELS, at : at + 1, lane]

                    return row_at

                for f in range(count):
                    adv[f, lev, :, lane] = total_of(
                        base[skip + f, lev, :, lane],
                        delta[lev, skip + f : skip + f + 1, lane],
                        gathered(near, f) if direct else None,
                        gathered(far, f),
                    )
                if direct:
                    adv[count, lev, :, lane] = total_of(
                        base_t[lev, :, lane],
                        delta_t[lev : lev + 1, lane],
                        gathered_t(near),
                        gathered_t(far),
                    )

    both(parity(), body)


def pack_columns(upper, share, quotient, ground, out):
    levels = upper.shape[0]
    out[:levels] = upper[...].astype(jnp.float32)
    out[levels : 2 * levels] = share[...]
    out[2 * levels : 3 * levels] = quotient[...]
    out[3 * levels] = ground[...]


def mix_weights(levels, columns, weights):
    group = lax.axis_index("lev")
    for k in range(levels):
        upper = columns[k]
        share = columns[levels + k]
        for s in range(2 * LEVELS):
            level = (group if s < LEVELS else 1 - group) * LEVELS + s % LEVELS
            at = level.astype(jnp.float32)
            weights[k, s] = jnp.where(
                upper == at, 1.0 - share, jnp.where(upper + 1.0 == at, share, 0.0)
            )


def mixed(weights, values):
    total = weights[0] * values[0]
    for w, v in zip(weights[1:], values[1:]):
        total = total + w * v
    return total


def blend(own, peer, weights, out, fields, skip=0):
    group = lax.axis_index("lev")
    for chunk in range(own.shape[-1] // LANE):
        lane = lanes(chunk)
        ws = [
            [weights[group * LEVELS + lev, s, :, lane] for s in range(2 * LEVELS)]
            for lev in range(LEVELS)
        ]
        for f in fields:
            values = [adv[f, lev, :, lane] for adv in (own, peer) for lev in range(LEVELS)]
            for lev in range(LEVELS):
                out[skip + f, lev, :, lane] = mixed(ws[lev], values)


def remap_first_kernel(levels, own, peer, weights, columns, out, thick):
    count = out.shape[0]
    vapour = [adv[0, lev] for adv in (own, peer) for lev in range(LEVELS)]
    temp = [adv[count, lev] for adv in (own, peer) for lev in range(LEVELS)]
    for k in range(levels):
        ws = [weights[k, s] for s in range(2 * LEVELS)]
        water = mixed(ws, vapour)
        heat = mixed(ws, temp)
        thick[k] = heat * (1.0 + 0.608 * water) * columns[2 * levels + k]
        thick[levels + k] = heat
    deeper = columns[3 * levels]
    for k in range(levels - 1, -1, -1):
        layer = thick[k]
        thick[k] = deeper + 0.5 * layer
        deeper = deeper + layer
    blend(own, peer, weights, out, range(count))


def remap_last_kernel(levels, own, peer, weights, first, thick, out, out_t, out_phi, buffer, sems):
    group = lax.axis_index("lev")
    count = first.shape[0]
    copies = []

    def send(source, target):
        copy = pltpu.make_async_copy(source, target, sems.at[len(copies)])
        copy.start()
        copies.append(copy)

    send(first, out.at[pl.ds(0, count)])
    mine = group * LEVELS
    send(thick.at[pl.ds(mine, LEVELS)], out_phi)
    send(thick.at[pl.ds(levels + mine, LEVELS)], out_t)
    step = 4
    for start in range(0, buffer.shape[0], step):
        blend(own, peer, weights, buffer, range(start, start + step))
        send(buffer.at[pl.ds(start, step)], out.at[pl.ds(count + start, step)])
    for copy in copies:
        copy.wait()


def call(kernel, outs, scratch=(), specs=None, cost=0, limit=12, aliases=None, out_specs=None):
    single = not isinstance(outs, list)
    shapes = tuple(jax.ShapeDtypeStruct(s, jnp.float32) for s in ([outs] if single else outs))
    extra = {} if specs is None else {"in_specs": specs}
    if out_specs is not None:
        extra["out_specs"] = out_specs
    return pl.pallas_call(
        kernel,
        out_shape=shapes[0] if single else shapes,
        scratch_shapes=[pltpu.VMEM(s, jnp.float32) if isinstance(s, tuple) else s for s in scratch],
        compiler_params=pltpu.CompilerParams(vmem_limit_bytes=limit * 2**20),
        cost_estimate=pl.CostEstimate(flops=cost * 10**6, bytes_accessed=1000, transcendentals=0),
        input_output_aliases=aliases or {},
        **extra,
    )


def on_device(
    constituent_densities,
    thermal_state,
    integer_boxes_traversed,
    partial_crossing_share,
    northward_crossing_share,
    higher_donor_stratum,
    deeper_donor_share,
    napierian_thickness_quotient,
    ground_gravity_height,
):
    x, t, c = constituent_densities, thermal_state, northward_crossing_share
    fields, _, _, lons = x.shape
    levels = higher_donor_stratum.shape[0]
    bands = lax.axis_size("lat")
    lat_total = bands * ROWS

    pairs = [(i, i ^ 1) for i in range(bands)]
    across = [(i, i + 1 if i % 2 else i - 1) for i in range(1, bands - 1)]
    relays = [(i, i + 2) for i in range(0, bands - 2, 2)] + [(i, i - 2) for i in range(3, bands, 2)]
    cores = [(0, 1), (1, 0)]

    def swap(v):
        return lax.ppermute(v, "lat", pairs)

    def exchange_across(v):
        return lax.ppermute(v, "lat", across)

    def pass_on(v):
        return lax.ppermute(v, "lat", relays)

    def other_core(v):
        return lax.ppermute(v, "lev", cores)

    face = np.arange(lat_total + 1)
    face_sine = np.sin(math.pi * np.minimum(face, lat_total - face) / lat_total)
    row_sine = np.sin(math.pi * (np.arange(lat_total) + 0.5) / lat_total)
    scale = np.stack([face_sine[:-1] / row_sine, face_sine[1:] / row_sine], 1)
    scale = jnp.asarray(scale.reshape(-1).astype(np.float32))

    smem, vmem = pl.BlockSpec(memory_space=pltpu.SMEM), pl.BlockSpec(memory_space=pltpu.VMEM)
    direct = fields // 2
    swapped = fields - direct
    direct_shape = (3 * LEVELS + 1, direct, lons)

    payload = call(copy_kernel, (swapped,) + x.shape[1:])(x)
    near_a = swap(payload)
    zon, zon_t, near_rows, far_rows, columns = call(
        functools.partial(zonal_kernel, fields),
        [
            x.shape,
            t.shape,
            direct_shape,
            direct_shape,
            (3 * levels + 1,) + ground_gravity_height.shape,
        ],
        [(7, LEVELS * ROWS, lons)],
        cost=COST["zonal"],
    )(
        x,
        t,
        integer_boxes_traversed,
        partial_crossing_share,
        c,
        higher_donor_stratum,
        deeper_donor_share,
        napierian_thickness_quotient,
        ground_gravity_height,
    )
    far_b = exchange_across(far_rows)
    near_b = swap(near_rows)

    relay = call(relay_kernel, (3 * LEVELS, swapped, lons), cost=COST["relay"])(near_a, zon_t)
    far_a = pass_on(relay)

    peer_columns = other_core(columns)
    columns = jnp.where(
        lax.axis_index("lev") == 0,
        jnp.concatenate([columns, peer_columns], -1),
        jnp.concatenate([peer_columns, columns], -1),
    )

    mix, weights, base, base_t, factor, south_rows, south_rows_t, south_near = call(
        functools.partial(early_kernel, fields, levels, bands - 1),
        [
            (levels, 2 * LEVELS, ROWS, lons),
            (ROWS + 6, LEVELS, ROWS, lons),
            x.shape,
            t.shape,
            (LEVELS, lons),
            (3 * LEVELS, fields, lons),
            (3 * LEVELS, lons),
            (3 * LEVELS, swapped, lons),
        ],
        [(3, LEVELS * ROWS, lons)],
        [smem] + [vmem] * 7,
        cost=COST["early"],
    )(scale, columns, c, x, t, zon, zon_t, near_a)
    low, delta, delta_t = call(
        patch_kernel,
        [(3, LEVELS, ROWS, lons), (LEVELS, fields, lons), (LEVELS, lons)],
        cost=COST["patch"],
    )(factor, near_b, far_b, weights, south_rows, south_rows_t, south_near)

    adv_b = call(
        functools.partial(fin_kernel, 0, direct, True),
        (direct + 1,) + x.shape[1:],
        cost=COST["fin_b"],
    )(base, near_b, far_b, weights, low, delta, base_t, delta_t)
    peer_b = other_core(adv_b)
    adv_a = call(
        functools.partial(fin_kernel, direct, swapped, False),
        (swapped,) + x.shape[1:],
        cost=COST["fin_a"],
    )(base, far_a, weights, low, delta)
    peer_a = other_core(adv_a)

    anywhere = pl.BlockSpec(memory_space=pl.ANY)
    first, thick = call(
        functools.partial(remap_first_kernel, levels),
        [(direct,) + x.shape[1:], (2 * levels, ROWS, lons)],
        cost=COST["first"],
    )(adv_b, peer_b, mix, columns)
    return call(
        functools.partial(remap_last_kernel, levels),
        [x.shape, t.shape, t.shape],
        [(swapped,) + x.shape[1:], pltpu.SemaphoreType.DMA((3 + swapped // 4,))],
        cost=COST["last"],
        out_specs=(anywhere,) * 3,
    )(adv_a, peer_a, mix, first, thick)


def solution(mesh):
    return jax.shard_map(
        on_device,
        mesh=mesh,
        in_specs=(
            P("ens", "lev", "lat", None),
            P(("ens", "lev"), "lat", None),
            P(("ens", "lev"), "lat", None),
            P(("ens", "lev"), "lat", None),
            P(("ens", "lev"), "lat", None),
            P("ens", "lat", "lev"),
            P("ens", "lat", "lev"),
            P("ens", "lat", "lev"),
            P(("ens", "lat"), "lev"),
        ),
        out_specs=(
            P("ens", "lev", "lat", None),
            P(("ens", "lev"), "lat", None),
            P(("ens", "lev"), "lat", None),
        ),
        check_vma=False,
    )
```
